512 devices in a mesh: col: 64 (over y, z_lo, core), row: 8 (over x, z_hi).
Axes of the slice: x: 4, y: 8, z: 8 (z_hi: 2, z_lo: 4; z = z_hi * 4 + z_lo), core: 2. Of those that a mesh axis runs over, the one named last changes fastest.
Arguments:
- field: bfloat16 [128, 1024, 128], P('row', 'col'), may hold values from -6 to 6
- cotangent: bfloat16 [128, 1024, 128], P('row', 'col'), may hold values from -6 to 6
- w_first: bfloat16 [3, 3, 128, 128], replicated, may hold values from -0.1875 to 0.1875
- w_down: bfloat16 [3, 3, 128, 256], replicated, may hold values from -0.1875 to 0.1875
- w_up: bfloat16 [2, 2, 256, 128], replicated, may hold values from -0.375 to 0.375
- offsets: int32 [8, 64, 2], replicated, may hold values from -8 to 8
- blend_table: int32 [32, 32], replicated, may hold values from 1 to 16
Outputs:
- blended: bfloat16 [128, 1024, 128], P('row', 'col')
- field_grad: float32 [128, 1024, 128], P('row', 'col')
- grad_first: float32 [3, 3, 128, 128], replicated
- grad_down: float32 [3, 3, 128, 256], replicated
- grad_up: float32 [2, 2, 256, 128], replicated
The draws below stay inside these ranges and needn't reach their ends.
Inputs may be any that keep to these rules, and one draw needn't show every extreme that they name: `offsets`: A patch's first cell lies 8 cells minus its offset before its tile's first cell on each axis.
All inputs are finite; a program needn't handle non-finite values.
Results may differ from the reference program's by a relative error of at most 0.015.
Values may be sent and summed in bfloat16 or wider, within the bound.
No kernel may reach another device: no remote copies, remote signals or barrier semaphores. Data moves between devices by JAX's collectives and lax.ppermute only.
A program may use at most 64 MiB of HBM per device.

```python
import math
import jax
import jax.numpy as jnp
from jax import lax

TH = 16
TW = 16
MARGIN = 8
C1 = 128
C2 = 256
PH = 32
PW = 32
GRID_H = 128
GRID_W = 1024
PROWS = 8
PCOLS = 64


def touch_ends(entries, key, least, top_value):
    longest = entries.shape.index(max(entries.shape))
    spots = []
    for shift in (0, 1):
        where = [jax.random.randint(jax.random.fold_in(key, axis), (), 0, length) for axis, length in enumerate(entries.shape)]
        where[longest] = (where[longest] + shift) % entries.shape[longest]
        spots.append(tuple(where))
    return entries.at[spots[0]].set(least).at[spots[1]].set(top_value)


def steps_of(stream_key, shape, cuts, least, largest):
    def one(dim, shards_of):
        draws = jax.random.uniform(jax.random.fold_in(jax.random.fold_in(stream_key, 6), dim), (shards_of,), jnp.float32, least / len(cuts), largest / len(cuts))
        return jnp.repeat(jnp.exp(draws), shape[dim] // shards_of).reshape((-1,) + (1,) * (len(shape) - dim - 1))

    gain = one(*cuts[0])
    for cut in cuts[1:]:
        gain = gain * one(*cut)
    return gain


def centred(own_key, dims, deviation, reach, shards=(), kind=jnp.bfloat16):
    result = jax.random.normal(own_key, dims, jnp.float32) * deviation
    if len(shards) > 0:
        result = steps_of(own_key, dims, shards, -0.22, 0.18) * result
    return jnp.clip(result, min=-reach, max=reach).astype(kind)


def setup_inputs(seed: int = 0) -> dict:
    key_of = jax.random.split(jax.random.key(seed), 8)
    return {
        "field": centred(key_of[0], (GRID_H, GRID_W, C1), 1.0, 6.0, ((0, 8), (1, 64))),
        "cotangent": centred(key_of[1], (GRID_H, GRID_W, C1), 1.0, 6.0, ((0, 8), (1, 64))),
        "w_first": centred(key_of[2], (3, 3, C1, C1), (9 * C1) ** -0.5, 0.1875),
        "w_down": centred(key_of[3], (3, 3, C1, C2), (9 * C1) ** -0.5, 0.1875),
        "w_up": centred(key_of[4], (2, 2, C2, C1), C2 ** -0.5, 0.375),
        "offsets": touch_ends(jax.random.randint(key_of[5], (PROWS, PCOLS, 2), 0 - MARGIN, MARGIN + 1), jax.random.fold_in(key_of[5], 1), 0 - MARGIN, MARGIN).astype(jnp.int32),
        "blend_table": touch_ends(jax.random.randint(key_of[6], (PH, PW), 1, 17), jax.random.fold_in(key_of[6], 1), 1, 16).astype(jnp.int32),
    }


def conv_same(inputs, kernel):
    rows, cols, chans = inputs.shape
    padded = jnp.pad(inputs, ((1, 1), (1, 1), (0, 0)))
    total = jnp.zeros((rows * cols, kernel.shape[3]), jnp.float32)
    for row_tap in range(3):
        for col_tap in range(3):
            window = padded[row_tap:row_tap + rows, col_tap:col_tap + cols].reshape(rows * cols, chans)
            total = total + jnp.dot(window, kernel[row_tap, col_tap], preferred_element_type=jnp.float32)
    return total.reshape(rows, cols, kernel.shape[3])

def conv_down(inputs, kernel):
    rows, cols, chans = inputs.shape
    padded = jnp.pad(inputs, ((1, 1), (1, 1), (0, 0)))
    half_r = rows // 2
    half_c = cols // 2
    total = jnp.zeros((half_r * half_c, kernel.shape[3]), jnp.float32)
    for row_tap in range(3):
        for col_tap in range(3):
            window = padded[row_tap:row_tap + rows:2, col_tap:col_tap + cols:2].reshape(half_r * half_c, chans)
            total = total + jnp.dot(window, kernel[row_tap, col_tap], preferred_element_type=jnp.float32)
    return total.reshape(half_r, half_c, kernel.shape[3])

def conv_up(inputs, kernel):
    rows, cols, chans = inputs.shape
    flat = inputs.reshape(rows * cols, chans)
    lines = []
    for row_tap in range(2):
        pieces = []
        for col_tap in range(2):
            pieces.append(jnp.dot(flat, kernel[row_tap, col_tap], preferred_element_type=jnp.float32).reshape(rows, cols, kernel.shape[3]))
        lines.append(jnp.stack(pieces, axis=2))
    return jnp.stack(lines, axis=1).reshape(2 * rows, 2 * cols, kernel.shape[3])

def patch_net(patch, w_first, w_down, w_up):
    hidden = jax.nn.silu(conv_same(patch, w_first)).astype(jnp.bfloat16)
    lower = jax.nn.silu(conv_down(hidden, w_down)).astype(jnp.bfloat16)
    return hidden.astype(jnp.float32) + conv_up(lower, w_up)

def reference(field, cotangent, w_first, w_down, w_up, offsets, blend_table):
    edge = 2 * MARGIN
    table_f = blend_table.astype(jnp.float32)

    def anchor(index):
        index = index.astype(jnp.int32)
        row_at = index // PCOLS
        col_at = index % PCOLS
        top = (row_at * TH + MARGIN + offsets[row_at, col_at, 0]).astype(jnp.int32)
        left = (col_at * TW + MARGIN + offsets[row_at, col_at, 1]).astype(jnp.int32)
        return (top, left)

    def add_table(index, canvas):
        top, left = anchor(index)
        current = lax.dynamic_slice(canvas, (top, left), (PH, PW))
        return lax.dynamic_update_slice(canvas, current + table_f, (top, left))
    den_canvas = jnp.zeros((GRID_H + 2 * edge, GRID_W + 2 * edge), jnp.float32)
    den_canvas = lax.fori_loop(0, PROWS * PCOLS, add_table, den_canvas)
    weight_sum = den_canvas[edge:edge + GRID_H, edge:edge + GRID_W]
    ratio = cotangent.astype(jnp.float32) / weight_sum[:, :, None]
    ratio_pad = jnp.pad(ratio, ((edge, edge), (edge, edge), (0, 0)))
    field_pad = jnp.pad(field, ((edge, edge), (edge, edge), (0, 0)))
    zero = jnp.int32(0)

    def one_patch(index, carry):
        numer, d_canvas, g_first, g_down, g_up = carry
        top, left = anchor(index)
        patch = lax.dynamic_slice(field_pad, (top, left, zero), (PH, PW, C1))
        out_patch, back = jax.vjp(patch_net, patch, w_first, w_down, w_up)
        current = lax.dynamic_slice(numer, (top, left, zero), (PH, PW, C1))
        numer = lax.dynamic_update_slice(numer, current + table_f[:, :, None] * out_patch, (top, left, zero))
        out_grad = table_f[:, :, None] * lax.dynamic_slice(ratio_pad, (top, left, zero), (PH, PW, C1))
        d_patch, d_first, d_down, d_up = back(out_grad)
        current = lax.dynamic_slice(d_canvas, (top, left, zero), (PH, PW, C1))
        d_canvas = lax.dynamic_update_slice(d_canvas, current + d_patch.astype(jnp.float32), (top, left, zero))
        return (numer, d_canvas, g_first + d_first.astype(jnp.float32), g_down + d_down.astype(jnp.float32), g_up + d_up.astype(jnp.float32))
    start = (jnp.zeros((GRID_H + 2 * edge, GRID_W + 2 * edge, C1), jnp.float32), jnp.zeros((GRID_H + 2 * edge, GRID_W + 2 * edge, C1), jnp.float32), jnp.zeros((3, 3, C1, C1), jnp.float32), jnp.zeros((3, 3, C1, C2), jnp.float32), jnp.zeros((2, 2, C2, C1), jnp.float32))
    numer, d_canvas, g_first, g_down, g_up = lax.fori_loop(0, PROWS * PCOLS, one_patch, start)
    blended = (numer[edge:edge + GRID_H, edge:edge + GRID_W] / weight_sum[:, :, None]).astype(jnp.bfloat16)
    field_grad = d_canvas[edge:edge + GRID_H, edge:edge + GRID_W]
    scale = 1.0 / math.sqrt(GRID_H * GRID_W)
    return (blended, field_grad, g_first * scale, g_down * scale, g_up * scale)
```

```python
import math

import jax
import jax.numpy as jnp
from jax import lax
from jax.sharding import Mesh, PartitionSpec as P

MARGIN = 8
ROW = ("x", "zh")
COL = ("y", "zl", "core")


def passed_along(block, axis, distance):
    devices = range(lax.axis_size(axis))
    route = [(i - distance, i) for i in devices if i - distance in devices]
    return lax.ppermute(block, axis, route)


def extended(x, sides, width):
    for axis, dim in sides:
        size, length = (lax.axis_size(axis), x.shape[dim])
        up = [(i, (i + 1) % size) for i in range(size - 1)]
        down = [(j, i) for i, j in up]
        last = lax.slice_in_dim(x, length - width, length, axis=dim)
        leading = lax.slice_in_dim(x, 0, width, axis=dim)
        before = lax.ppermute(last, axis, up)
        after = lax.ppermute(leading, axis, down)
        x = jnp.concatenate([before, x, after], axis=dim)
    return x


def conv_same(inputs, kernel):
    rows, cols, chans = inputs.shape
    padded = jnp.pad(inputs, ((1, 1), (1, 1), (0, 0)))
    total = jnp.zeros((rows * cols, kernel.shape[3]), jnp.float32)
    for row_tap in range(3):
        for col_tap in range(3):
            window = padded[row_tap : row_tap + rows, col_tap : col_tap + cols].reshape(
                rows * cols, chans
            )
            total = total + jnp.dot(
                window, kernel[row_tap, col_tap], preferred_element_type=jnp.float32
            )
    return total.reshape(rows, cols, kernel.shape[3])


def conv_down(inputs, kernel):
    rows, cols, chans = inputs.shape
    padded = jnp.pad(inputs, ((1, 1), (1, 1), (0, 0)))
    half_r = rows // 2
    half_c = cols // 2
    total = jnp.zeros((half_r * half_c, kernel.shape[3]), jnp.float32)
    for row_tap in range(3):
        for col_tap in range(3):
            window = padded[row_tap : row_tap + rows : 2, col_tap : col_tap + cols : 2].reshape(
                half_r * half_c, chans
            )
            total = total + jnp.dot(
                window, kernel[row_tap, col_tap], preferred_element_type=jnp.float32
            )
    return total.reshape(half_r, half_c, kernel.shape[3])


def conv_up(inputs, kernel):
    rows, cols, chans = inputs.shape
    flat = inputs.reshape(rows * cols, chans)
    lines = []
    for row_tap in range(2):
        pieces = []
        for col_tap in range(2):
            pieces.append(
                jnp.dot(flat, kernel[row_tap, col_tap], preferred_element_type=jnp.float32).reshape(
                    rows, cols, kernel.shape[3]
                )
            )
        lines.append(jnp.stack(pieces, axis=2))
    return jnp.stack(lines, axis=1).reshape(2 * rows, 2 * cols, kernel.shape[3])


def patch_net(patch, w_first, w_down, w_up):
    hidden = jax.nn.silu(conv_same(patch, w_first)).astype(jnp.bfloat16)
    lower = jax.nn.silu(conv_down(hidden, w_down)).astype(jnp.bfloat16)
    return hidden.astype(jnp.float32) + conv_up(lower, w_up)


def return_margins(canvas, tile_h, tile_w, edge):
    summed = canvas
    for heading in (1, -1):
        strip = canvas[tile_h + edge :] if heading == 1 else canvas[:edge]
        arrived = passed_along(strip.astype(jnp.bfloat16), ROW, heading).astype(strip.dtype)
        if heading == 1:
            summed = summed.at[edge : 2 * edge].add(arrived)
        else:
            summed = summed.at[tile_h : tile_h + edge].add(arrived)
    middle = summed[edge : tile_h + edge]
    result = middle
    for heading in (1, -1):
        strip = middle[:, tile_w + edge :] if heading == 1 else middle[:, :edge]
        arrived = passed_along(strip.astype(jnp.bfloat16), COL, heading).astype(strip.dtype)
        if heading == 1:
            result = result.at[:, edge : 2 * edge].add(arrived)
        else:
            result = result.at[:, tile_w : tile_w + edge].add(arrived)
    return result[:, edge : tile_w + edge]


def weight_total(offsets, table_f, row_at, col_at, rows_n, cols_n, tile_h, tile_w, lead, reach):
    patch_h, patch_w = table_f.shape
    total = jnp.zeros((tile_h + 2 * lead, tile_w + 2 * lead), jnp.float32)
    for row_step in range(-reach, reach + 1):
        for col_step in range(-reach, reach + 1):
            near_row = row_at + row_step
            near_col = col_at + col_step
            inside = (
                (near_row >= 0) & (near_row < rows_n) & (near_col >= 0) & (near_col < cols_n)
            ).astype(jnp.float32)
            shift_pair = offsets[
                jnp.clip(near_row, 0, rows_n - 1), jnp.clip(near_col, 0, cols_n - 1)
            ]
            top = row_step * tile_h - MARGIN + shift_pair[0] + lead
            left = col_step * tile_w - MARGIN + shift_pair[1] + lead
            pick_rows = (
                jnp.arange(tile_h + 2 * lead)[:, None] - top == jnp.arange(patch_h)[None, :]
            ).astype(jnp.float32)
            pick_cols = (
                jnp.arange(tile_w + 2 * lead)[:, None] - left == jnp.arange(patch_w)[None, :]
            ).astype(jnp.float32)
            placed = jnp.dot(
                jnp.dot(pick_rows, table_f, precision=lax.Precision.HIGHEST),
                pick_cols.T,
                precision=lax.Precision.HIGHEST,
            )
            total = total + inside * placed
    return total


def scattered(x, axes):
    size = lax.axis_size(axes)
    parts = x.reshape(size, x.shape[0] // size, x.shape[1])
    got = lax.all_to_all(parts, axes, 0, 0, tiled=True)
    return got.astype(jnp.float32).sum(0).astype(jnp.bfloat16)


def gathered(x, axes):
    size = lax.axis_size(axes)
    parts = jnp.broadcast_to(x[None], (size,) + x.shape)
    return lax.all_to_all(parts, axes, 0, 0, tiled=True)


def summed_over_mesh(flat):
    rows = flat.shape[0]
    part = jnp.pad(flat, ((0, -rows % 512), (0, 0)))
    part = scattered(part, "core")
    part = scattered(part, "x")
    part = scattered(part, "y")
    part = gathered(part, ("zl", "zh")).astype(jnp.float32).sum(0).astype(jnp.bfloat16)
    for axis in ("y", "x", "core"):
        part = gathered(part, axis).reshape(-1, part.shape[1])
    return part


def per_device(field, cotangent, w_first, w_down, w_up, offsets, blend_table):
    tile_h, tile_w, chans = field.shape
    patch_h, patch_w = blend_table.shape
    edge = 2 * MARGIN
    rows_n = lax.axis_size(ROW)
    cols_n = lax.axis_size(COL)
    row_at = lax.axis_index(ROW)
    col_at = lax.axis_index(COL)
    table_f = blend_table.astype(jnp.float32)
    grown = extended(field, ((ROW, 0), (COL, 1)), edge)
    own_shift = offsets[row_at, col_at]
    start_r = MARGIN + own_shift[0]
    start_c = MARGIN + own_shift[1]
    zero = jnp.int32(0)
    patch = lax.dynamic_slice(grown, (start_r, start_c, zero), (patch_h, patch_w, chans))
    out_patch, back = jax.vjp(patch_net, patch, w_first, w_down, w_up)
    empty = jnp.zeros((tile_h + 2 * edge, tile_w + 2 * edge, chans), jnp.float32)
    canvas = lax.dynamic_update_slice(
        empty, table_f[:, :, None] * out_patch, (start_r, start_c, zero)
    )
    numer = return_margins(canvas, tile_h, tile_w, edge)
    weight_sum = weight_total(
        offsets, table_f, row_at, col_at, rows_n, cols_n, tile_h, tile_w, 0, 1
    )
    ratio = cotangent.astype(jnp.float32) / weight_sum[:, :, None]
    ratio_grown = extended(ratio.astype(jnp.bfloat16), ((ROW, 0), (COL, 1)), edge).astype(
        ratio.dtype
    )
    blended = (numer / weight_sum[:, :, None]).astype(jnp.bfloat16)
    out_grad = table_f[:, :, None] * lax.dynamic_slice(
        ratio_grown, (start_r, start_c, zero), (patch_h, patch_w, chans)
    )
    d_patch, d_first, d_down, d_up = back(out_grad)
    d_canvas = lax.dynamic_update_slice(
        empty, d_patch.astype(jnp.float32), (start_r, start_c, zero)
    )
    field_grad = return_margins(d_canvas, tile_h, tile_w, edge)
    flat = jnp.concatenate(
        [d_first.reshape(-1, 128), d_down.reshape(-1, 128), d_up.reshape(-1, 128)], axis=0
    )
    total = summed_over_mesh(flat)
    n_first, n_down = d_first.size // 128, d_down.size // 128
    g_first = total[:n_first].reshape(d_first.shape).astype(jnp.float32)
    g_down = total[n_first : n_first + n_down].reshape(d_down.shape).astype(jnp.float32)
    g_up = total[n_first + n_down : n_first + n_down + d_up.size // 128]
    g_up = g_up.reshape(d_up.shape).astype(jnp.float32)
    scale = 1.0 / math.sqrt(tile_h * rows_n * tile_w * cols_n)
    return (blended, field_grad, g_first * scale, g_down * scale, g_up * scale)


def solution(mesh):
    fine = Mesh(mesh.devices.reshape(8, 4, 2, 4, 2), ("y", "zl", "core", "x", "zh"))
    tiles = P(ROW, COL, None)
    return jax.shard_map(
        per_device,
        mesh=fine,
        in_specs=(tiles, tiles, P(), P(), P(), P(), P()),
        out_specs=(tiles, tiles, P(), P(), P()),
        check_vma=False,
    )
```

```python
import math

import jax
import jax.numpy as jnp
from jax import lax
from jax.experimental import pallas as pl
from jax.experimental.pallas import tpu as pltpu
from jax.sharding import Mesh, PartitionSpec as P

MARGIN = 8
ROW = ("x", "zh")
COL = ("y", "zl", "core")
F32 = jnp.float32
BF16 = jnp.bfloat16
REACH = 2
FAR = 1000
TILE = 16
C1 = 128
C2 = 256
FIRST_ROWS = 9 * C1
DOWN_ROWS = 18 * C1
UP_ROWS = 4 * C2
FLAT_ROWS = 4608


def dot(a, b):
    return lax.dot_general(a, b, (((1,), (0,)), ((), ())), preferred_element_type=F32)


def dot_nt(a, b):
    return lax.dot_general(a, b, (((1,), (1,)), ((), ())), preferred_element_type=F32)


def prepare_kernel(where, offsets, table, w_first, w_down, w_up, fb, rf, rft, rdt, ru):
    row_at, col_at = where[0], where[1]
    rows_n, cols_n = offsets.shape[0], offsets.shape[1] // 2
    sub = lax.broadcasted_iota(jnp.int32, (32, 32), 0)
    lane = lax.broadcasted_iota(jnp.int32, (32, 32), 1)
    column = jnp.where(sub < 16, 2 * sub, 2 * (sub - 16) + 1)
    table_t = table[...].astype(F32).T.astype(BF16)
    own_r = offsets[row_at, 2 * col_at]
    own_c = offsets[row_at, 2 * col_at + 1]
    total = jnp.zeros((32, 32), F32)
    own = jnp.zeros((32, 32), F32)
    for row_step in range(-REACH, REACH + 1):
        for col_step in range(-REACH, REACH + 1):
            near_r, near_c = row_at + row_step, col_at + col_step
            inside = (near_r >= 0) & (near_r < rows_n) & (near_c >= 0) & (near_c < cols_n)
            at_r = jnp.clip(near_r, 0, rows_n - 1)
            at_c = jnp.clip(near_c, 0, cols_n - 1)
            down_by = row_step * TILE + offsets[at_r, 2 * at_c] - own_r
            right_by = col_step * TILE + offsets[at_r, 2 * at_c + 1] - own_c
            down_by = jnp.where(inside, down_by, FAR)
            pick_c = (column - right_by == lane).astype(F32).astype(BF16)
            pick_r = (lane - down_by == sub).astype(F32).astype(BF16)
            placed = dot(pick_c, table_t)
            if row_step == 0 and col_step == 0:
                own = placed
            total = total + dot(placed.astype(BF16), pick_r)
    share = own / total
    for r in range(32):
        fb[r % 2, r // 2, :, :C1] = jnp.broadcast_to(share[:16, r : r + 1], (16, C1))
        fb[r % 2, r // 2, :, C1:] = jnp.broadcast_to(share[16:, r : r + 1], (16, C1))
    none = jnp.zeros((C1, C1), BF16)
    for t in range(3):
        for v in range(4):
            for b in range(2):
                rows, cols = pl.ds(v * C1, C1), pl.ds(b * C1, C1)
                held = 0 <= v - b <= 2
                rf[t, rows, cols] = w_first[t, v - b] if held else none
                rft[t, cols, rows] = w_first[2 - t, 2 - v + b] if held else none
        rdt[t, :C1, :C2] = w_down[t, 1]
        rdt[t, :C1, C2:] = jnp.zeros((C1, C2), BF16)
        rdt[t, C1:, :C2] = w_down[t, 2]
        rdt[t, C1:, C2:] = w_down[t, 0]
    for a in range(2):
        for b in range(2):
            ru[a, :, pl.ds(b * C1, C1)] = w_up[a, b]


def shifted(x, by):
    j = lax.broadcasted_iota(jnp.int32, x.shape, 0) % 16
    moved = pltpu.roll(x, by % x.shape[0], 0)
    return jnp.where(j == (0 if by > 0 else 15), 0.0, moved)


def spread(x):
    return jnp.concatenate(
        [shifted(x[:, C1:], 1).astype(BF16), x.astype(BF16), shifted(x[:, :C1], -1).astype(BF16)], axis=1
    )


def window(ref, a, t):
    part = ref[(a + t) % 2, (a + t) // 2 : (a + t) // 2 + 16]
    return part.reshape(256, part.shape[-1])


def net_kernel(
    start, left, middle, right, fb, rf, rft, wd, rdt, ru,
    up_o, mid_o, down_o, flat,
    fs, cs, xv, hv, gv, g4, gs, bs, can_b, can_g,
):
    start_r, start_c = start[0], start[1]
    for ref in (xv, hv, gv):
        edge = jnp.zeros((16, ref.shape[-1]), BF16)
        ref[0, 0] = edge
        ref[1, 16] = edge
    g4[16] = jnp.zeros((16, 2 * C2), BF16)

    def stage(r, carry):
        for k, ref in enumerate((left, middle, right)):
            cells = ref[start_r + r].astype(F32)
            fs[r, 8 + 16 * k : 24 + 16 * k, :] = cells[:, :C1]
            cs[r, 8 + 16 * k : 24 + 16 * k, :] = cells[:, C1:]
        return carry

    lax.fori_loop(0, 32, stage, 0, unroll=4)
    j = lax.broadcasted_iota(jnp.int32, (16, C1), 0)

    def load(i, carry):
        for a in range(2):
            r = 2 * i + a
            at = start_c + 8
            before = jnp.where(j == 0, 0.0, fs[r, pl.ds(at - 1, 16, 2), :])
            even = fs[r, pl.ds(at, 16, 2), :]
            odd = fs[r, pl.ds(at + 1, 16, 2), :]
            after = jnp.where(j == 15, 0.0, fs[r, pl.ds(at + 2, 16, 2), :])
            xv[1 - a, i + a] = jnp.concatenate([before, even, odd, after], axis=1).astype(BF16)
            gs[a, i, :, :C1] = cs[r, pl.ds(at, 16, 2), :] * fb[a, i, :, :C1]
            gs[a, i, :, C1:] = cs[r, pl.ds(at + 1, 16, 2), :] * fb[a, i, :, C1:]
        return carry

    lax.fori_loop(0, 16, load, 0, unroll=2)

    h, slope_h = [], []
    for a in range(2):
        pre = dot(window(xv, a, 0), rf[0]) + dot(window(xv, a, 1), rf[1]) + dot(window(xv, a, 2), rf[2])
        sig = lax.logistic(pre)
        value = pre * sig
        slope_h.append(sig + value * (1.0 - sig))
        h.append(value.astype(BF16))
        hv[1 - a, a : a + 16] = jnp.concatenate(
            [shifted(value[:, C1:], 1).astype(BF16), h[a]], axis=1
        ).reshape(16, 16, 3 * C1)
    pre = dot(window(hv, 0, 0), wd[0]) + dot(window(hv, 0, 1), wd[1]) + dot(window(hv, 0, 2), wd[2])
    sig = lax.logistic(pre)
    value = pre * sig
    slope_d = sig + value * (1.0 - sig)
    d = value.astype(BF16)
    d_t = value.T.astype(BF16)
    g_d = jnp.zeros((256, C2), F32)
    for a in range(2):
        out = h[a].astype(F32) + dot(d, ru[a])
        bs[a] = (fb[a].reshape(256, 2 * C1) * out).reshape(16, 16, 2 * C1)
        g = gs[a].reshape(256, 2 * C1).astype(BF16)
        g_d = g_d + dot_nt(g, ru[a])
        g_up = dot(d_t, g).astype(BF16)
        base = FIRST_ROWS + DOWN_ROWS + 2 * a * C2
        flat[base : base + C2] = g_up[:, :C1]
        flat[base + C2 : base + 2 * C2] = g_up[:, C1:]
    g_pre = g_d.astype(BF16).astype(F32) * slope_d
    g4[0:16] = jnp.concatenate([g_pre.astype(BF16), shifted(g_pre, -1).astype(BF16)], axis=1).reshape(
        16, 16, 2 * C2
    )
    g_pre_t = g_pre.T.astype(BF16)
    for t in range(3):
        g_down = dot(g_pre_t, window(hv, 0, t)).T.astype(BF16)
        base = FIRST_ROWS + 6 * t * C1
        flat[base : base + 3 * C1] = g_down[:, :C1]
        flat[base + 3 * C1 : base + 6 * C1] = g_down[:, C1:]
    here = g4[0:16].reshape(256, 2 * C2)
    below = g4[1:17].reshape(256, 2 * C2)
    g_h = [dot_nt(here, rdt[1]), dot_nt(here, rdt[2]) + dot_nt(below, rdt[0])]
    g_t = []
    for a in range(2):
        g_pre = (gs[a].reshape(256, 2 * C1) + g_h[a]) * slope_h[a]
        gv[1 - a, a : a + 16] = spread(g_pre).reshape(16, 16, 4 * C1)
        g_t.append(g_pre.T.astype(BF16))
    for t in range(3):
        g_first = dot(g_t[0], window(xv, 0, t)) + dot(g_t[1], window(xv, 1, t))
        for ct in range(3):
            block = (
                g_first[:C1, ct * C1 : (ct + 1) * C1] + g_first[C1:, (ct + 1) * C1 : (ct + 2) * C1]
            )
            base = (3 * t + ct) * C1
            flat[base : base + C1] = block.T.astype(BF16)
    flat[FIRST_ROWS + DOWN_ROWS + UP_ROWS :] = jnp.zeros(
        (FLAT_ROWS - FIRST_ROWS - DOWN_ROWS - UP_ROWS, C1), BF16
    )
    for a in range(2):
        g_x = (
            dot_nt(window(gv, a, 0), rft[0])
            + dot_nt(window(gv, a, 1), rft[1])
            + dot_nt(window(gv, a, 2), rft[2])
        )
        gs[a] = g_x.reshape(16, 16, 2 * C1)

    def clear(r, carry):
        can_b[r] = jnp.zeros((48, C1), F32)
        can_g[r] = jnp.zeros((48, C1), F32)
        return carry

    lax.fori_loop(0, 48, clear, 0, unroll=4)

    def place(i, carry):
        for a in range(2):
            r = start_r + 2 * i + a
            for b in range(2):
                can_b[r, pl.ds(start_c + b, 16, 2), :] = bs[a, i, :, b * C1 : (b + 1) * C1]
                can_g[r, pl.ds(start_c + b, 16, 2), :] = gs[a, i, :, b * C1 : (b + 1) * C1]
        return carry

    lax.fori_loop(0, 16, place, 0, unroll=2)

    def give(r, carry):
        up_o[r, :, :C1] = can_b[r].astype(BF16)
        up_o[r, :, C1:] = can_g[r].astype(BF16)
        mid_o[r, :, :C1] = can_b[r + 16]
        mid_o[r, :, C1:] = can_g[r + 16]
        down_o[r, :, :C1] = can_b[r + 32].astype(BF16)
        down_o[r, :, C1:] = can_g[r + 32].astype(BF16)
        return carry

    lax.fori_loop(0, 16, give, 0, unroll=2)


VMEM = pl.BlockSpec(memory_space=pltpu.VMEM)
SMEM = pl.BlockSpec(memory_space=pltpu.SMEM)


def prepared(where, offsets, table, w_first, w_down, w_up):
    return pl.pallas_call(
        prepare_kernel,
        out_shape=(
            jax.ShapeDtypeStruct((2, 16, 16, 2 * C1), F32),
            jax.ShapeDtypeStruct((3, 4 * C1, 2 * C1), BF16),
            jax.ShapeDtypeStruct((3, 2 * C1, 4 * C1), BF16),
            jax.ShapeDtypeStruct((3, 2 * C1, 2 * C2), BF16),
            jax.ShapeDtypeStruct((2, C2, 2 * C1), BF16),
        ),
        in_specs=[SMEM, SMEM, VMEM, VMEM, VMEM, VMEM],
        out_specs=[VMEM] * 5,
        compiler_params=pltpu.CompilerParams(vmem_limit_bytes=16 * 2**20),
        cost_estimate=pl.CostEstimate(flops=5 * 10**6, bytes_accessed=10**7, transcendentals=0),
        name="prepare",
    )(where, offsets, table, w_first, w_down, w_up)


def patch_work(start, left, middle, right, fb, rf, rft, wd, rdt, ru):
    strip = jax.ShapeDtypeStruct((16, 48, 2 * C1), BF16)
    return pl.pallas_call(
        net_kernel,
        out_shape=(
            strip,
            jax.ShapeDtypeStruct((16, 48, 2 * C1), F32),
            strip,
            jax.ShapeDtypeStruct((FLAT_ROWS, C1), BF16),
        ),
        in_specs=[SMEM] + [VMEM] * 9,
        out_specs=[VMEM] * 4,
        scratch_shapes=[
            pltpu.VMEM((32, 64, C1), F32),
            pltpu.VMEM((32, 64, C1), F32),
            pltpu.VMEM((2, 17, 16, 4 * C1), BF16),
            pltpu.VMEM((2, 17, 16, 3 * C1), BF16),
            pltpu.VMEM((2, 17, 16, 4 * C1), BF16),
            pltpu.VMEM((17, 16, 2 * C2), BF16),
            pltpu.VMEM((2, 16, 16, 2 * C1), F32),
            pltpu.VMEM((2, 16, 16, 2 * C1), F32),
            pltpu.VMEM((48, 48, C1), F32),
            pltpu.VMEM((48, 48, C1), F32),
        ],
        compiler_params=pltpu.CompilerParams(vmem_limit_bytes=40 * 2**20),
        cost_estimate=pl.CostEstimate(flops=2 * 10**9, bytes_accessed=10**7, transcendentals=200000),
        name="patch_work",
    )(start, left, middle, right, fb, rf, rft, wd, rdt, ru)


def neighbours(axes, before, after):
    size = lax.axis_size(axes)
    ahead = [(i, i + 1) for i in range(size - 1)]
    back = [(i + 1, i) for i in range(size - 1)]
    return lax.ppermute(before, axes, ahead), lax.ppermute(after, axes, back)


def scattered(x, axes):
    size = lax.axis_size(axes)
    parts = x.reshape(size, x.shape[0] // size, x.shape[1])
    got = lax.all_to_all(parts, axes, 0, 0, tiled=True)
    return got.astype(F32).sum(0).astype(BF16)


def gathered(x, axes):
    size = lax.axis_size(axes)
    parts = jnp.broadcast_to(x[None], (size,) + x.shape)
    return lax.all_to_all(parts, axes, 0, 0, tiled=True)


def summed_over_mesh(part):
    part = scattered(part, "core")
    part = scattered(part, "x")
    part = scattered(part, "y")
    part = gathered(part, ("zl", "zh")).astype(F32).sum(0).astype(BF16)
    for axis in ("y", "x", "core"):
        part = gathered(part, axis).reshape(-1, part.shape[1])
    return part


def per_device(field, cotangent, w_first, w_down, w_up, offsets, blend_table):
    rows_n = lax.axis_size(ROW)
    cols_n = lax.axis_size(COL)
    row_at = lax.axis_index(ROW)
    col_at = lax.axis_index(COL)
    where = jnp.stack([row_at, col_at]).astype(jnp.int32)
    both = jnp.concatenate([field, cotangent], axis=2)
    fb, rf, rft, rdt, ru = prepared(
        where, offsets.reshape(rows_n, 2 * cols_n), blend_table, w_first, w_down, w_up
    )
    above, under = neighbours(ROW, both, both)
    middle = jnp.concatenate([above, both, under], axis=0)
    left, right = neighbours(COL, middle, middle)
    start = MARGIN + offsets[row_at, col_at]
    up, mid, down, flat = patch_work(
        start, left, middle, right, fb, rf, rft, w_down.reshape(3, 3 * C1, C2), rdt, ru
    )
    from_above, from_under = neighbours(ROW, down, up)
    total = summed_over_mesh(flat)
    mid = mid + from_above.astype(F32) + from_under.astype(F32)
    from_left, from_right = neighbours(
        COL, mid[:, 32:].astype(BF16), mid[:, :16].astype(BF16)
    )
    own = mid[:, 16:32] + from_left.astype(F32) + from_right.astype(F32)
    blended = own[:, :, :C1].astype(BF16)
    field_grad = own[:, :, C1:]
    scale = 1.0 / math.sqrt(TILE * rows_n * TILE * cols_n)
    total = total.astype(F32) * scale
    g_first = total[:FIRST_ROWS].reshape(w_first.shape)
    g_down = total[FIRST_ROWS : FIRST_ROWS + DOWN_ROWS].reshape(3, 2, 3 * C1, C1)
    g_down = g_down.transpose(0, 2, 1, 3).reshape(w_down.shape)
    g_up = total[FIRST_ROWS + DOWN_ROWS : FIRST_ROWS + DOWN_ROWS + UP_ROWS].reshape(w_up.shape)
    return (blended, field_grad, g_first, g_down, g_up)


def solution(mesh):
    fine = Mesh(mesh.devices.reshape(8, 4, 2, 4, 2), ("y", "zl", "core", "x", "zh"))
    tiles = P(ROW, COL, None)
    return jax.shard_map(
        per_device,
        mesh=fine,
        in_specs=(tiles, tiles, P(), P(), P(), P(), P()),
        out_specs=(tiles, tiles, P(), P(), P()),
        check_vma=False,
    )
```

```python
import functools
import math

import jax
import jax.numpy as jnp
from jax import lax
from jax.experimental import pallas as pl
from jax.experimental.pallas import tpu as pltpu
from jax.sharding import Mesh, PartitionSpec as P

MARGIN = 8
ROW = ("x", "zh")
COL = ("y", "zl", "core")
F32 = jnp.float32
BF16 = jnp.bfloat16
REACH = 2
FAR = 1000
TILE = 16
C1 = 128
C2 = 256
FIRST_ROWS = 9 * C1
DOWN_ROWS = 18 * C1
UP_ROWS = 4 * C2
FLAT_ROWS = 4608


def dot(a, b):
    return lax.dot_general(a, b, (((1,), (0,)), ((), ())), preferred_element_type=F32)


def dot_nt(a, b):
    return lax.dot_general(a, b, (((1,), (1,)), ((), ())), preferred_element_type=F32)


def prepare_kernel(where, offsets, table, w_first, w_down, w_up, fb, rf, rft, rdt, ru):
    row_at, col_at = where[0], where[1]
    rows_n, cols_n = offsets.shape[0], offsets.shape[1] // 2
    sub = lax.broadcasted_iota(jnp.int32, (32, 32), 0)
    lane = lax.broadcasted_iota(jnp.int32, (32, 32), 1)
    column = jnp.where(sub < 16, 2 * sub, 2 * (sub - 16) + 1)
    table_t = table[...].astype(F32).T.astype(BF16)
    own_r = offsets[row_at, 2 * col_at]
    own_c = offsets[row_at, 2 * col_at + 1]
    total = jnp.zeros((32, 32), F32)
    own = jnp.zeros((32, 32), F32)
    for row_step in range(-REACH, REACH + 1):
        for col_step in range(-REACH, REACH + 1):
            near_r, near_c = row_at + row_step, col_at + col_step
            inside = (near_r >= 0) & (near_r < rows_n) & (near_c >= 0) & (near_c < cols_n)
            at_r = jnp.clip(near_r, 0, rows_n - 1)
            at_c = jnp.clip(near_c, 0, cols_n - 1)
            down_by = row_step * TILE + offsets[at_r, 2 * at_c] - own_r
            right_by = col_step * TILE + offsets[at_r, 2 * at_c + 1] - own_c
            down_by = jnp.where(inside, down_by, FAR)
            pick_c = (column - right_by == lane).astype(F32).astype(BF16)
            pick_r = (lane - down_by == sub).astype(F32).astype(BF16)
            placed = dot(pick_c, table_t)
            if row_step == 0 and col_step == 0:
                own = placed
            total = total + dot(placed.astype(BF16), pick_r)
    share = own / total
    for r in range(32):
        fb[r % 2, r // 2, :, :C1] = jnp.broadcast_to(share[:16, r : r + 1], (16, C1))
        fb[r % 2, r // 2, :, C1:] = jnp.broadcast_to(share[16:, r : r + 1], (16, C1))
    none = jnp.zeros((C1, C1), BF16)
    for t in range(3):
        for v in range(4):
            for b in range(2):
                rows, cols = pl.ds(v * C1, C1), pl.ds(b * C1, C1)
                held = 0 <= v - b <= 2
                rf[t, rows, cols] = w_first[t, v - b] if held else none
                rft[t, cols, rows] = w_first[2 - t, 2 - v + b] if held else none
        rdt[t, :C1, :C2] = w_down[t, 1]
        rdt[t, :C1, C2:] = jnp.zeros((C1, C2), BF16)
        rdt[t, C1:, :C2] = w_down[t, 2]
        rdt[t, C1:, C2:] = w_down[t, 0]
    for a in range(2):
        for b in range(2):
            ru[a, :, pl.ds(b * C1, C1)] = w_up[a, b]


def assemble_kernel(starts, above, both, under, to_left, own, to_right, grown):
    grown[:, 0:16] = above[...]
    grown[:, 16:32] = both[...]
    grown[:, 32:48] = under[...]
    for side, out in enumerate((to_left, own, to_right)):
        out[...] = grown[:, pl.ds(starts[side], 32)]


def combine_kernel(starts, from_left, own, from_right, up, mid, down, canvas):
    canvas[...] = jnp.zeros_like(canvas)
    canvas[:, pl.ds(starts[1], 32)] = own[...]
    for side, part in ((0, from_left), (2, from_right)):
        spot = (slice(None), pl.ds(starts[side], 32))
        canvas[spot] = canvas[spot] + part[...].astype(F32)
    up[...] = canvas[:, 0:16].astype(BF16)
    mid[...] = canvas[:, 16:32]
    down[...] = canvas[:, 32:48].astype(BF16)


def finish_kernel(own, from_above, from_under, blended, field_grad):
    total = own[...] + from_above[...].astype(F32) + from_under[...].astype(F32)
    blended[...] = total[0].astype(BF16)
    field_grad[...] = total[1]


def unpack_kernel(scale, halves, g_first, g_down, g_up):
    def rows(base, count):
        return halves[base : base + count].astype(F32) * scale

    for t in range(9):
        g_first[t] = rows(t * C1, C1)
    for t in range(3):
        base = FIRST_ROWS + 6 * t * C1
        g_down[t, :, :C1] = rows(base, 3 * C1)
        g_down[t, :, C1:] = rows(base + 3 * C1, 3 * C1)
    for t in range(4):
        g_up[t] = rows(FIRST_ROWS + DOWN_ROWS + t * C2, C2)


def shifted(x, by):
    j = lax.broadcasted_iota(jnp.int32, x.shape, 0) % 16
    moved = pltpu.roll(x, by % x.shape[0], 0)
    return jnp.where(j == (0 if by > 0 else 15), 0.0, moved)


def spread(x):
    return jnp.concatenate(
        [shifted(x[:, C1:], 1).astype(BF16), x.astype(BF16), shifted(x[:, :C1], -1).astype(BF16)], axis=1
    )


def window(ref, a, t):
    part = ref[(a + t) % 2, (a + t) // 2 : (a + t) // 2 + 16]
    return part.reshape(256, part.shape[-1])


def net_kernel(
    start, left, middle, right, fb, rf, rft, wd, rdt, ru,
    left_o, mid_o, right_o, flat,
    fs, cs, xv, hv, gv, g4, gs, bs, can_b, can_g,
):
    start_c = start[0]
    for ref in (xv, hv, gv):
        edge = jnp.zeros((16, ref.shape[-1]), BF16)
        ref[0, 0] = edge
        ref[1, 16] = edge
    g4[16] = jnp.zeros((16, 2 * C2), BF16)

    def stage(r, carry):
        for k, ref in enumerate((left, middle, right)):
            fs[r, 8 + 16 * k : 24 + 16 * k, :] = ref[0, r].astype(F32)
            cs[r, 8 + 16 * k : 24 + 16 * k, :] = ref[1, r].astype(F32)
        return carry

    lax.fori_loop(0, 32, stage, 0, unroll=4)
    j = lax.broadcasted_iota(jnp.int32, (16, C1), 0)

    def load(i, carry):
        for a in range(2):
            r = 2 * i + a
            at = start_c + 8
            before = jnp.where(j == 0, 0.0, fs[r, pl.ds(at - 1, 16, 2), :])
            even = fs[r, pl.ds(at, 16, 2), :]
            odd = fs[r, pl.ds(at + 1, 16, 2), :]
            after = jnp.where(j == 15, 0.0, fs[r, pl.ds(at + 2, 16, 2), :])
            xv[1 - a, i + a] = jnp.concatenate([before, even, odd, after], axis=1).astype(BF16)
            gs[a, i, :, :C1] = cs[r, pl.ds(at, 16, 2), :] * fb[a, i, :, :C1]
            gs[a, i, :, C1:] = cs[r, pl.ds(at + 1, 16, 2), :] * fb[a, i, :, C1:]
        return carry

    lax.fori_loop(0, 16, load, 0, unroll=2)

    h, slope_h = [], []
    for a in range(2):
        pre = dot(window(xv, a, 0), rf[0]) + dot(window(xv, a, 1), rf[1]) + dot(window(xv, a, 2), rf[2])
        sig = lax.logistic(pre)
        value = pre * sig
        slope_h.append(sig + value * (1.0 - sig))
        h.append(value.astype(BF16))
        hv[1 - a, a : a + 16] = jnp.concatenate(
            [shifted(value[:, C1:], 1).astype(BF16), h[a]], axis=1
        ).reshape(16, 16, 3 * C1)
    pre = dot(window(hv, 0, 0), wd[0]) + dot(window(hv, 0, 1), wd[1]) + dot(window(hv, 0, 2), wd[2])
    sig = lax.logistic(pre)
    value = pre * sig
    slope_d = sig + value * (1.0 - sig)
    d = value.astype(BF16)
    d_t = value.T.astype(BF16)
    g_d = jnp.zeros((256, C2), F32)
    for a in range(2):
        out = h[a].astype(F32) + dot(d, ru[a])
        bs[a] = (fb[a].reshape(256, 2 * C1) * out).reshape(16, 16, 2 * C1)
        g = gs[a].reshape(256, 2 * C1).astype(BF16)
        g_d = g_d + dot_nt(g, ru[a])
        g_up = dot(d_t, g).astype(BF16)
        base = FIRST_ROWS + DOWN_ROWS + 2 * a * C2
        flat[base : base + C2] = g_up[:, :C1]
        flat[base + C2 : base + 2 * C2] = g_up[:, C1:]
    g_pre = g_d.astype(BF16).astype(F32) * slope_d
    g4[0:16] = jnp.concatenate([g_pre.astype(BF16), shifted(g_pre, -1).astype(BF16)], axis=1).reshape(
        16, 16, 2 * C2
    )
    g_pre_t = g_pre.T.astype(BF16)
    for t in range(3):
        g_down = dot(g_pre_t, window(hv, 0, t)).T.astype(BF16)
        base = FIRST_ROWS + 6 * t * C1
        flat[base : base + 3 * C1] = g_down[:, :C1]
        flat[base + 3 * C1 : base + 6 * C1] = g_down[:, C1:]
    here = g4[0:16].reshape(256, 2 * C2)
    below = g4[1:17].reshape(256, 2 * C2)
    g_h = [dot_nt(here, rdt[1]), dot_nt(here, rdt[2]) + dot_nt(below, rdt[0])]
    g_t = []
    for a in range(2):
        g_pre = (gs[a].reshape(256, 2 * C1) + g_h[a]) * slope_h[a]
        gv[1 - a, a : a + 16] = spread(g_pre).reshape(16, 16, 4 * C1)
        g_t.append(g_pre.T.astype(BF16))
    for t in range(3):
        g_first = dot(g_t[0], window(xv, 0, t)) + dot(g_t[1], window(xv, 1, t))
        for ct in range(3):
            block = (
                g_first[:C1, ct * C1 : (ct + 1) * C1] + g_first[C1:, (ct + 1) * C1 : (ct + 2) * C1]
            )
            base = (3 * t + ct) * C1
            flat[base : base + C1] = block.T.astype(BF16)
    flat[FIRST_ROWS + DOWN_ROWS + UP_ROWS :] = jnp.zeros(
        (FLAT_ROWS - FIRST_ROWS - DOWN_ROWS - UP_ROWS, C1), BF16
    )
    for a in range(2):
        g_x = (
            dot_nt(window(gv, a, 0), rft[0])
            + dot_nt(window(gv, a, 1), rft[1])
            + dot_nt(window(gv, a, 2), rft[2])
        )
        gs[a] = g_x.reshape(16, 16, 2 * C1)

    def clear(r, carry):
        can_b[r] = jnp.zeros((48, C1), F32)
        can_g[r] = jnp.zeros((48, C1), F32)
        return carry

    lax.fori_loop(0, 32, clear, 0, unroll=4)

    def place(i, carry):
        for a in range(2):
            r = 2 * i + a
            for b in range(2):
                can_b[r, pl.ds(start_c + b, 16, 2), :] = bs[a, i, :, b * C1 : (b + 1) * C1]
                can_g[r, pl.ds(start_c + b, 16, 2), :] = gs[a, i, :, b * C1 : (b + 1) * C1]
        return carry

    lax.fori_loop(0, 16, place, 0, unroll=2)

    def give(r, carry):
        for k, canvas in enumerate((can_b, can_g)):
            left_o[k, r] = canvas[r, 0:16].astype(BF16)
            mid_o[k, r] = canvas[r, 16:32]
            right_o[k, r] = canvas[r, 32:48].astype(BF16)
        return carry

    lax.fori_loop(0, 32, give, 0, unroll=2)


VMEM = pl.BlockSpec(memory_space=pltpu.VMEM)
SMEM = pl.BlockSpec(memory_space=pltpu.SMEM)


def prepared(where, offsets, table, w_first, w_down, w_up):
    return pl.pallas_call(
        prepare_kernel,
        out_shape=(
            jax.ShapeDtypeStruct((2, 16, 16, 2 * C1), F32),
            jax.ShapeDtypeStruct((3, 4 * C1, 2 * C1), BF16),
            jax.ShapeDtypeStruct((3, 2 * C1, 4 * C1), BF16),
            jax.ShapeDtypeStruct((3, 2 * C1, 2 * C2), BF16),
            jax.ShapeDtypeStruct((2, C2, 2 * C1), BF16),
        ),
        in_specs=[SMEM, SMEM, VMEM, VMEM, VMEM, VMEM],
        out_specs=[VMEM] * 5,
        compiler_params=pltpu.CompilerParams(vmem_limit_bytes=16 * 2**20),
        cost_estimate=pl.CostEstimate(flops=5 * 10**6, bytes_accessed=10**7, transcendentals=0),
        name="prepare",
    )(where, offsets, table, w_first, w_down, w_up)


def patch_work(start, left, middle, right, fb, rf, rft, wd, rdt, ru):
    strip = jax.ShapeDtypeStruct((2, 32, 16, C1), BF16)
    return pl.pallas_call(
        net_kernel,
        out_shape=(
            strip,
            jax.ShapeDtypeStruct((2, 32, 16, C1), F32),
            strip,
            jax.ShapeDtypeStruct((FLAT_ROWS, C1), BF16),
        ),
        in_specs=[SMEM] + [VMEM] * 9,
        out_specs=[VMEM] * 4,
        scratch_shapes=[
            pltpu.VMEM((32, 64, C1), F32),
            pltpu.VMEM((32, 64, C1), F32),
            pltpu.VMEM((2, 17, 16, 4 * C1), BF16),
            pltpu.VMEM((2, 17, 16, 3 * C1), BF16),
            pltpu.VMEM((2, 17, 16, 4 * C1), BF16),
            pltpu.VMEM((17, 16, 2 * C2), BF16),
            pltpu.VMEM((2, 16, 16, 2 * C1), F32),
            pltpu.VMEM((2, 16, 16, 2 * C1), F32),
            pltpu.VMEM((32, 48, C1), F32),
            pltpu.VMEM((32, 48, C1), F32),
        ],
        compiler_params=pltpu.CompilerParams(vmem_limit_bytes=40 * 2**20),
        cost_estimate=pl.CostEstimate(flops=2 * 10**9, bytes_accessed=10**7, transcendentals=200000),
        name="patch_work",
    )(start, left, middle, right, fb, rf, rft, wd, rdt, ru)


def small_call(body, name, outs, scratch, *args, smem=0):
    return pl.pallas_call(
        body,
        out_shape=tuple(jax.ShapeDtypeStruct(shape, kind) for shape, kind in outs),
        in_specs=[SMEM] * smem + [VMEM] * (len(args) - smem),
        out_specs=[VMEM] * len(outs),
        scratch_shapes=scratch,
        compiler_params=pltpu.CompilerParams(vmem_limit_bytes=16 * 2**20),
        cost_estimate=pl.CostEstimate(flops=10**6, bytes_accessed=2 * 10**6, transcendentals=0),
        name=name,
    )(*args)


def neighbours(axes, before, after):
    size = lax.axis_size(axes)
    ahead = [(i, i + 1) for i in range(size - 1)]
    back = [(i + 1, i) for i in range(size - 1)]
    return lax.ppermute(before, axes, ahead), lax.ppermute(after, axes, back)


def scattered(x, axes):
    size = lax.axis_size(axes)
    parts = x.reshape(size, x.shape[0] // size, x.shape[1])
    got = lax.all_to_all(parts, axes, 0, 0, tiled=True)
    return got.astype(F32).sum(0).astype(BF16)


def gathered(x, axes):
    size = lax.axis_size(axes)
    parts = jnp.broadcast_to(x[None], (size,) + x.shape)
    return lax.all_to_all(parts, axes, 0, 0, tiled=True)


def spread_back(part):
    for axis in ("y", "x", "core"):
        part = gathered(part, axis).reshape(-1, part.shape[1])
    return part


def per_device(field, cotangent, w_first, w_down, w_up, offsets, blend_table):
    rows_n = lax.axis_size(ROW)
    cols_n = lax.axis_size(COL)
    row_at = lax.axis_index(ROW)
    col_at = lax.axis_index(COL)
    where = jnp.stack([row_at, col_at]).astype(jnp.int32)
    both = jnp.stack([field, cotangent])
    starts = jnp.stack(
        [MARGIN + offsets[row_at, jnp.clip(col_at + step, 0, cols_n - 1), 0] for step in (-1, 0, 1)]
    )
    start_c = (MARGIN + offsets[row_at, col_at, 1])[None]
    fb, rf, rft, rdt, ru = prepared(
        where, offsets.reshape(rows_n, 2 * cols_n), blend_table, w_first, w_down, w_up
    )
    above, under = neighbours(ROW, both, both)
    window_shape = (2, 32, TILE, C1)
    to_left, own, to_right = small_call(
        assemble_kernel,
        "assemble",
        [(window_shape, BF16)] * 3,
        [pltpu.VMEM((2, 48, TILE, C1), BF16)],
        starts,
        above,
        both,
        under,
        smem=1,
    )
    left, right = neighbours(COL, to_right, to_left)
    to_left, own, to_right, flat = patch_work(
        start_c, left, own, right, fb, rf, rft, w_down.reshape(3, 3 * C1, C2), rdt, ru
    )
    from_left, from_right = neighbours(COL, to_right, to_left)
    part = scattered(flat, "core")
    part, from_left, from_right = lax.optimization_barrier((part, from_left, from_right))
    part = scattered(part, "x")
    tile_shape = (2, TILE, TILE, C1)
    up, own, down = small_call(
        combine_kernel,
        "combine",
        [(tile_shape, BF16), (tile_shape, F32), (tile_shape, BF16)],
        [pltpu.VMEM((2, 48, TILE, C1), F32)],
        starts,
        from_left,
        own,
        from_right,
        smem=1,
    )
    from_above, from_under = neighbours(ROW, down, up)
    part, from_above, from_under = lax.optimization_barrier((part, from_above, from_under))
    part = scattered(part, "y")
    part = gathered(part, ("zl", "zh")).astype(F32).sum(0).astype(BF16)
    blended, field_grad = small_call(
        finish_kernel,
        "finish",
        [(field.shape, BF16), (field.shape, F32)],
        [],
        own,
        from_above,
        from_under,
    )
    total = spread_back(part)
    scale = 1.0 / math.sqrt(TILE * rows_n * TILE * cols_n)
    g_first, g_down, g_up = small_call(
        functools.partial(unpack_kernel, scale),
        "unpack",
        [((9, C1, C1), F32), ((3, 3 * C1, C2), F32), ((4, C2, C1), F32)],
        [],
        total,
    )
    return (
        blended,
        field_grad,
        g_first.reshape(w_first.shape),
        g_down.reshape(w_down.shape),
        g_up.reshape(w_up.shape),
    )


def solution(mesh):
    fine = Mesh(mesh.devices.reshape(8, 4, 2, 4, 2), ("y", "zl", "core", "x", "zh"))
    tiles = P(ROW, COL, None)
    return jax.shard_map(
        per_device,
        mesh=fine,
        in_specs=(tiles, tiles, P(), P(), P(), P(), P()),
        out_specs=(tiles, tiles, P(), P(), P()),
        check_vma=False,
    )
```

```python
import functools
import math

import jax
import jax.numpy as jnp
from jax import lax
from jax.experimental import pallas as pl
from jax.experimental.pallas import tpu as pltpu
from jax.sharding import Mesh, PartitionSpec as P

MARGIN = 8
ROW = ("x", "zh")
COL = ("y", "zl", "core")
F32 = jnp.float32
BF16 = jnp.bfloat16
REACH = 2
FAR = 1000
TILE = 16
C1 = 128
C2 = 256
FIRST_ROWS = 9 * C1
DOWN_ROWS = 18 * C1
UP_ROWS = 4 * C2
FLAT_ROWS = 4608


def dot(a, b):
    return lax.dot_general(a, b, (((1,), (0,)), ((), ())), preferred_element_type=F32)


def dot_nt(a, b):
    return lax.dot_general(a, b, (((1,), (1,)), ((), ())), preferred_element_type=F32)


def prepare_kernel(where, offsets, table, w_first, w_down, w_up, fb, rf, rft, rdt, ru):
    row_at, col_at = where[0], where[1]
    rows_n, cols_n = offsets.shape[0], offsets.shape[1] // 2
    sub = lax.broadcasted_iota(jnp.int32, (32, 32), 0)
    lane = lax.broadcasted_iota(jnp.int32, (32, 32), 1)
    column = jnp.where(sub < 16, 2 * sub, 2 * (sub - 16) + 1)
    table_t = table[...].astype(F32).T.astype(BF16)
    own_r = offsets[row_at, 2 * col_at]
    own_c = offsets[row_at, 2 * col_at + 1]
    total = jnp.zeros((32, 32), F32)
    own = jnp.zeros((32, 32), F32)
    for row_step in range(-REACH, REACH + 1):
        for col_step in range(-REACH, REACH + 1):
            near_r, near_c = row_at + row_step, col_at + col_step
            inside = (near_r >= 0) & (near_r < rows_n) & (near_c >= 0) & (near_c < cols_n)
            at_r = jnp.clip(near_r, 0, rows_n - 1)
            at_c = jnp.clip(near_c, 0, cols_n - 1)
            down_by = row_step * TILE + offsets[at_r, 2 * at_c] - own_r
            right_by = col_step * TILE + offsets[at_r, 2 * at_c + 1] - own_c
            down_by = jnp.where(inside, down_by, FAR)
            pick_c = (column - right_by == lane).astype(F32).astype(BF16)
            pick_r = (lane - down_by == sub).astype(F32).astype(BF16)
            placed = dot(pick_c, table_t)
            if row_step == 0 and col_step == 0:
                own = placed
            total = total + dot(placed.astype(BF16), pick_r)
    share = own / total
    for r in range(32):
        fb[r % 2, r // 2, :, :C1] = jnp.broadcast_to(share[:16, r : r + 1], (16, C1))
        fb[r % 2, r // 2, :, C1:] = jnp.broadcast_to(share[16:, r : r + 1], (16, C1))
    none = jnp.zeros((C1, C1), BF16)
    for t in range(3):
        for v in range(4):
            for b in range(2):
                rows, cols = pl.ds(v * C1, C1), pl.ds(b * C1, C1)
                held = 0 <= v - b <= 2
                rf[t, rows, cols] = w_first[t, v - b] if held else none
                rft[t, cols, rows] = w_first[2 - t, 2 - v + b] if held else none
        rdt[t, :C1, :C2] = w_down[t, 1]
        rdt[t, :C1, C2:] = jnp.zeros((C1, C2), BF16)
        rdt[t, C1:, :C2] = w_down[t, 2]
        rdt[t, C1:, C2:] = w_down[t, 0]
    for a in range(2):
        for b in range(2):
            ru[a, :, pl.ds(b * C1, C1)] = w_up[a, b]


def assemble_kernel(starts, above, both, under, to_left, own, to_right, grown):
    grown[:, 0:16] = above[...]
    grown[:, 16:32] = both[...]
    grown[:, 32:48] = under[...]
    for side, out in enumerate((to_left, own, to_right)):
        out[...] = grown[:, pl.ds(starts[side], 32)]


def combine_kernel(starts, from_left, own, from_right, up, mid, down, canvas):
    canvas[...] = jnp.zeros_like(canvas)
    canvas[:, pl.ds(starts[1], 32)] = own[...]
    for side, part in ((0, from_left), (2, from_right)):
        spot = (slice(None), pl.ds(starts[side], 32))
        canvas[spot] = canvas[spot] + part[...].astype(F32)
    up[...] = canvas[:, 0:16].astype(BF16)
    mid[...] = canvas[:, 16:32]
    down[...] = canvas[:, 32:48].astype(BF16)


def finish_kernel(own, from_above, from_under, blended, field_grad):
    total = own[...] + from_above[...].astype(F32) + from_under[...].astype(F32)
    blended[...] = total[0].astype(BF16)
    field_grad[...] = total[1]


def unpack_kernel(scale, halves, g_first, g_down, g_up):
    def rows(base, count):
        return halves[base : base + count].astype(F32) * scale

    for t in range(9):
        g_first[t] = rows(t * C1, C1)
    for t in range(3):
        base = FIRST_ROWS + 6 * t * C1
        g_down[t, :, :C1] = rows(base, 3 * C1)
        g_down[t, :, C1:] = rows(base + 3 * C1, 3 * C1)
    for t in range(4):
        g_up[t] = rows(FIRST_ROWS + DOWN_ROWS + t * C2, C2)


def shifted(x, by):
    j = lax.broadcasted_iota(jnp.int32, x.shape, 0) % 16
    moved = pltpu.roll(x, by % x.shape[0], 0)
    return jnp.where(j == (0 if by > 0 else 15), 0.0, moved)


def spread(x):
    return jnp.concatenate(
        [shifted(x[:, C1:], 1).astype(BF16), x.astype(BF16), shifted(x[:, :C1], -1).astype(BF16)], axis=1
    )


def window(ref, a, t):
    part = ref[(a + t) % 2, (a + t) // 2 : (a + t) // 2 + 16]
    return part.reshape(256, part.shape[-1])


def net_kernel(
    start, left, middle, right, fb, rf, rft, wd, rdt, ru,
    left_o, mid_o, right_o, flat,
    fs, cs, xv, hv, gv, g4, gs, bs, can_b, can_g,
):
    start_c = start[0]
    for ref in (xv, hv, gv):
        edge = jnp.zeros((16, ref.shape[-1]), BF16)
        ref[0, 0] = edge
        ref[1, 16] = edge
    g4[16] = jnp.zeros((16, 2 * C2), BF16)

    def stage(r, carry):
        for k, ref in enumerate((left, middle, right)):
            fs[r, 8 + 16 * k : 24 + 16 * k, :] = ref[0, r].astype(F32)
            cs[r, 8 + 16 * k : 24 + 16 * k, :] = ref[1, r].astype(F32)
        return carry

    lax.fori_loop(0, 32, stage, 0, unroll=4)
    j = lax.broadcasted_iota(jnp.int32, (16, C1), 0)

    def load(i, carry):
        for a in range(2):
            r = 2 * i + a
            at = start_c + 8
            before = jnp.where(j == 0, 0.0, fs[r, pl.ds(at - 1, 16, 2), :])
            even = fs[r, pl.ds(at, 16, 2), :]
            odd = fs[r, pl.ds(at + 1, 16, 2), :]
            after = jnp.where(j == 15, 0.0, fs[r, pl.ds(at + 2, 16, 2), :])
            xv[1 - a, i + a] = jnp.concatenate([before, even, odd, after], axis=1).astype(BF16)
            gs[a, i, :, :C1] = cs[r, pl.ds(at, 16, 2), :] * fb[a, i, :, :C1]
            gs[a, i, :, C1:] = cs[r, pl.ds(at + 1, 16, 2), :] * fb[a, i, :, C1:]
        return carry

    lax.fori_loop(0, 16, load, 0, unroll=2)

    h, slope_h = [], []
    for a in range(2):
        pre = dot(window(xv, a, 0), rf[0]) + dot(window(xv, a, 1), rf[1]) + dot(window(xv, a, 2), rf[2])
        sig = lax.logistic(pre)
        value = pre * sig
        slope_h.append(sig + value * (1.0 - sig))
        h.append(value.astype(BF16))
        hv[1 - a, a : a + 16] = jnp.concatenate(
            [shifted(value[:, C1:], 1).astype(BF16), h[a]], axis=1
        ).reshape(16, 16, 3 * C1)
    pre = dot(window(hv, 0, 0), wd[0]) + dot(window(hv, 0, 1), wd[1]) + dot(window(hv, 0, 2), wd[2])
    sig = lax.logistic(pre)
    value = pre * sig
    slope_d = sig + value * (1.0 - sig)
    d = value.astype(BF16)
    d_t = value.T.astype(BF16)
    g_d = jnp.zeros((256, C2), F32)
    for a in range(2):
        out = h[a].astype(F32) + dot(d, ru[a])
        bs[a] = (fb[a].reshape(256, 2 * C1) * out).reshape(16, 16, 2 * C1)
        g = gs[a].reshape(256, 2 * C1).astype(BF16)
        g_d = g_d + dot_nt(g, ru[a])
        g_up = dot(d_t, g).astype(BF16)
        base = FIRST_ROWS + DOWN_ROWS + 2 * a * C2
        flat[base : base + C2] = g_up[:, :C1]
        flat[base + C2 : base + 2 * C2] = g_up[:, C1:]
    g_pre = g_d.astype(BF16).astype(F32) * slope_d
    g4[0:16] = jnp.concatenate([g_pre.astype(BF16), shifted(g_pre, -1).astype(BF16)], axis=1).reshape(
        16, 16, 2 * C2
    )
    g_pre_t = g_pre.T.astype(BF16)
    for t in range(3):
        g_down = dot(g_pre_t, window(hv, 0, t)).T.astype(BF16)
        base = FIRST_ROWS + 6 * t * C1
        flat[base : base + 3 * C1] = g_down[:, :C1]
        flat[base + 3 * C1 : base + 6 * C1] = g_down[:, C1:]
    here = g4[0:16].reshape(256, 2 * C2)
    below = g4[1:17].reshape(256, 2 * C2)
    g_h = [dot_nt(here, rdt[1]), dot_nt(here, rdt[2]) + dot_nt(below, rdt[0])]
    g_t = []
    for a in range(2):
        g_pre = (gs[a].reshape(256, 2 * C1) + g_h[a]) * slope_h[a]
        gv[1 - a, a : a + 16] = spread(g_pre).reshape(16, 16, 4 * C1)
        g_t.append(g_pre.T.astype(BF16))
    for t in range(3):
        g_first = dot(g_t[0], window(xv, 0, t)) + dot(g_t[1], window(xv, 1, t))
        for ct in range(3):
            block = (
                g_first[:C1, ct * C1 : (ct + 1) * C1] + g_first[C1:, (ct + 1) * C1 : (ct + 2) * C1]
            )
            base = (3 * t + ct) * C1
            flat[base : base + C1] = block.T.astype(BF16)
    flat[FIRST_ROWS + DOWN_ROWS + UP_ROWS :] = jnp.zeros(
        (FLAT_ROWS - FIRST_ROWS - DOWN_ROWS - UP_ROWS, C1), BF16
    )
    for a in range(2):
        g_x = (
            dot_nt(window(gv, a, 0), rft[0])
            + dot_nt(window(gv, a, 1), rft[1])
            + dot_nt(window(gv, a, 2), rft[2])
        )
        gs[a] = g_x.reshape(16, 16, 2 * C1)

    def clear(r, carry):
        can_b[r] = jnp.zeros((48, C1), F32)
        can_g[r] = jnp.zeros((48, C1), F32)
        return carry

    lax.fori_loop(0, 32, clear, 0, unroll=4)

    def place(i, carry):
        for a in range(2):
            r = 2 * i + a
            for b in range(2):
                can_b[r, pl.ds(start_c + b, 16, 2), :] = bs[a, i, :, b * C1 : (b + 1) * C1]
                can_g[r, pl.ds(start_c + b, 16, 2), :] = gs[a, i, :, b * C1 : (b + 1) * C1]
        return carry

    lax.fori_loop(0, 16, place, 0, unroll=2)

    def give(r, carry):
        for k, canvas in enumerate((can_b, can_g)):
            left_o[k, r] = canvas[r, 0:16].astype(BF16)
            mid_o[k, r] = canvas[r, 16:32]
            right_o[k, r] = canvas[r, 32:48].astype(BF16)
        return carry

    lax.fori_loop(0, 32, give, 0, unroll=2)


VMEM = pl.BlockSpec(memory_space=pltpu.VMEM)
SMEM = pl.BlockSpec(memory_space=pltpu.SMEM)


def prepared(where, offsets, table, w_first, w_down, w_up):
    return pl.pallas_call(
        prepare_kernel,
        out_shape=(
            jax.ShapeDtypeStruct((2, 16, 16, 2 * C1), F32),
            jax.ShapeDtypeStruct((3, 4 * C1, 2 * C1), BF16),
            jax.ShapeDtypeStruct((3, 2 * C1, 4 * C1), BF16),
            jax.ShapeDtypeStruct((3, 2 * C1, 2 * C2), BF16),
            jax.ShapeDtypeStruct((2, C2, 2 * C1), BF16),
        ),
        in_specs=[SMEM, SMEM, VMEM, VMEM, VMEM, VMEM],
        out_specs=[VMEM] * 5,
        compiler_params=pltpu.CompilerParams(vmem_limit_bytes=10 * 2**20),
        cost_estimate=pl.CostEstimate(flops=5 * 10**6, bytes_accessed=10**7, transcendentals=0),
        name="prepare",
    )(where, offsets, table, w_first, w_down, w_up)


def patch_work(start, left, middle, right, fb, rf, rft, wd, rdt, ru):
    strip = jax.ShapeDtypeStruct((2, 32, 16, C1), BF16)
    return pl.pallas_call(
        net_kernel,
        out_shape=(
            strip,
            jax.ShapeDtypeStruct((2, 32, 16, C1), F32),
            strip,
            jax.ShapeDtypeStruct((FLAT_ROWS, C1), BF16),
        ),
        in_specs=[SMEM] + [VMEM] * 9,
        out_specs=[VMEM] * 4,
        scratch_shapes=[
            pltpu.VMEM((32, 64, C1), F32),
            pltpu.VMEM((32, 64, C1), F32),
            pltpu.VMEM((2, 17, 16, 4 * C1), BF16),
            pltpu.VMEM((2, 17, 16, 3 * C1), BF16),
            pltpu.VMEM((2, 17, 16, 4 * C1), BF16),
            pltpu.VMEM((17, 16, 2 * C2), BF16),
            pltpu.VMEM((2, 16, 16, 2 * C1), F32),
            pltpu.VMEM((2, 16, 16, 2 * C1), F32),
            pltpu.VMEM((32, 48, C1), F32),
            pltpu.VMEM((32, 48, C1), F32),
        ],
        compiler_params=pltpu.CompilerParams(vmem_limit_bytes=24 * 2**20),
        cost_estimate=pl.CostEstimate(flops=2 * 10**9, bytes_accessed=10**7, transcendentals=200000),
        name="patch_work",
    )(start, left, middle, right, fb, rf, rft, wd, rdt, ru)


def small_call(body, name, outs, scratch, *args, smem=0):
    return pl.pallas_call(
        body,
        out_shape=tuple(jax.ShapeDtypeStruct(shape, kind) for shape, kind in outs),
        in_specs=[SMEM] * smem + [VMEM] * (len(args) - smem),
        out_specs=[VMEM] * len(outs),
        scratch_shapes=scratch,
        compiler_params=pltpu.CompilerParams(vmem_limit_bytes=10 * 2**20),
        cost_estimate=pl.CostEstimate(flops=10**6, bytes_accessed=2 * 10**6, transcendentals=0),
        name=name,
    )(*args)


def from_before(axes, x):
    return lax.ppermute(x, axes, [(i, i + 1) for i in range(lax.axis_size(axes) - 1)])


def from_after(axes, x):
    return lax.ppermute(x, axes, [(i + 1, i) for i in range(lax.axis_size(axes) - 1)])


def scattered(x, axes):
    size = lax.axis_size(axes)
    parts = x.reshape(size, x.shape[0] // size, x.shape[1])
    got = lax.all_to_all(parts, axes, 0, 0, tiled=True)
    return got.astype(F32).sum(0).astype(BF16)


def gathered(x, axes):
    size = lax.axis_size(axes)
    parts = jnp.broadcast_to(x[None], (size,) + x.shape)
    return lax.all_to_all(parts, axes, 0, 0, tiled=True)


def per_device(field, cotangent, w_first, w_down, w_up, offsets, blend_table):
    rows_n = lax.axis_size(ROW)
    cols_n = lax.axis_size(COL)
    row_at = lax.axis_index(ROW)
    col_at = lax.axis_index(COL)
    where = jnp.stack([row_at, col_at]).astype(jnp.int32)
    both = jnp.stack([field, cotangent])
    starts = jnp.stack(
        [MARGIN + offsets[row_at, jnp.clip(col_at + step, 0, cols_n - 1), 0] for step in (-1, 0, 1)]
    )
    start_c = (MARGIN + offsets[row_at, col_at, 1])[None]
    fb, rf, rft, rdt, ru = prepared(
        where, offsets.reshape(rows_n, 2 * cols_n), blend_table, w_first, w_down, w_up
    )
    above, under = from_before(ROW, both), from_after(ROW, both)
    window_shape = (2, 32, TILE, C1)
    to_left, own, to_right = small_call(
        assemble_kernel,
        "assemble",
        [(window_shape, BF16)] * 3,
        [pltpu.VMEM((2, 48, TILE, C1), BF16)],
        starts,
        above,
        both,
        under,
        smem=1,
    )
    left, right = from_before(COL, to_right), from_after(COL, to_left)
    to_left, own, to_right, flat = patch_work(
        start_c, left, own, right, fb, rf, rft, w_down.reshape(3, 3 * C1, C2), rdt, ru
    )
    from_left = from_before(COL, to_right)
    part = scattered(flat, "core")
    part = scattered(part, "x")
    part, from_left, to_left = lax.optimization_barrier((part, from_left, to_left))
    from_right = from_after(COL, to_left)
    part = scattered(part, "y")
    part, from_left, from_right = lax.optimization_barrier((part, from_left, from_right))
    part = gathered(part, ("zl", "zh")).astype(F32).sum(0).astype(BF16)
    tile_shape = (2, TILE, TILE, C1)
    up, own, down = small_call(
        combine_kernel,
        "combine",
        [(tile_shape, BF16), (tile_shape, F32), (tile_shape, BF16)],
        [pltpu.VMEM((2, 48, TILE, C1), F32)],
        starts,
        from_left,
        own,
        from_right,
        smem=1,
    )
    part, up, own, down = lax.optimization_barrier((part, up, own, down))
    from_above = from_before(ROW, down)
    part = gathered(part, "y").reshape(-1, C1)
    part, from_above, up = lax.optimization_barrier((part, from_above, up))
    from_under = from_after(ROW, up)
    part = gathered(part, "x").reshape(-1, C1)
    part, from_above, from_under = lax.optimization_barrier((part, from_above, from_under))
    total = gathered(part, "core").reshape(-1, C1)
    blended, field_grad = small_call(
        finish_kernel,
        "finish",
        [(field.shape, BF16), (field.shape, F32)],
        [],
        own,
        from_above,
        from_under,
    )
    scale = 1.0 / math.sqrt(TILE * rows_n * TILE * cols_n)
    g_first, g_down, g_up = small_call(
        functools.partial(unpack_kernel, scale),
        "unpack",
        [((9, C1, C1), F32), ((3, 3 * C1, C2), F32), ((4, C2, C1), F32)],
        [],
        total,
    )
    return (
        blended,
        field_grad,
        g_first.reshape(w_first.shape),
        g_down.reshape(w_down.shape),
        g_up.reshape(w_up.shape),
    )


def solution(mesh):
    fine = Mesh(mesh.devices.reshape(8, 4, 2, 4, 2), ("y", "zl", "core", "x", "zh"))
    tiles = P(ROW, COL, None)
    return jax.shard_map(
        per_device,
        mesh=fine,
        in_specs=(tiles, tiles, P(), P(), P(), P(), P()),
        out_specs=(tiles, tiles, P(), P(), P()),
        check_vma=False,
    )
```

```python
import functools
import math

import jax
import jax.numpy as jnp
from jax import lax
from jax.experimental import pallas as pl
from jax.experimental.pallas import tpu as pltpu
from jax.sharding import Mesh, PartitionSpec as P

MARGIN = 8
ROW = ("x", "zh")
COL = ("y", "zl", "core")
F32 = jnp.float32
BF16 = jnp.bfloat16
REACH = 2
FAR = 1000
TILE = 16
C1 = 128
C2 = 256
FIRST_ROWS = 9 * C1
DOWN_ROWS = 18 * C1
UP_ROWS = 4 * C2
USED_ROWS = FIRST_ROWS + DOWN_ROWS + UP_ROWS
HALF_ROWS = 2304


def dot(a, b):
    return lax.dot_general(a, b, (((1,), (0,)), ((), ())), preferred_element_type=F32)


def dot_nt(a, b):
    return lax.dot_general(a, b, (((1,), (1,)), ((), ())), preferred_element_type=F32)


def prepare_kernel(where, offsets, table, w_first, w_down, w_up, fb, rf, rft, rdt, ru):
    row_at, col_at = where[0], where[1]
    rows_n, cols_n = offsets.shape[0], offsets.shape[1] // 2
    sub = lax.broadcasted_iota(jnp.int32, (32, 32), 0)
    lane = lax.broadcasted_iota(jnp.int32, (32, 32), 1)
    column = jnp.where(sub < 16, 2 * sub, 2 * (sub - 16) + 1)
    table_t = table[...].astype(F32).T.astype(BF16)
    own_r = offsets[row_at, 2 * col_at]
    own_c = offsets[row_at, 2 * col_at + 1]
    total = jnp.zeros((32, 32), F32)
    own = jnp.zeros((32, 32), F32)
    for row_step in range(-REACH, REACH + 1):
        for col_step in range(-REACH, REACH + 1):
            near_r, near_c = row_at + row_step, col_at + col_step
            inside = (near_r >= 0) & (near_r < rows_n) & (near_c >= 0) & (near_c < cols_n)
            at_r = jnp.clip(near_r, 0, rows_n - 1)
            at_c = jnp.clip(near_c, 0, cols_n - 1)
            down_by = row_step * TILE + offsets[at_r, 2 * at_c] - own_r
            right_by = col_step * TILE + offsets[at_r, 2 * at_c + 1] - own_c
            down_by = jnp.where(inside, down_by, FAR)
            pick_c = (column - right_by == lane).astype(F32).astype(BF16)
            pick_r = (lane - down_by == sub).astype(F32).astype(BF16)
            placed = dot(pick_c, table_t)
            if row_step == 0 and col_step == 0:
                own = placed
            total = total + dot(placed.astype(BF16), pick_r)
    share = own / total
    for r in range(32):
        fb[r % 2, r // 2, :, :C1] = jnp.broadcast_to(share[:16, r : r + 1], (16, C1))
        fb[r % 2, r // 2, :, C1:] = jnp.broadcast_to(share[16:, r : r + 1], (16, C1))
    none = jnp.zeros((C1, C1), BF16)
    for t in range(3):
        for v in range(4):
            for b in range(2):
                rows, cols = pl.ds(v * C1, C1), pl.ds(b * C1, C1)
                held = 0 <= v - b <= 2
                rf[t, rows, cols] = w_first[t, v - b] if held else none
                rft[t, cols, rows] = w_first[2 - t, 2 - v + b] if held else none
        rdt[t, :C1, :C2] = w_down[t, 1]
        rdt[t, :C1, C2:] = jnp.zeros((C1, C2), BF16)
        rdt[t, C1:, :C2] = w_down[t, 2]
        rdt[t, C1:, C2:] = w_down[t, 0]
    for a in range(2):
        for b in range(2):
            ru[a, :, pl.ds(b * C1, C1)] = w_up[a, b]


def assemble_kernel(starts, above, both, under, to_left, own, to_right, grown):
    grown[:, 0:16] = above[...]
    grown[:, 16:32] = both[...]
    grown[:, 32:48] = under[...]
    for side, out in enumerate((to_left, own, to_right)):
        out[...] = grown[:, pl.ds(starts[side], 32)]


def add_left_kernel(starts, from_left, own, canvas):
    canvas[...] = jnp.zeros_like(canvas)
    canvas[:, pl.ds(starts[1], 32)] = own[...]
    spot = (slice(None), pl.ds(starts[0], 32))
    canvas[spot] = canvas[spot] + from_left[...].astype(F32)


def add_right_kernel(starts, given, from_right, up, mid, down, canvas):
    canvas[...] = given[...]
    spot = (slice(None), pl.ds(starts[2], 32))
    canvas[spot] = canvas[spot] + from_right[...].astype(F32)
    up[...] = canvas[:, 0:16].astype(BF16)
    mid[...] = canvas[:, 16:32]
    down[...] = canvas[:, 32:48].astype(BF16)


def finish_kernel(own, from_above, from_under, blended, field_grad):
    total = own[...] + from_above[...].astype(F32) + from_under[...].astype(F32)
    blended[...] = total[0].astype(BF16)
    field_grad[...] = total[1]


def unpack_kernel(scale, core, own, other, g_first, g_down, g_up, halves):
    halves[core[0]] = own[...]
    halves[1 - core[0]] = other[...]

    def rows(base, count):
        half, at = base // HALF_ROWS, base % HALF_ROWS
        return halves[half, at : at + count].astype(F32) * scale

    for t in range(9):
        g_first[t] = rows(t * C1, C1)
    for t in range(3):
        base = FIRST_ROWS + 6 * t * C1
        g_down[t, :, :C1] = rows(base, 3 * C1)
        g_down[t, :, C1:] = rows(base + 3 * C1, 3 * C1)
    for t in range(4):
        g_up[t] = rows(FIRST_ROWS + DOWN_ROWS + t * C2, C2)


def shifted(x, by):
    j = lax.broadcasted_iota(jnp.int32, x.shape, 0) % 16
    moved = pltpu.roll(x, by % x.shape[0], 0)
    return jnp.where(j == (0 if by > 0 else 15), 0.0, moved)


def spread(x):
    return jnp.concatenate(
        [shifted(x[:, C1:], 1).astype(BF16), x.astype(BF16), shifted(x[:, :C1], -1).astype(BF16)], axis=1
    )


def window(ref, a, t):
    part = ref[(a + t) % 2, (a + t) // 2 : (a + t) // 2 + 16]
    return part.reshape(256, part.shape[-1])


def net_kernel(
    start, left, middle, right, fb, rf, rft, wd, rdt, ru,
    left_o, mid_o, right_o, keep, send,
    fs, cs, xv, hv, gv, g4, gs, bs, can_b, can_g, halves,
):
    start_c, core = start[0], start[1]

    def put(base, value):
        half, at = base // HALF_ROWS, base % HALF_ROWS
        halves[core if half == 0 else 1 - core, at : at + value.shape[0]] = value.astype(BF16)

    for ref in (xv, hv, gv):
        edge = jnp.zeros((16, ref.shape[-1]), BF16)
        ref[0, 0] = edge
        ref[1, 16] = edge
    g4[16] = jnp.zeros((16, 2 * C2), BF16)

    def stage(r, carry):
        for k, ref in enumerate((left, middle, right)):
            fs[r, 8 + 16 * k : 24 + 16 * k, :] = ref[0, r].astype(F32)
            cs[r, 8 + 16 * k : 24 + 16 * k, :] = ref[1, r].astype(F32)
        return carry

    lax.fori_loop(0, 32, stage, 0, unroll=4)
    j = lax.broadcasted_iota(jnp.int32, (16, C1), 0)

    def load(i, carry):
        for a in range(2):
            r = 2 * i + a
            at = start_c + 8
            before = jnp.where(j == 0, 0.0, fs[r, pl.ds(at - 1, 16, 2), :])
            even = fs[r, pl.ds(at, 16, 2), :]
            odd = fs[r, pl.ds(at + 1, 16, 2), :]
            after = jnp.where(j == 15, 0.0, fs[r, pl.ds(at + 2, 16, 2), :])
            xv[1 - a, i + a] = jnp.concatenate([before, even, odd, after], axis=1).astype(BF16)
            gs[a, i, :, :C1] = cs[r, pl.ds(at, 16, 2), :] * fb[a, i, :, :C1]
            gs[a, i, :, C1:] = cs[r, pl.ds(at + 1, 16, 2), :] * fb[a, i, :, C1:]
        return carry

    lax.fori_loop(0, 16, load, 0, unroll=2)

    h, slope_h = [], []
    for a in range(2):
        pre = dot(window(xv, a, 0), rf[0]) + dot(window(xv, a, 1), rf[1]) + dot(window(xv, a, 2), rf[2])
        sig = lax.logistic(pre)
        value = pre * sig
        slope_h.append(sig + value * (1.0 - sig))
        h.append(value.astype(BF16))
        hv[1 - a, a : a + 16] = jnp.concatenate(
            [shifted(value[:, C1:], 1).astype(BF16), h[a]], axis=1
        ).reshape(16, 16, 3 * C1)
    pre = dot(window(hv, 0, 0), wd[0]) + dot(window(hv, 0, 1), wd[1]) + dot(window(hv, 0, 2), wd[2])
    sig = lax.logistic(pre)
    value = pre * sig
    slope_d = sig + value * (1.0 - sig)
    d = value.astype(BF16)
    d_t = value.T.astype(BF16)
    g_d = jnp.zeros((256, C2), F32)
    for a in range(2):
        out = h[a].astype(F32) + dot(d, ru[a])
        bs[a] = (fb[a].reshape(256, 2 * C1) * out).reshape(16, 16, 2 * C1)
        g = gs[a].reshape(256, 2 * C1).astype(BF16)
        g_d = g_d + dot_nt(g, ru[a])
        g_up = dot(d_t, g)
        base = FIRST_ROWS + DOWN_ROWS + 2 * a * C2
        put(base, g_up[:, :C1])
        put(base + C2, g_up[:, C1:])
    g_pre = g_d.astype(BF16).astype(F32) * slope_d
    g4[0:16] = jnp.concatenate([g_pre.astype(BF16), shifted(g_pre, -1).astype(BF16)], axis=1).reshape(
        16, 16, 2 * C2
    )
    g_pre_t = g_pre.T.astype(BF16)
    for t in range(3):
        g_down = dot(g_pre_t, window(hv, 0, t)).T
        base = FIRST_ROWS + 6 * t * C1
        put(base, g_down[:, :C1])
        put(base + 3 * C1, g_down[:, C1:])
    here = g4[0:16].reshape(256, 2 * C2)
    below = g4[1:17].reshape(256, 2 * C2)
    g_h = [dot_nt(here, rdt[1]), dot_nt(here, rdt[2]) + dot_nt(below, rdt[0])]
    g_t = []
    for a in range(2):
        g_pre = (gs[a].reshape(256, 2 * C1) + g_h[a]) * slope_h[a]
        gv[1 - a, a : a + 16] = spread(g_pre).reshape(16, 16, 4 * C1)
        g_t.append(g_pre.T.astype(BF16))
    for t in range(3):
        g_first = dot(g_t[0], window(xv, 0, t)) + dot(g_t[1], window(xv, 1, t))
        for ct in range(3):
            block = (
                g_first[:C1, ct * C1 : (ct + 1) * C1] + g_first[C1:, (ct + 1) * C1 : (ct + 2) * C1]
            )
            put((3 * t + ct) * C1, block.T)
    put(USED_ROWS, jnp.zeros((2 * HALF_ROWS - USED_ROWS, C1), F32))
    keep[...] = halves[0]
    send[...] = halves[1]
    for a in range(2):
        g_x = (
            dot_nt(window(gv, a, 0), rft[0])
            + dot_nt(window(gv, a, 1), rft[1])
            + dot_nt(window(gv, a, 2), rft[2])
        )
        gs[a] = g_x.reshape(16, 16, 2 * C1)

    def clear(r, carry):
        can_b[r] = jnp.zeros((48, C1), F32)
        can_g[r] = jnp.zeros((48, C1), F32)
        return carry

    lax.fori_loop(0, 32, clear, 0, unroll=4)

    def place(i, carry):
        for a in range(2):
            r = 2 * i + a
            for b in range(2):
                can_b[r, pl.ds(start_c + b, 16, 2), :] = bs[a, i, :, b * C1 : (b + 1) * C1]
                can_g[r, pl.ds(start_c + b, 16, 2), :] = gs[a, i, :, b * C1 : (b + 1) * C1]
        return carry

    lax.fori_loop(0, 16, place, 0, unroll=2)

    def give(r, carry):
        for k, canvas in enumerate((can_b, can_g)):
            left_o[k, r] = canvas[r, 0:16].astype(BF16)
            mid_o[k, r] = canvas[r, 16:32]
            right_o[k, r] = canvas[r, 32:48].astype(BF16)
        return carry

    lax.fori_loop(0, 32, give, 0, unroll=2)


VMEM = pl.BlockSpec(memory_space=pltpu.VMEM)
SMEM = pl.BlockSpec(memory_space=pltpu.SMEM)


def prepared(where, offsets, table, w_first, w_down, w_up):
    return pl.pallas_call(
        prepare_kernel,
        out_shape=(
            jax.ShapeDtypeStruct((2, 16, 16, 2 * C1), F32),
            jax.ShapeDtypeStruct((3, 4 * C1, 2 * C1), BF16),
            jax.ShapeDtypeStruct((3, 2 * C1, 4 * C1), BF16),
            jax.ShapeDtypeStruct((3, 2 * C1, 2 * C2), BF16),
            jax.ShapeDtypeStruct((2, C2, 2 * C1), BF16),
        ),
        in_specs=[SMEM, SMEM, VMEM, VMEM, VMEM, VMEM],
        out_specs=[VMEM] * 5,
        compiler_params=pltpu.CompilerParams(vmem_limit_bytes=10 * 2**20),
        cost_estimate=pl.CostEstimate(flops=5 * 10**6, bytes_accessed=10**7, transcendentals=0),
        name="prepare",
    )(where, offsets, table, w_first, w_down, w_up)


def patch_work(start, left, middle, right, fb, rf, rft, wd, rdt, ru):
    strip = jax.ShapeDtypeStruct((2, 32, 16, C1), BF16)
    return pl.pallas_call(
        net_kernel,
        out_shape=(
            strip,
            jax.ShapeDtypeStruct((2, 32, 16, C1), F32),
            strip,
            jax.ShapeDtypeStruct((HALF_ROWS, C1), BF16),
            jax.ShapeDtypeStruct((HALF_ROWS, C1), BF16),
        ),
        in_specs=[SMEM] + [VMEM] * 9,
        out_specs=[VMEM] * 5,
        scratch_shapes=[
            pltpu.VMEM((32, 64, C1), F32),
            pltpu.VMEM((32, 64, C1), F32),
            pltpu.VMEM((2, 17, 16, 4 * C1), BF16),
            pltpu.VMEM((2, 17, 16, 3 * C1), BF16),
            pltpu.VMEM((2, 17, 16, 4 * C1), BF16),
            pltpu.VMEM((17, 16, 2 * C2), BF16),
            pltpu.VMEM((2, 16, 16, 2 * C1), F32),
            pltpu.VMEM((2, 16, 16, 2 * C1), F32),
            pltpu.VMEM((32, 48, C1), F32),
            pltpu.VMEM((32, 48, C1), F32),
            pltpu.VMEM((2, HALF_ROWS, C1), BF16),
        ],
        compiler_params=pltpu.CompilerParams(vmem_limit_bytes=24 * 2**20),
        cost_estimate=pl.CostEstimate(flops=2 * 10**9, bytes_accessed=10**7, transcendentals=200000),
        name="patch_work",
    )(start, left, middle, right, fb, rf, rft, wd, rdt, ru)


def small_call(body, name, outs, scratch, *args, smem=0):
    return pl.pallas_call(
        body,
        out_shape=tuple(jax.ShapeDtypeStruct(shape, kind) for shape, kind in outs),
        in_specs=[SMEM] * smem + [VMEM] * (len(args) - smem),
        out_specs=[VMEM] * len(outs),
        scratch_shapes=scratch,
        compiler_params=pltpu.CompilerParams(vmem_limit_bytes=10 * 2**20),
        cost_estimate=pl.CostEstimate(flops=10**6, bytes_accessed=2 * 10**6, transcendentals=0),
        name=name,
    )(*args)


def from_before(axes, x):
    return lax.ppermute(x, axes, [(i, i + 1) for i in range(lax.axis_size(axes) - 1)])


def from_after(axes, x):
    return lax.ppermute(x, axes, [(i + 1, i) for i in range(lax.axis_size(axes) - 1)])


def swapped(x):
    return lax.ppermute(x, "core", [(0, 1), (1, 0)])


def added(x, y):
    return (x.astype(F32) + y.astype(F32)).astype(BF16)


def scattered(x, axes):
    size = lax.axis_size(axes)
    parts = x.reshape(size, x.shape[0] // size, x.shape[1])
    got = lax.all_to_all(parts, axes, 0, 0, tiled=True)
    return got.astype(F32).sum(0).astype(BF16)


def gathered(x, axes):
    size = lax.axis_size(axes)
    parts = jnp.broadcast_to(x[None], (size,) + x.shape)
    return lax.all_to_all(parts, axes, 0, 0, tiled=True)


def per_device(field, cotangent, w_first, w_down, w_up, offsets, blend_table):
    rows_n = lax.axis_size(ROW)
    cols_n = lax.axis_size(COL)
    row_at = lax.axis_index(ROW)
    col_at = lax.axis_index(COL)
    where = jnp.stack([row_at, col_at]).astype(jnp.int32)
    both = jnp.stack([field, cotangent])
    starts = jnp.stack(
        [MARGIN + offsets[row_at, jnp.clip(col_at + step, 0, cols_n - 1), 0] for step in (-1, 0, 1)]
    )
    core = lax.axis_index("core").astype(jnp.int32)
    start = jnp.stack([MARGIN + offsets[row_at, col_at, 1], core])
    fb, rf, rft, rdt, ru = prepared(
        where, offsets.reshape(rows_n, 2 * cols_n), blend_table, w_first, w_down, w_up
    )
    above, under = from_before(ROW, both), from_after(ROW, both)
    above, under, fb, rf, rft, rdt, ru = lax.optimization_barrier((above, under, fb, rf, rft, rdt, ru))
    window_shape = (2, 32, TILE, C1)
    to_left, own, to_right = small_call(
        assemble_kernel,
        "assemble",
        [(window_shape, BF16)] * 3,
        [pltpu.VMEM((2, 48, TILE, C1), BF16)],
        starts,
        above,
        both,
        under,
        smem=1,
    )
    left, right = from_before(COL, to_right), from_after(COL, to_left)
    to_left, own, to_right, keep, send = patch_work(
        start, left, own, right, fb, rf, rft, w_down.reshape(3, 3 * C1, C2), rdt, ru
    )
    from_left = from_before(COL, to_right)
    part = added(keep, swapped(send))
    part = scattered(part, "x")
    part, from_left, to_left = lax.optimization_barrier((part, from_left, to_left))
    from_right = from_after(COL, to_left)
    part = scattered(part, "y")
    canvas = small_call(
        add_left_kernel, "add_left", [((2, 48, TILE, C1), F32)], [], starts, from_left, own, smem=1
    )[0]
    part, canvas, from_right = lax.optimization_barrier((part, canvas, from_right))
    part = gathered(part, ("zl", "zh")).astype(F32).sum(0).astype(BF16)
    tile_shape = (2, TILE, TILE, C1)
    up, own, down = small_call(
        add_right_kernel,
        "add_right",
        [(tile_shape, BF16), (tile_shape, F32), (tile_shape, BF16)],
        [pltpu.VMEM((2, 48, TILE, C1), F32)],
        starts,
        canvas,
        from_right,
        smem=1,
    )
    part, up, own, down = lax.optimization_barrier((part, up, own, down))
    from_above, from_under = from_before(ROW, down), from_after(ROW, up)
    part = gathered(part, "y").reshape(-1, C1)
    part, own, from_above, from_under = lax.optimization_barrier((part, own, from_above, from_under))
    part = gathered(part, "x").reshape(-1, C1)
    blended, field_grad = small_call(
        finish_kernel,
        "finish",
        [(field.shape, BF16), (field.shape, F32)],
        [],
        own,
        from_above,
        from_under,
    )
    part, blended, field_grad = lax.optimization_barrier((part, blended, field_grad))
    other = swapped(part)
    scale = 1.0 / math.sqrt(TILE * rows_n * TILE * cols_n)
    g_first, g_down, g_up = small_call(
        functools.partial(unpack_kernel, scale),
        "unpack",
        [((9, C1, C1), F32), ((3, 3 * C1, C2), F32), ((4, C2, C1), F32)],
        [pltpu.VMEM((2, HALF_ROWS, C1), BF16)],
        core[None],
        part,
        other,
        smem=1,
    )
    return (
        blended,
        field_grad,
        g_first.reshape(w_first.shape),
        g_down.reshape(w_down.shape),
        g_up.reshape(w_up.shape),
    )


def solution(mesh):
    fine = Mesh(mesh.devices.reshape(8, 4, 2, 4, 2), ("y", "zl", "core", "x", "zh"))
    tiles = P(ROW, COL, None)
    return jax.shard_map(
        per_device,
        mesh=fine,
        in_specs=(tiles, tiles, P(), P(), P(), P(), P()),
        out_specs=(tiles, tiles, P(), P(), P()),
        check_vma=False,
    )
```

```python
import functools
import math

import jax
import jax.numpy as jnp
from jax import lax
from jax.experimental import pallas as pl
from jax.experimental.pallas import tpu as pltpu
from jax.sharding import Mesh, PartitionSpec as P

MARGIN = 8
ROW = ("x", "zh")
COL = ("y", "zl", "core")
F32 = jnp.float32
BF16 = jnp.bfloat16
REACH = 2
FAR = 1000
TILE = 16
C1 = 128
C2 = 256
FIRST_ROWS = 9 * C1
DOWN_ROWS = 18 * C1
UP_ROWS = 4 * C2
USED_ROWS = FIRST_ROWS + DOWN_ROWS + UP_ROWS
HALF_ROWS = 2304


def dot(a, b):
    return lax.dot_general(a, b, (((1,), (0,)), ((), ())), preferred_element_type=F32)


def dot_nt(a, b):
    return lax.dot_general(a, b, (((1,), (1,)), ((), ())), preferred_element_type=F32)


def prepare_kernel(where, offsets, table, w_first, w_down, w_up, fb, rf, rft, rdt, ru):
    row_at, col_at = where[0], where[1]
    rows_n, cols_n = offsets.shape[0], offsets.shape[1] // 2
    sub = lax.broadcasted_iota(jnp.int32, (32, 32), 0)
    lane = lax.broadcasted_iota(jnp.int32, (32, 32), 1)
    column = jnp.where(sub < 16, 2 * sub, 2 * (sub - 16) + 1)
    table_t = table[...].astype(F32).T.astype(BF16)
    own_r = offsets[row_at, 2 * col_at]
    own_c = offsets[row_at, 2 * col_at + 1]
    total = jnp.zeros((32, 32), F32)
    own = jnp.zeros((32, 32), F32)
    for row_step in range(-REACH, REACH + 1):
        for col_step in range(-REACH, REACH + 1):
            near_r, near_c = row_at + row_step, col_at + col_step
            inside = (near_r >= 0) & (near_r < rows_n) & (near_c >= 0) & (near_c < cols_n)
            at_r = jnp.clip(near_r, 0, rows_n - 1)
            at_c = jnp.clip(near_c, 0, cols_n - 1)
            down_by = row_step * TILE + offsets[at_r, 2 * at_c] - own_r
            right_by = col_step * TILE + offsets[at_r, 2 * at_c + 1] - own_c
            down_by = jnp.where(inside, down_by, FAR)
            pick_c = (column - right_by == lane).astype(F32).astype(BF16)
            pick_r = (lane - down_by == sub).astype(F32).astype(BF16)
            placed = dot(pick_c, table_t)
            if row_step == 0 and col_step == 0:
                own = placed
            total = total + dot(placed.astype(BF16), pick_r)
    share = own / total
    for r in range(32):
        fb[r % 2, r // 2, :, :C1] = jnp.broadcast_to(share[:16, r : r + 1], (16, C1))
        fb[r % 2, r // 2, :, C1:] = jnp.broadcast_to(share[16:, r : r + 1], (16, C1))
    none = jnp.zeros((C1, C1), BF16)
    for t in range(3):
        for v in range(4):
            for b in range(2):
                rows, cols = pl.ds(v * C1, C1), pl.ds(b * C1, C1)
                held = 0 <= v - b <= 2
                rf[t, rows, cols] = w_first[t, v - b] if held else none
                rft[t, cols, rows] = w_first[2 - t, 2 - v + b] if held else none
        rdt[t, :C1, :C2] = w_down[t, 1]
        rdt[t, :C1, C2:] = jnp.zeros((C1, C2), BF16)
        rdt[t, C1:, :C2] = w_down[t, 2]
        rdt[t, C1:, C2:] = w_down[t, 0]
    for a in range(2):
        for b in range(2):
            ru[a, :, pl.ds(b * C1, C1)] = w_up[a, b]


def assemble_kernel(places, from_a, both, from_b, to_a, own, to_b, grown):
    grown[:, pl.ds(places[3], 16)] = from_a[...]
    grown[:, 16:32] = both[...]
    grown[:, pl.ds(places[4], 16)] = from_b[...]
    for side, out in enumerate((to_a, own, to_b)):
        out[...] = grown[:, pl.ds(places[side], 32)]


def add_a_kernel(places, from_a, own, canvas):
    canvas[...] = jnp.zeros_like(canvas)
    canvas[:, pl.ds(places[1], 32)] = own[...]
    spot = (slice(None), pl.ds(places[0], 32))
    strip = from_a[HALF_ROWS:].reshape(2, 32, 16, C1)
    canvas[spot] = canvas[spot] + strip.astype(F32)


def add_b_kernel(places, given, from_b, to_a, mid, to_b, canvas):
    canvas[...] = given[...]
    spot = (slice(None), pl.ds(places[2], 32))
    canvas[spot] = canvas[spot] + from_b[...].astype(F32)
    to_a[...] = canvas[:, pl.ds(places[3], 16)].astype(BF16)
    mid[...] = canvas[:, 16:32]
    to_b[...] = canvas[:, pl.ds(places[4], 16)].astype(BF16)


def finish_kernel(own, from_a, from_b, blended, field_grad):
    total = own[...] + from_a[...].astype(F32) + from_b[...].astype(F32)
    blended[...] = total[0].astype(BF16)
    field_grad[...] = total[1]


def unpack_kernel(scale, core, own, other, g_first, g_down, g_up, halves):
    halves[core[0]] = own[...]
    halves[1 - core[0]] = other[...]

    def rows(base, count):
        half, at = base // HALF_ROWS, base % HALF_ROWS
        return halves[half, at : at + count].astype(F32) * scale

    for t in range(9):
        g_first[t] = rows(t * C1, C1)
    for t in range(3):
        base = FIRST_ROWS + 6 * t * C1
        g_down[t, :, :C1] = rows(base, 3 * C1)
        g_down[t, :, C1:] = rows(base + 3 * C1, 3 * C1)
    for t in range(4):
        g_up[t] = rows(FIRST_ROWS + DOWN_ROWS + t * C2, C2)


def shifted(x, by):
    j = lax.broadcasted_iota(jnp.int32, x.shape, 0) % 16
    moved = pltpu.roll(x, by % x.shape[0], 0)
    return jnp.where(j == (0 if by > 0 else 15), 0.0, moved)


def spread(x):
    return jnp.concatenate(
        [shifted(x[:, C1:], 1).astype(BF16), x.astype(BF16), shifted(x[:, :C1], -1).astype(BF16)], axis=1
    )


def window(ref, a, t):
    part = ref[(a + t) % 2, (a + t) // 2 : (a + t) // 2 + 16]
    return part.reshape(256, part.shape[-1])


def net_kernel(
    start, side_a, middle, side_b, fb, rf, rft, wd, rdt, ru,
    mid_o, strip_b, keep, send,
    fs, cs, xv, hv, gv, g4, gs, bs, can_b, can_g, halves,
):
    start_c, core = start[0], start[1]
    at_a, at_b = 32 * (1 - core), 32 * core

    def put(base, value):
        half, at = base // HALF_ROWS, base % HALF_ROWS
        halves[core if half == 0 else 1 - core, at : at + value.shape[0]] = value.astype(BF16)

    for ref in (xv, hv, gv):
        edge = jnp.zeros((16, ref.shape[-1]), BF16)
        ref[0, 0] = edge
        ref[1, 16] = edge
    g4[16] = jnp.zeros((16, 2 * C2), BF16)

    def stage(r, carry):
        for at, ref in ((at_a, side_a), (16, middle), (at_b, side_b)):
            spot = pl.ds(pl.multiple_of(at + 8, 8), 16)
            fs[r, spot, :] = ref[0, r].astype(F32)
            cs[r, spot, :] = ref[1, r].astype(F32)
        return carry

    lax.fori_loop(0, 32, stage, 0, unroll=4)
    j = lax.broadcasted_iota(jnp.int32, (16, C1), 0)

    def load(i, carry):
        for a in range(2):
            r = 2 * i + a
            at = start_c + 8
            before = jnp.where(j == 0, 0.0, fs[r, pl.ds(at - 1, 16, 2), :])
            even = fs[r, pl.ds(at, 16, 2), :]
            odd = fs[r, pl.ds(at + 1, 16, 2), :]
            after = jnp.where(j == 15, 0.0, fs[r, pl.ds(at + 2, 16, 2), :])
            xv[1 - a, i + a] = jnp.concatenate([before, even, odd, after], axis=1).astype(BF16)
            gs[a, i, :, :C1] = cs[r, pl.ds(at, 16, 2), :] * fb[a, i, :, :C1]
            gs[a, i, :, C1:] = cs[r, pl.ds(at + 1, 16, 2), :] * fb[a, i, :, C1:]
        return carry

    lax.fori_loop(0, 16, load, 0, unroll=2)

    h, slope_h = [], []
    for a in range(2):
        pre = dot(window(xv, a, 0), rf[0]) + dot(window(xv, a, 1), rf[1]) + dot(window(xv, a, 2), rf[2])
        sig = lax.logistic(pre)
        value = pre * sig
        slope_h.append(sig + value * (1.0 - sig))
        h.append(value.astype(BF16))
        hv[1 - a, a : a + 16] = jnp.concatenate(
            [shifted(value[:, C1:], 1).astype(BF16), h[a]], axis=1
        ).reshape(16, 16, 3 * C1)
    pre = dot(window(hv, 0, 0), wd[0]) + dot(window(hv, 0, 1), wd[1]) + dot(window(hv, 0, 2), wd[2])
    sig = lax.logistic(pre)
    value = pre * sig
    slope_d = sig + value * (1.0 - sig)
    d = value.astype(BF16)
    d_t = value.T.astype(BF16)
    g_d = jnp.zeros((256, C2), F32)
    for a in range(2):
        out = h[a].astype(F32) + dot(d, ru[a])
        bs[a] = (fb[a].reshape(256, 2 * C1) * out).reshape(16, 16, 2 * C1)
        g = gs[a].reshape(256, 2 * C1).astype(BF16)
        g_d = g_d + dot_nt(g, ru[a])
        g_up = dot(d_t, g)
        base = FIRST_ROWS + DOWN_ROWS + 2 * a * C2
        put(base, g_up[:, :C1])
        put(base + C2, g_up[:, C1:])
    g_pre = g_d.astype(BF16).astype(F32) * slope_d
    g4[0:16] = jnp.concatenate([g_pre.astype(BF16), shifted(g_pre, -1).astype(BF16)], axis=1).reshape(
        16, 16, 2 * C2
    )
    g_pre_t = g_pre.T.astype(BF16)
    for t in range(3):
        g_down = dot(g_pre_t, window(hv, 0, t)).T
        base = FIRST_ROWS + 6 * t * C1
        put(base, g_down[:, :C1])
        put(base + 3 * C1, g_down[:, C1:])
    here = g4[0:16].reshape(256, 2 * C2)
    below = g4[1:17].reshape(256, 2 * C2)
    g_h = [dot_nt(here, rdt[1]), dot_nt(here, rdt[2]) + dot_nt(below, rdt[0])]
    g_t = []
    for a in range(2):
        g_pre = (gs[a].reshape(256, 2 * C1) + g_h[a]) * slope_h[a]
        gv[1 - a, a : a + 16] = spread(g_pre).reshape(16, 16, 4 * C1)
        g_t.append(g_pre.T.astype(BF16))
    for t in range(3):
        g_first = dot(g_t[0], window(xv, 0, t)) + dot(g_t[1], window(xv, 1, t))
        for ct in range(3):
            block = (
                g_first[:C1, ct * C1 : (ct + 1) * C1] + g_first[C1:, (ct + 1) * C1 : (ct + 2) * C1]
            )
            put((3 * t + ct) * C1, block.T)
    put(USED_ROWS, jnp.zeros((2 * HALF_ROWS - USED_ROWS, C1), F32))
    keep[...] = halves[0]
    send[:HALF_ROWS] = halves[1]
    for a in range(2):
        g_x = (
            dot_nt(window(gv, a, 0), rft[0])
            + dot_nt(window(gv, a, 1), rft[1])
            + dot_nt(window(gv, a, 2), rft[2])
        )
        gs[a] = g_x.reshape(16, 16, 2 * C1)

    def clear(r, carry):
        can_b[r] = jnp.zeros((48, C1), F32)
        can_g[r] = jnp.zeros((48, C1), F32)
        return carry

    lax.fori_loop(0, 32, clear, 0, unroll=4)

    def place(i, carry):
        for a in range(2):
            r = 2 * i + a
            for b in range(2):
                can_b[r, pl.ds(start_c + b, 16, 2), :] = bs[a, i, :, b * C1 : (b + 1) * C1]
                can_g[r, pl.ds(start_c + b, 16, 2), :] = gs[a, i, :, b * C1 : (b + 1) * C1]
        return carry

    lax.fori_loop(0, 16, place, 0, unroll=2)

    def give(r, carry):
        for k, canvas in enumerate((can_b, can_g)):
            mid_o[k, r] = canvas[r, 16:32]
            strip = canvas[r, pl.ds(pl.multiple_of(at_a, 16), 16), :].astype(BF16)
            send[pl.ds(pl.multiple_of(HALF_ROWS + (32 * k + r) * 16, 16), 16)] = strip
            strip_b[k, r] = canvas[r, pl.ds(pl.multiple_of(at_b, 16), 16), :].astype(BF16)
        return carry

    lax.fori_loop(0, 32, give, 0, unroll=2)


VMEM = pl.BlockSpec(memory_space=pltpu.VMEM)
SMEM = pl.BlockSpec(memory_space=pltpu.SMEM)


def prepared(where, offsets, table, w_first, w_down, w_up):
    return pl.pallas_call(
        prepare_kernel,
        out_shape=(
            jax.ShapeDtypeStruct((2, 16, 16, 2 * C1), F32),
            jax.ShapeDtypeStruct((3, 4 * C1, 2 * C1), BF16),
            jax.ShapeDtypeStruct((3, 2 * C1, 4 * C1), BF16),
            jax.ShapeDtypeStruct((3, 2 * C1, 2 * C2), BF16),
            jax.ShapeDtypeStruct((2, C2, 2 * C1), BF16),
        ),
        in_specs=[SMEM, SMEM, VMEM, VMEM, VMEM, VMEM],
        out_specs=[VMEM] * 5,
        compiler_params=pltpu.CompilerParams(vmem_limit_bytes=10 * 2**20),
        cost_estimate=pl.CostEstimate(flops=5 * 10**6, bytes_accessed=10**7, transcendentals=0),
        name="prepare",
    )(where, offsets, table, w_first, w_down, w_up)


def patch_work(start, side_a, middle, side_b, fb, rf, rft, wd, rdt, ru):
    return pl.pallas_call(
        net_kernel,
        out_shape=(
            jax.ShapeDtypeStruct((2, 32, 16, C1), F32),
            jax.ShapeDtypeStruct((2, 32, 16, C1), BF16),
            jax.ShapeDtypeStruct((HALF_ROWS, C1), BF16),
            jax.ShapeDtypeStruct((HALF_ROWS + 2 * 32 * 16, C1), BF16),
        ),
        in_specs=[SMEM] + [VMEM] * 9,
        out_specs=[VMEM] * 4,
        scratch_shapes=[
            pltpu.VMEM((32, 64, C1), F32),
            pltpu.VMEM((32, 64, C1), F32),
            pltpu.VMEM((2, 17, 16, 4 * C1), BF16),
            pltpu.VMEM((2, 17, 16, 3 * C1), BF16),
            pltpu.VMEM((2, 17, 16, 4 * C1), BF16),
            pltpu.VMEM((17, 16, 2 * C2), BF16),
            pltpu.VMEM((2, 16, 16, 2 * C1), F32),
            pltpu.VMEM((2, 16, 16, 2 * C1), F32),
            pltpu.VMEM((32, 48, C1), F32),
            pltpu.VMEM((32, 48, C1), F32),
            pltpu.VMEM((2, HALF_ROWS, C1), BF16),
        ],
        compiler_params=pltpu.CompilerParams(vmem_limit_bytes=24 * 2**20),
        cost_estimate=pl.CostEstimate(flops=2 * 10**9, bytes_accessed=10**7, transcendentals=200000),
        name="patch_work",
    )(start, side_a, middle, side_b, fb, rf, rft, wd, rdt, ru)


def small_call(body, name, outs, scratch, *args, smem=0):
    return pl.pallas_call(
        body,
        out_shape=tuple(jax.ShapeDtypeStruct(shape, kind) for shape, kind in outs),
        in_specs=[SMEM] * smem + [VMEM] * (len(args) - smem),
        out_specs=[VMEM] * len(outs),
        scratch_shapes=scratch,
        compiler_params=pltpu.CompilerParams(vmem_limit_bytes=10 * 2**20),
        cost_estimate=pl.CostEstimate(flops=10**6, bytes_accessed=2 * 10**6, transcendentals=0),
        name=name,
    )(*args)


def swapped_b(x, axes):
    size = lax.axis_size(axes)
    pairs = [(i, i + 1) for i in range(1, size - 1, 2)]
    return lax.ppermute(x, axes, pairs + [(j, i) for i, j in pairs])


def swapped_a(x, axis):
    return lax.ppermute(x, axis, [(0, 1), (1, 0)])


def added(x, y):
    return (x.astype(F32) + y.astype(F32)).astype(BF16)


def scattered(x, axes):
    size = lax.axis_size(axes)
    parts = x.reshape(size, x.shape[0] // size, x.shape[1])
    got = lax.all_to_all(parts, axes, 0, 0, tiled=True)
    return got.astype(F32).sum(0).astype(BF16)


def gathered(x, axes):
    size = lax.axis_size(axes)
    parts = jnp.broadcast_to(x[None], (size,) + x.shape)
    return lax.all_to_all(parts, axes, 0, 0, tiled=True)


def per_device(field, cotangent, w_first, w_down, w_up, offsets, blend_table):
    rows_n = lax.axis_size(ROW)
    cols_n = lax.axis_size(COL)
    row_at = lax.axis_index(ROW)
    col_at = lax.axis_index(COL)
    where = jnp.stack([row_at, col_at]).astype(jnp.int32)
    both = jnp.stack([field, cotangent])
    core = lax.axis_index("core").astype(jnp.int32)
    zh = lax.axis_index("zh").astype(jnp.int32)
    col_a = col_at + 1 - 2 * core
    col_b = jnp.clip(col_at - 1 + 2 * core, 0, cols_n - 1)
    firsts = [MARGIN + offsets[row_at, col, 0] for col in (col_a, col_at, col_b)]
    places = jnp.stack(firsts + [32 * (1 - zh), 32 * zh]).astype(jnp.int32)
    start = jnp.stack([MARGIN + offsets[row_at, col_at, 1], core])
    fb, rf, rft, rdt, ru = prepared(
        where, offsets.reshape(rows_n, 2 * cols_n), blend_table, w_first, w_down, w_up
    )
    row_a, row_b = swapped_a(both, "zh"), swapped_b(both, ROW)
    row_a, row_b, fb, rf, rft, rdt, ru = lax.optimization_barrier((row_a, row_b, fb, rf, rft, rdt, ru))
    window_shape = (2, 32, TILE, C1)
    to_a, own, to_b = small_call(
        assemble_kernel,
        "assemble",
        [(window_shape, BF16)] * 3,
        [pltpu.VMEM((2, 48, TILE, C1), BF16)],
        places,
        row_a,
        both,
        row_b,
        smem=1,
    )
    side_b, side_a = swapped_b(to_b, COL), swapped_a(to_a, "core")
    own, strip_b, keep, send = patch_work(
        start, side_a, own, side_b, fb, rf, rft, w_down.reshape(3, 3 * C1, C2), rdt, ru
    )
    got = swapped_a(send, "core")
    from_b = swapped_b(strip_b, COL)
    part = added(keep, got[:HALF_ROWS])
    part = scattered(part, "x")
    part, from_b = lax.optimization_barrier((part, from_b))
    part = scattered(part, "y")
    canvas = small_call(
        add_a_kernel, "add_a", [((2, 48, TILE, C1), F32)], [], places, got, own, smem=1
    )[0]
    part, canvas = lax.optimization_barrier((part, canvas))
    part = gathered(part, ("zl", "zh")).astype(F32).sum(0).astype(BF16)
    tile_shape = (2, TILE, TILE, C1)
    to_a, own, to_b = small_call(
        add_b_kernel,
        "add_b",
        [(tile_shape, BF16), (tile_shape, F32), (tile_shape, BF16)],
        [pltpu.VMEM((2, 48, TILE, C1), F32)],
        places,
        canvas,
        from_b,
        smem=1,
    )
    part, to_a, own, to_b = lax.optimization_barrier((part, to_a, own, to_b))
    row_a, row_b = swapped_a(to_a, "zh"), swapped_b(to_b, ROW)
    part = gathered(part, "y").reshape(-1, C1)
    part, own, row_a, row_b = lax.optimization_barrier((part, own, row_a, row_b))
    part = gathered(part, "x").reshape(-1, C1)
    blended, field_grad = small_call(
        finish_kernel,
        "finish",
        [(field.shape, BF16), (field.shape, F32)],
        [],
        own,
        row_a,
        row_b,
    )
    part, blended, field_grad = lax.optimization_barrier((part, blended, field_grad))
    other = swapped_a(part, "core")
    scale = 1.0 / math.sqrt(TILE * rows_n * TILE * cols_n)
    g_first, g_down, g_up = small_call(
        functools.partial(unpack_kernel, scale),
        "unpack",
        [((9, C1, C1), F32), ((3, 3 * C1, C2), F32), ((4, C2, C1), F32)],
        [pltpu.VMEM((2, HALF_ROWS, C1), BF16)],
        core[None],
        part,
        other,
        smem=1,
    )
    return (
        blended,
        field_grad,
        g_first.reshape(w_first.shape),
        g_down.reshape(w_down.shape),
        g_up.reshape(w_up.shape),
    )


def solution(mesh):
    fine = Mesh(mesh.devices.reshape(8, 4, 2, 4, 2), ("y", "zl", "core", "x", "zh"))
    tiles = P(ROW, COL, None)
    return jax.shard_map(
        per_device,
        mesh=fine,
        in_specs=(tiles, tiles, P(), P(), P(), P(), P()),
        out_specs=(tiles, tiles, P(), P(), P()),
        check_vma=False,
    )
```

```python
import functools
import math

import jax
import jax.numpy as jnp
from jax import lax
from jax.experimental import pallas as pl
from jax.experimental.pallas import tpu as pltpu
from jax.sharding import Mesh, PartitionSpec as P

MARGIN = 8
ROW = ("x", "zh")
COL = ("y", "zl", "core")
F32 = jnp.float32
BF16 = jnp.bfloat16
REACH = 2
FAR = 1000
TILE = 16
C1 = 128
C2 = 256
FIRST_ROWS = 9 * C1
DOWN_ROWS = 18 * C1
UP_ROWS = 4 * C2
USED_ROWS = FIRST_ROWS + DOWN_ROWS + UP_ROWS
HALF_ROWS = 2304


def dot(a, b):
    return lax.dot_general(a, b, (((1,), (0,)), ((), ())), preferred_element_type=F32)


def dot_nt(a, b):
    return lax.dot_general(a, b, (((1,), (1,)), ((), ())), preferred_element_type=F32)


def prepare_kernel(
    where, offsets, table, w_first, w_down, w_up,
    places, fb, rf, rft, rdt, ru,
):
    row_at, col_at = where[0], where[1]
    rows_n, cols_n = offsets.shape[0], offsets.shape[2]
    core, zh = lax.rem(col_at, 2), lax.rem(row_at, 2)
    col_b = jnp.clip(col_at - 1 + 2 * core, 0, cols_n - 1)
    for k, col in enumerate((col_at + 1 - 2 * core, col_at, col_b)):
        places[k] = MARGIN + offsets[row_at, 0, col]
    places[3] = 32 * (1 - zh)
    places[4] = 32 * zh
    places[5] = MARGIN + offsets[row_at, 1, col_at]
    places[6] = core
    places[7] = 0
    sub = lax.broadcasted_iota(jnp.int32, (32, 32), 0)
    lane = lax.broadcasted_iota(jnp.int32, (32, 32), 1)
    column = jnp.where(sub < 16, 2 * sub, 2 * (sub - 16) + 1)
    table_t = table[...].astype(F32).T.astype(BF16)
    own_r = offsets[row_at, 0, col_at]
    own_c = offsets[row_at, 1, col_at]
    total = jnp.zeros((32, 32), F32)
    own = jnp.zeros((32, 32), F32)
    for row_step in range(-REACH, REACH + 1):
        for col_step in range(-REACH, REACH + 1):
            near_r, near_c = row_at + row_step, col_at + col_step
            inside = (near_r >= 0) & (near_r < rows_n) & (near_c >= 0) & (near_c < cols_n)
            at_r = jnp.clip(near_r, 0, rows_n - 1)
            at_c = jnp.clip(near_c, 0, cols_n - 1)
            down_by = row_step * TILE + offsets[at_r, 0, at_c] - own_r
            right_by = col_step * TILE + offsets[at_r, 1, at_c] - own_c
            down_by = jnp.where(inside, down_by, FAR)
            pick_c = (column - right_by == lane).astype(F32).astype(BF16)
            pick_r = (lane - down_by == sub).astype(F32).astype(BF16)
            placed = dot(pick_c, table_t)
            if row_step == 0 and col_step == 0:
                own = placed
            total = total + dot(placed.astype(BF16), pick_r)
    share = own / total
    for r in range(32):
        fb[r % 2, r // 2, :, :C1] = jnp.broadcast_to(share[:16, r : r + 1], (16, C1))
        fb[r % 2, r // 2, :, C1:] = jnp.broadcast_to(share[16:, r : r + 1], (16, C1))
    none = jnp.zeros((C1, C1), BF16)
    for t in range(3):
        for v in range(4):
            for b in range(2):
                rows, cols = pl.ds(v * C1, C1), pl.ds(b * C1, C1)
                held = 0 <= v - b <= 2
                rf[t, rows, cols] = w_first[t, v - b] if held else none
                rft[t, cols, rows] = w_first[2 - t, 2 - v + b] if held else none
        rdt[t, :C1, :C2] = w_down[t, 1]
        rdt[t, :C1, C2:] = jnp.zeros((C1, C2), BF16)
        rdt[t, C1:, :C2] = w_down[t, 2]
        rdt[t, C1:, C2:] = w_down[t, 0]
    for a in range(2):
        for b in range(2):
            ru[a, :, pl.ds(b * C1, C1)] = w_up[a, b]


def assemble_kernel(places, from_a, both, from_b, to_a, own, to_b, grown):
    grown[:, pl.ds(places[3], 16)] = from_a[...]
    grown[:, 16:32] = both[...]
    grown[:, pl.ds(places[4], 16)] = from_b[...]
    for side, out in enumerate((to_a, own, to_b)):
        out[...] = grown[:, pl.ds(places[side], 32)]


def add_kernel(places, from_a, own, from_b, to_a, mid, to_b, canvas):
    canvas[...] = jnp.zeros_like(canvas)
    canvas[:, pl.ds(places[1], 32)] = own[...]
    for side, strip in ((0, from_a[HALF_ROWS:].reshape(2, 32, 16, C1)), (2, from_b[...])):
        spot = (slice(None), pl.ds(places[side], 32))
        canvas[spot] = canvas[spot] + strip.astype(F32)
    to_a[...] = canvas[:, pl.ds(places[3], 16)].astype(BF16)
    mid[...] = canvas[:, 16:32]
    to_b[...] = canvas[:, pl.ds(places[4], 16)].astype(BF16)


def finish_kernel(which, own, from_a, from_b, out):
    total = own[which] + from_a[which].astype(F32) + from_b[which].astype(F32)
    out[...] = total.astype(out.dtype)


def unpack_kernel(scale, places, own, other, g_first, g_down, g_up, halves):
    halves[places[6]] = own[...]
    halves[1 - places[6]] = other[...]

    def rows(base, count):
        half, at = base // HALF_ROWS, base % HALF_ROWS
        return halves[half, at : at + count].astype(F32) * scale

    for t in range(9):
        g_first[t] = rows(t * C1, C1)
    for t in range(3):
        base = FIRST_ROWS + 6 * t * C1
        g_down[t, :, :C1] = rows(base, 3 * C1)
        g_down[t, :, C1:] = rows(base + 3 * C1, 3 * C1)
    for t in range(4):
        g_up[t] = rows(FIRST_ROWS + DOWN_ROWS + t * C2, C2)


def shifted(x, by):
    j = lax.broadcasted_iota(jnp.int32, x.shape, 0) % 16
    moved = pltpu.roll(x, by % x.shape[0], 0)
    return jnp.where(j == (0 if by > 0 else 15), 0.0, moved)


def spread(x):
    return jnp.concatenate(
        [shifted(x[:, C1:], 1).astype(BF16), x.astype(BF16), shifted(x[:, :C1], -1).astype(BF16)], axis=1
    )


def window(ref, a, t):
    part = ref[(a + t) % 2, (a + t) // 2 : (a + t) // 2 + 16]
    return part.reshape(256, part.shape[-1])


def net_kernel(
    places, side_a, middle, side_b, fb, rf, rft, wd, rdt, ru,
    mid_o, strip_b, keep, send,
    fs, cs, xv, hv, gv, g4, gs, bs, can_b, can_g, halves,
):
    start_c, core = places[5], places[6]
    at_a, at_b = 32 * (1 - core), 32 * core

    def put(base, value):
        half, at = base // HALF_ROWS, base % HALF_ROWS
        halves[core if half == 0 else 1 - core, at : at + value.shape[0]] = value.astype(BF16)

    for ref in (xv, hv, gv):
        edge = jnp.zeros((16, ref.shape[-1]), BF16)
        ref[0, 0] = edge
        ref[1, 16] = edge
    g4[16] = jnp.zeros((16, 2 * C2), BF16)

    def stage(r, carry):
        for at, ref in ((at_a, side_a), (16, middle), (at_b, side_b)):
            spot = pl.ds(pl.multiple_of(at + 8, 8), 16)
            fs[r, spot, :] = ref[0, r].astype(F32)
            cs[r, spot, :] = ref[1, r].astype(F32)
        return carry

    lax.fori_loop(0, 32, stage, 0, unroll=4)
    j = lax.broadcasted_iota(jnp.int32, (16, C1), 0)

    def load(i, carry):
        for a in range(2):
            r = 2 * i + a
            at = start_c + 8
            before = jnp.where(j == 0, 0.0, fs[r, pl.ds(at - 1, 16, 2), :])
            even = fs[r, pl.ds(at, 16, 2), :]
            odd = fs[r, pl.ds(at + 1, 16, 2), :]
            after = jnp.where(j == 15, 0.0, fs[r, pl.ds(at + 2, 16, 2), :])
            xv[1 - a, i + a] = jnp.concatenate([before, even, odd, after], axis=1).astype(BF16)
            gs[a, i, :, :C1] = cs[r, pl.ds(at, 16, 2), :] * fb[a, i, :, :C1]
            gs[a, i, :, C1:] = cs[r, pl.ds(at + 1, 16, 2), :] * fb[a, i, :, C1:]
        return carry

    lax.fori_loop(0, 16, load, 0, unroll=2)

    h, slope_h = [], []
    for a in range(2):
        pre = dot(window(xv, a, 0), rf[0]) + dot(window(xv, a, 1), rf[1]) + dot(window(xv, a, 2), rf[2])
        sig = lax.logistic(pre)
        value = pre * sig
        slope_h.append(sig + value * (1.0 - sig))
        h.append(value.astype(BF16))
        hv[1 - a, a : a + 16] = jnp.concatenate(
            [shifted(value[:, C1:], 1).astype(BF16), h[a]], axis=1
        ).reshape(16, 16, 3 * C1)
    pre = dot(window(hv, 0, 0), wd[0]) + dot(window(hv, 0, 1), wd[1]) + dot(window(hv, 0, 2), wd[2])
    sig = lax.logistic(pre)
    value = pre * sig
    slope_d = sig + value * (1.0 - sig)
    d = value.astype(BF16)
    d_t = value.T.astype(BF16)
    g_d = jnp.zeros((256, C2), F32)
    for a in range(2):
        out = h[a].astype(F32) + dot(d, ru[a])
        bs[a] = (fb[a].reshape(256, 2 * C1) * out).reshape(16, 16, 2 * C1)
        g = gs[a].reshape(256, 2 * C1).astype(BF16)
        g_d = g_d + dot_nt(g, ru[a])
        g_up = dot(d_t, g)
        base = FIRST_ROWS + DOWN_ROWS + 2 * a * C2
        put(base, g_up[:, :C1])
        put(base + C2, g_up[:, C1:])
    g_pre = g_d.astype(BF16).astype(F32) * slope_d
    g4[0:16] = jnp.concatenate([g_pre.astype(BF16), shifted(g_pre, -1).astype(BF16)], axis=1).reshape(
        16, 16, 2 * C2
    )
    g_pre_t = g_pre.T.astype(BF16)
    for t in range(3):
        g_down = dot(g_pre_t, window(hv, 0, t)).T
        base = FIRST_ROWS + 6 * t * C1
        put(base, g_down[:, :C1])
        put(base + 3 * C1, g_down[:, C1:])
    here = g4[0:16].reshape(256, 2 * C2)
    below = g4[1:17].reshape(256, 2 * C2)
    g_h = [dot_nt(here, rdt[1]), dot_nt(here, rdt[2]) + dot_nt(below, rdt[0])]
    g_t = []
    for a in range(2):
        g_pre = (gs[a].reshape(256, 2 * C1) + g_h[a]) * slope_h[a]
        gv[1 - a, a : a + 16] = spread(g_pre).reshape(16, 16, 4 * C1)
        g_t.append(g_pre.T.astype(BF16))
    for t in range(3):
        g_first = dot(g_t[0], window(xv, 0, t)) + dot(g_t[1], window(xv, 1, t))
        for ct in range(3):
            block = (
                g_first[:C1, ct * C1 : (ct + 1) * C1] + g_first[C1:, (ct + 1) * C1 : (ct + 2) * C1]
            )
            put((3 * t + ct) * C1, block.T)
    put(USED_ROWS, jnp.zeros((2 * HALF_ROWS - USED_ROWS, C1), F32))
    keep[...] = halves[0]
    send[:HALF_ROWS] = halves[1]
    for a in range(2):
        g_x = (
            dot_nt(window(gv, a, 0), rft[0])
            + dot_nt(window(gv, a, 1), rft[1])
            + dot_nt(window(gv, a, 2), rft[2])
        )
        gs[a] = g_x.reshape(16, 16, 2 * C1)

    def clear(r, carry):
        can_b[r] = jnp.zeros((48, C1), F32)
        can_g[r] = jnp.zeros((48, C1), F32)
        return carry

    lax.fori_loop(0, 32, clear, 0, unroll=4)

    def place(i, carry):
        for a in range(2):
            r = 2 * i + a
            for b in range(2):
                can_b[r, pl.ds(start_c + b, 16, 2), :] = bs[a, i, :, b * C1 : (b + 1) * C1]
                can_g[r, pl.ds(start_c + b, 16, 2), :] = gs[a, i, :, b * C1 : (b + 1) * C1]
        return carry

    lax.fori_loop(0, 16, place, 0, unroll=2)

    def give(r, carry):
        for k, canvas in enumerate((can_b, can_g)):
            mid_o[k, r] = canvas[r, 16:32]
            strip = canvas[r, pl.ds(pl.multiple_of(at_a, 16), 16), :].astype(BF16)
            send[pl.ds(pl.multiple_of(HALF_ROWS + (32 * k + r) * 16, 16), 16)] = strip
            strip_b[k, r] = canvas[r, pl.ds(pl.multiple_of(at_b, 16), 16), :].astype(BF16)
        return carry

    lax.fori_loop(0, 32, give, 0, unroll=2)


VMEM = pl.BlockSpec(memory_space=pltpu.VMEM)
SMEM = pl.BlockSpec(memory_space=pltpu.SMEM)


def prepared(where, offsets, table, w_first, w_down, w_up):
    return pl.pallas_call(
        prepare_kernel,
        out_shape=(
            jax.ShapeDtypeStruct((8,), jnp.int32),
            jax.ShapeDtypeStruct((2, 16, 16, 2 * C1), F32),
            jax.ShapeDtypeStruct((3, 4 * C1, 2 * C1), BF16),
            jax.ShapeDtypeStruct((3, 2 * C1, 4 * C1), BF16),
            jax.ShapeDtypeStruct((3, 2 * C1, 2 * C2), BF16),
            jax.ShapeDtypeStruct((2, C2, 2 * C1), BF16),
        ),
        in_specs=[SMEM, SMEM, VMEM, VMEM, VMEM, VMEM],
        out_specs=[SMEM] + [VMEM] * 5,
        compiler_params=pltpu.CompilerParams(vmem_limit_bytes=10 * 2**20),
        cost_estimate=pl.CostEstimate(flops=5 * 10**6, bytes_accessed=10**7, transcendentals=0),
        name="prepare",
    )(where, offsets, table, w_first, w_down, w_up)


def patch_work(places, side_a, middle, side_b, fb, rf, rft, wd, rdt, ru):
    return pl.pallas_call(
        net_kernel,
        out_shape=(
            jax.ShapeDtypeStruct((2, 32, 16, C1), F32),
            jax.ShapeDtypeStruct((2, 32, 16, C1), BF16),
            jax.ShapeDtypeStruct((HALF_ROWS, C1), BF16),
            jax.ShapeDtypeStruct((HALF_ROWS + 2 * 32 * 16, C1), BF16),
        ),
        in_specs=[SMEM] + [VMEM] * 9,
        out_specs=[VMEM] * 4,
        scratch_shapes=[
            pltpu.VMEM((32, 64, C1), F32),
            pltpu.VMEM((32, 64, C1), F32),
            pltpu.VMEM((2, 17, 16, 4 * C1), BF16),
            pltpu.VMEM((2, 17, 16, 3 * C1), BF16),
            pltpu.VMEM((2, 17, 16, 4 * C1), BF16),
            pltpu.VMEM((17, 16, 2 * C2), BF16),
            pltpu.VMEM((2, 16, 16, 2 * C1), F32),
            pltpu.VMEM((2, 16, 16, 2 * C1), F32),
            pltpu.VMEM((32, 48, C1), F32),
            pltpu.VMEM((32, 48, C1), F32),
            pltpu.VMEM((2, HALF_ROWS, C1), BF16),
        ],
        compiler_params=pltpu.CompilerParams(vmem_limit_bytes=24 * 2**20),
        cost_estimate=pl.CostEstimate(flops=2 * 10**9, bytes_accessed=10**7, transcendentals=200000),
        name="patch_work",
    )(places, side_a, middle, side_b, fb, rf, rft, wd, rdt, ru)


def small_call(body, name, outs, scratch, *args, smem=0):
    return pl.pallas_call(
        body,
        out_shape=tuple(jax.ShapeDtypeStruct(shape, kind) for shape, kind in outs),
        in_specs=[SMEM] * smem + [VMEM] * (len(args) - smem),
        out_specs=[VMEM] * len(outs),
        scratch_shapes=scratch,
        compiler_params=pltpu.CompilerParams(vmem_limit_bytes=10 * 2**20),
        cost_estimate=pl.CostEstimate(flops=10**6, bytes_accessed=2 * 10**6, transcendentals=0),
        name=name,
    )(*args)


def swapped_b(x, axes):
    size = lax.axis_size(axes)
    pairs = [(i, i + 1) for i in range(1, size - 1, 2)]
    return lax.ppermute(x, axes, pairs + [(j, i) for i, j in pairs])


def swapped_a(x, axis):
    return lax.ppermute(x, axis, [(0, 1), (1, 0)])


def added(x, y):
    return (x.astype(F32) + y.astype(F32)).astype(BF16)


def scattered(x, axes):
    size = lax.axis_size(axes)
    parts = x.reshape(size, x.shape[0] // size, x.shape[1])
    got = lax.all_to_all(parts, axes, 0, 0, tiled=True)
    return got.astype(F32).sum(0).astype(BF16)


def gathered(x, axes):
    size = lax.axis_size(axes)
    parts = jnp.broadcast_to(x[None], (size,) + x.shape)
    return lax.all_to_all(parts, axes, 0, 0, tiled=True)


def per_device(field, cotangent, w_first, w_down, w_up, offsets, blend_table):
    rows_n = lax.axis_size(ROW)
    cols_n = lax.axis_size(COL)
    row_at = lax.axis_index(ROW)
    col_at = lax.axis_index(COL)
    where = jnp.stack([row_at, col_at]).astype(jnp.int32)
    both = jnp.stack([field, cotangent])
    places, fb, rf, rft, rdt, ru = prepared(
        where, offsets.transpose(0, 2, 1), blend_table, w_first, w_down, w_up
    )
    row_a, row_b = swapped_a(both, "zh"), swapped_b(both, ROW)
    row_a, row_b, places, fb, rf, rft, rdt, ru = lax.optimization_barrier(
        (row_a, row_b, places, fb, rf, rft, rdt, ru)
    )
    window_shape = (2, 32, TILE, C1)
    to_a, own, to_b = small_call(
        assemble_kernel,
        "assemble",
        [(window_shape, BF16)] * 3,
        [pltpu.VMEM((2, 48, TILE, C1), BF16)],
        places,
        row_a,
        both,
        row_b,
        smem=1,
    )
    side_a, side_b = swapped_a(to_a, "core"), swapped_b(to_b, COL)
    own, strip_b, keep, send = patch_work(
        places, side_a, own, side_b, fb, rf, rft, w_down.reshape(3, 3 * C1, C2), rdt, ru
    )
    got = swapped_a(send, "core")
    from_b = swapped_b(strip_b, COL)
    part = added(keep, got[:HALF_ROWS])
    part = scattered(part, "x")
    part, from_b = lax.optimization_barrier((part, from_b))
    part = scattered(part, "y")
    tile_shape = (2, TILE, TILE, C1)
    to_a, own, to_b = small_call(
        add_kernel,
        "add",
        [(tile_shape, BF16), (tile_shape, F32), (tile_shape, BF16)],
        [pltpu.VMEM((2, 48, TILE, C1), F32)],
        places,
        got,
        own,
        from_b,
        smem=1,
    )
    row_a = swapped_a(to_a, "zh")
    part, own, row_a, to_b = lax.optimization_barrier((part, own, row_a, to_b))
    row_b = swapped_b(to_b, ROW)
    part = gathered(part, ("zl", "zh")).astype(F32).sum(0).astype(BF16)
    part, row_b = lax.optimization_barrier((part, row_b))
    part = gathered(part, "y").reshape(-1, C1)
    blended = small_call(
        functools.partial(finish_kernel, 0), "blend", [(field.shape, BF16)], [], own, row_a, row_b
    )[0]
    part, blended, own, row_a, row_b = lax.optimization_barrier((part, blended, own, row_a, row_b))
    part = gathered(part, "x").reshape(-1, C1)
    field_grad = small_call(
        functools.partial(finish_kernel, 1), "grad", [(field.shape, F32)], [], own, row_a, row_b
    )[0]
    part, field_grad = lax.optimization_barrier((part, field_grad))
    other = swapped_a(part, "core")
    scale = 1.0 / math.sqrt(TILE * rows_n * TILE * cols_n)
    g_first, g_down, g_up = small_call(
        functools.partial(unpack_kernel, scale),
        "unpack",
        [((9, C1, C1), F32), ((3, 3 * C1, C2), F32), ((4, C2, C1), F32)],
        [pltpu.VMEM((2, HALF_ROWS, C1), BF16)],
        places,
        part,
        other,
        smem=1,
    )
    return (
        blended,
        field_grad,
        g_first.reshape(w_first.shape),
        g_down.reshape(w_down.shape),
        g_up.reshape(w_up.shape),
    )


def solution(mesh):
    fine = Mesh(mesh.devices.reshape(8, 4, 2, 4, 2), ("y", "zl", "core", "x", "zh"))
    tiles = P(ROW, COL, None)
    return jax.shard_map(
        per_device,
        mesh=fine,
        in_specs=(tiles, tiles, P(), P(), P(), P(), P()),
        out_specs=(tiles, tiles, P(), P(), P()),
        check_vma=False,
    )
```

```python
import functools
import math

import jax
import jax.numpy as jnp
from jax import lax
from jax.experimental import pallas as pl
from jax.experimental.pallas import tpu as pltpu
from jax.sharding import Mesh, PartitionSpec as P

MARGIN = 8
ROW = ("x", "zh")
COL = ("y", "zl", "core")
F32 = jnp.float32
BF16 = jnp.bfloat16
REACH = 2
FAR = 1000
TILE = 16
C1 = 128
C2 = 256
FIRST_ROWS = 9 * C1
DOWN_ROWS = 18 * C1
UP_ROWS = 4 * C2
USED_ROWS = FIRST_ROWS + DOWN_ROWS + UP_ROWS
HALF_ROWS = 2304


def dot(a, b):
    return lax.dot_general(a, b, (((1,), (0,)), ((), ())), preferred_element_type=F32)


def dot_nt(a, b):
    return lax.dot_general(a, b, (((1,), (1,)), ((), ())), preferred_element_type=F32)


def prepare_kernel(
    where, offsets, table, w_first, w_down, w_up,
    places, fb, rf, rft, rdt, ru,
):
    row_at, col_at = where[0], where[1]
    rows_n, cols_n = offsets.shape[0], offsets.shape[2]
    core, zh = lax.rem(col_at, 2), lax.rem(row_at, 2)
    col_b = jnp.clip(col_at - 1 + 2 * core, 0, cols_n - 1)
    for k, col in enumerate((col_at + 1 - 2 * core, col_at, col_b)):
        places[k] = MARGIN + offsets[row_at, 0, col]
    places[3] = 32 * (1 - zh)
    places[4] = 32 * zh
    places[5] = MARGIN + offsets[row_at, 1, col_at]
    places[6] = core
    places[7] = 0
    sub = lax.broadcasted_iota(jnp.int32, (32, 32), 0)
    lane = lax.broadcasted_iota(jnp.int32, (32, 32), 1)
    column = jnp.where(sub < 16, 2 * sub, 2 * (sub - 16) + 1)
    table_t = table[...].astype(F32).T.astype(BF16)
    own_r = offsets[row_at, 0, col_at]
    own_c = offsets[row_at, 1, col_at]
    total = jnp.zeros((32, 32), F32)
    own = jnp.zeros((32, 32), F32)
    for row_step in range(-REACH, REACH + 1):
        for col_step in range(-REACH, REACH + 1):
            near_r, near_c = row_at + row_step, col_at + col_step
            inside = (near_r >= 0) & (near_r < rows_n) & (near_c >= 0) & (near_c < cols_n)
            at_r = jnp.clip(near_r, 0, rows_n - 1)
            at_c = jnp.clip(near_c, 0, cols_n - 1)
            down_by = row_step * TILE + offsets[at_r, 0, at_c] - own_r
            right_by = col_step * TILE + offsets[at_r, 1, at_c] - own_c
            down_by = jnp.where(inside, down_by, FAR)
            pick_c = (column - right_by == lane).astype(F32).astype(BF16)
            pick_r = (lane - down_by == sub).astype(F32).astype(BF16)
            placed = dot(pick_c, table_t)
            if row_step == 0 and col_step == 0:
                own = placed
            total = total + dot(placed.astype(BF16), pick_r)
    share = own / total
    for r in range(32):
        fb[r % 2, r // 2, :, :C1] = jnp.broadcast_to(share[:16, r : r + 1], (16, C1))
        fb[r % 2, r // 2, :, C1:] = jnp.broadcast_to(share[16:, r : r + 1], (16, C1))
    none = jnp.zeros((C1, C1), BF16)
    for t in range(3):
        for v in range(4):
            for b in range(2):
                rows, cols = pl.ds(v * C1, C1), pl.ds(b * C1, C1)
                held = 0 <= v - b <= 2
                rf[t, rows, cols] = w_first[t, v - b] if held else none
                rft[t, cols, rows] = w_first[2 - t, 2 - v + b] if held else none
        rdt[t, :C1, :C2] = w_down[t, 1]
        rdt[t, :C1, C2:] = jnp.zeros((C1, C2), BF16)
        rdt[t, C1:, :C2] = w_down[t, 2]
        rdt[t, C1:, C2:] = w_down[t, 0]
    for a in range(2):
        for b in range(2):
            ru[a, :, pl.ds(b * C1, C1)] = w_up[a, b]


def assemble_kernel(places, from_a, both, from_b, to_a, own, to_b, grown):
    grown[:, pl.ds(places[3], 16)] = from_a[...]
    grown[:, 16:32] = both[...]
    grown[:, pl.ds(places[4], 16)] = from_b[...]
    for side, out in enumerate((to_a, own, to_b)):
        out[...] = grown[:, pl.ds(places[side], 32)]


def add_kernel(places, from_a, own, from_b, to_a, mid, to_b, canvas):
    canvas[...] = jnp.zeros_like(canvas)
    canvas[:, pl.ds(places[1], 32)] = own[...]
    for side, strip in ((0, from_a[HALF_ROWS:].reshape(2, 32, 16, C1)), (2, from_b[...])):
        spot = (slice(None), pl.ds(places[side], 32))
        canvas[spot] = canvas[spot] + strip.astype(F32)
    to_a[...] = canvas[:, pl.ds(places[3], 16)].astype(BF16)
    mid[...] = canvas[:, 16:32]
    to_b[...] = canvas[:, pl.ds(places[4], 16)].astype(BF16)


def finish_kernel(own, from_a, from_b, blended, field_grad):
    total = own[...] + from_a[...].astype(F32) + from_b[...].astype(F32)
    blended[...] = total[0].astype(BF16)
    field_grad[...] = total[1]


def unpack_kernel(scale, places, own, other, g_first, g_down, g_up, halves):
    halves[places[6]] = own[...]
    halves[1 - places[6]] = other[...]

    def rows(base, count):
        half, at = base // HALF_ROWS, base % HALF_ROWS
        return halves[half, at : at + count].astype(F32) * scale

    for t in range(9):
        g_first[t] = rows(t * C1, C1)
    for t in range(3):
        base = FIRST_ROWS + 6 * t * C1
        g_down[t, :, :C1] = rows(base, 3 * C1)
        g_down[t, :, C1:] = rows(base + 3 * C1, 3 * C1)
    for t in range(4):
        g_up[t] = rows(FIRST_ROWS + DOWN_ROWS + t * C2, C2)


def shifted(x, by):
    j = lax.broadcasted_iota(jnp.int32, x.shape, 0) % 16
    moved = pltpu.roll(x, by % x.shape[0], 0)
    return jnp.where(j == (0 if by > 0 else 15), 0.0, moved)


def spread(x):
    return jnp.concatenate(
        [shifted(x[:, C1:], 1).astype(BF16), x.astype(BF16), shifted(x[:, :C1], -1).astype(BF16)], axis=1
    )


def window(ref, a, t):
    part = ref[(a + t) % 2, (a + t) // 2 : (a + t) // 2 + 16]
    return part.reshape(256, part.shape[-1])


def net_kernel(
    places, side_a, middle, side_b, fb, rf, rft, wd, rdt, ru,
    mid_o, strip_b, keep, send,
    fs, cs, xv, hv, gv, g4, gs, bs, can_b, can_g, halves,
):
    start_c, core = places[5], places[6]
    at_a, at_b = 32 * (1 - core), 32 * core

    def put(base, value):
        half, at = base // HALF_ROWS, base % HALF_ROWS
        halves[core if half == 0 else 1 - core, at : at + value.shape[0]] = value.astype(BF16)

    for ref in (xv, hv, gv):
        edge = jnp.zeros((16, ref.shape[-1]), BF16)
        ref[0, 0] = edge
        ref[1, 16] = edge
    g4[16] = jnp.zeros((16, 2 * C2), BF16)

    def stage(r, carry):
        for at, ref in ((at_a, side_a), (16, middle), (at_b, side_b)):
            spot = pl.ds(pl.multiple_of(at + 8, 8), 16)
            fs[r, spot, :] = ref[0, r].astype(F32)
            cs[r, spot, :] = ref[1, r].astype(F32)
        return carry

    lax.fori_loop(0, 32, stage, 0, unroll=4)
    j = lax.broadcasted_iota(jnp.int32, (16, C1), 0)

    def load(i, carry):
        for a in range(2):
            r = 2 * i + a
            at = start_c + 8
            before = jnp.where(j == 0, 0.0, fs[r, pl.ds(at - 1, 16, 2), :])
            even = fs[r, pl.ds(at, 16, 2), :]
            odd = fs[r, pl.ds(at + 1, 16, 2), :]
            after = jnp.where(j == 15, 0.0, fs[r, pl.ds(at + 2, 16, 2), :])
            xv[1 - a, i + a] = jnp.concatenate([before, even, odd, after], axis=1).astype(BF16)
            gs[a, i, :, :C1] = cs[r, pl.ds(at, 16, 2), :] * fb[a, i, :, :C1]
            gs[a, i, :, C1:] = cs[r, pl.ds(at + 1, 16, 2), :] * fb[a, i, :, C1:]
        return carry

    lax.fori_loop(0, 16, load, 0, unroll=2)

    h, slope_h = [], []
    for a in range(2):
        pre = dot(window(xv, a, 0), rf[0]) + dot(window(xv, a, 1), rf[1]) + dot(window(xv, a, 2), rf[2])
        sig = lax.logistic(pre)
        value = pre * sig
        slope_h.append(sig + value * (1.0 - sig))
        h.append(value.astype(BF16))
        hv[1 - a, a : a + 16] = jnp.concatenate(
            [shifted(value[:, C1:], 1).astype(BF16), h[a]], axis=1
        ).reshape(16, 16, 3 * C1)
    pre = dot(window(hv, 0, 0), wd[0]) + dot(window(hv, 0, 1), wd[1]) + dot(window(hv, 0, 2), wd[2])
    sig = lax.logistic(pre)
    value = pre * sig
    slope_d = sig + value * (1.0 - sig)
    d = value.astype(BF16)
    d_t = value.T.astype(BF16)
    g_d = jnp.zeros((256, C2), F32)
    for a in range(2):
        out = h[a].astype(F32) + dot(d, ru[a])
        bs[a] = (fb[a].reshape(256, 2 * C1) * out).reshape(16, 16, 2 * C1)
        g = gs[a].reshape(256, 2 * C1).astype(BF16)
        g_d = g_d + dot_nt(g, ru[a])
        g_up = dot(d_t, g)
        base = FIRST_ROWS + DOWN_ROWS + 2 * a * C2
        put(base, g_up[:, :C1])
        put(base + C2, g_up[:, C1:])
    g_pre = g_d.astype(BF16).astype(F32) * slope_d
    g4[0:16] = jnp.concatenate([g_pre.astype(BF16), shifted(g_pre, -1).astype(BF16)], axis=1).reshape(
        16, 16, 2 * C2
    )
    g_pre_t = g_pre.T.astype(BF16)
    for t in range(3):
        g_down = dot(g_pre_t, window(hv, 0, t)).T
        base = FIRST_ROWS + 6 * t * C1
        put(base, g_down[:, :C1])
        put(base + 3 * C1, g_down[:, C1:])
    here = g4[0:16].reshape(256, 2 * C2)
    below = g4[1:17].reshape(256, 2 * C2)
    g_h = [dot_nt(here, rdt[1]), dot_nt(here, rdt[2]) + dot_nt(below, rdt[0])]
    g_t = []
    for a in range(2):
        g_pre = (gs[a].reshape(256, 2 * C1) + g_h[a]) * slope_h[a]
        gv[1 - a, a : a + 16] = spread(g_pre).reshape(16, 16, 4 * C1)
        g_t.append(g_pre.T.astype(BF16))
    for t in range(3):
        g_first = dot(g_t[0], window(xv, 0, t)) + dot(g_t[1], window(xv, 1, t))
        for ct in range(3):
            block = (
                g_first[:C1, ct * C1 : (ct + 1) * C1] + g_first[C1:, (ct + 1) * C1 : (ct + 2) * C1]
            )
            put((3 * t + ct) * C1, block.T)
    put(USED_ROWS, jnp.zeros((2 * HALF_ROWS - USED_ROWS, C1), F32))
    keep[...] = halves[0]
    send[:HALF_ROWS] = halves[1]
    for a in range(2):
        g_x = (
            dot_nt(window(gv, a, 0), rft[0])
            + dot_nt(window(gv, a, 1), rft[1])
            + dot_nt(window(gv, a, 2), rft[2])
        )
        gs[a] = g_x.reshape(16, 16, 2 * C1)

    def clear(r, carry):
        can_b[r] = jnp.zeros((48, C1), F32)
        can_g[r] = jnp.zeros((48, C1), F32)
        return carry

    lax.fori_loop(0, 32, clear, 0, unroll=4)

    def place(i, carry):
        for a in range(2):
            r = 2 * i + a
            for b in range(2):
                can_b[r, pl.ds(start_c + b, 16, 2), :] = bs[a, i, :, b * C1 : (b + 1) * C1]
                can_g[r, pl.ds(start_c + b, 16, 2), :] = gs[a, i, :, b * C1 : (b + 1) * C1]
        return carry

    lax.fori_loop(0, 16, place, 0, unroll=2)

    def give(r, carry):
        for k, canvas in enumerate((can_b, can_g)):
            mid_o[k, r] = canvas[r, 16:32]
            strip = canvas[r, pl.ds(pl.multiple_of(at_a, 16), 16), :].astype(BF16)
            send[pl.ds(pl.multiple_of(HALF_ROWS + (32 * k + r) * 16, 16), 16)] = strip
            strip_b[k, r] = canvas[r, pl.ds(pl.multiple_of(at_b, 16), 16), :].astype(BF16)
        return carry

    lax.fori_loop(0, 32, give, 0, unroll=2)


VMEM = pl.BlockSpec(memory_space=pltpu.VMEM)
SMEM = pl.BlockSpec(memory_space=pltpu.SMEM)


def prepared(where, offsets, table, w_first, w_down, w_up):
    return pl.pallas_call(
        prepare_kernel,
        out_shape=(
            jax.ShapeDtypeStruct((8,), jnp.int32),
            jax.ShapeDtypeStruct((2, 16, 16, 2 * C1), F32),
            jax.ShapeDtypeStruct((3, 4 * C1, 2 * C1), BF16),
            jax.ShapeDtypeStruct((3, 2 * C1, 4 * C1), BF16),
            jax.ShapeDtypeStruct((3, 2 * C1, 2 * C2), BF16),
            jax.ShapeDtypeStruct((2, C2, 2 * C1), BF16),
        ),
        in_specs=[SMEM, SMEM, VMEM, VMEM, VMEM, VMEM],
        out_specs=[SMEM] + [VMEM] * 5,
        compiler_params=pltpu.CompilerParams(vmem_limit_bytes=10 * 2**20),
        cost_estimate=pl.CostEstimate(flops=5 * 10**6, bytes_accessed=10**7, transcendentals=0),
        name="prepare",
    )(where, offsets, table, w_first, w_down, w_up)


def patch_work(places, side_a, middle, side_b, fb, rf, rft, wd, rdt, ru):
    return pl.pallas_call(
        net_kernel,
        out_shape=(
            jax.ShapeDtypeStruct((2, 32, 16, C1), F32),
            jax.ShapeDtypeStruct((2, 32, 16, C1), BF16),
            jax.ShapeDtypeStruct((HALF_ROWS, C1), BF16),
            jax.ShapeDtypeStruct((HALF_ROWS + 2 * 32 * 16, C1), BF16),
        ),
        in_specs=[SMEM] + [VMEM] * 9,
        out_specs=[VMEM] * 4,
        scratch_shapes=[
            pltpu.VMEM((32, 64, C1), F32),
            pltpu.VMEM((32, 64, C1), F32),
            pltpu.VMEM((2, 17, 16, 4 * C1), BF16),
            pltpu.VMEM((2, 17, 16, 3 * C1), BF16),
            pltpu.VMEM((2, 17, 16, 4 * C1), BF16),
            pltpu.VMEM((17, 16, 2 * C2), BF16),
            pltpu.VMEM((2, 16, 16, 2 * C1), F32),
            pltpu.VMEM((2, 16, 16, 2 * C1), F32),
            pltpu.VMEM((32, 48, C1), F32),
            pltpu.VMEM((32, 48, C1), F32),
            pltpu.VMEM((2, HALF_ROWS, C1), BF16),
        ],
        compiler_params=pltpu.CompilerParams(vmem_limit_bytes=24 * 2**20),
        cost_estimate=pl.CostEstimate(flops=2 * 10**9, bytes_accessed=10**7, transcendentals=200000),
        name="patch_work",
    )(places, side_a, middle, side_b, fb, rf, rft, wd, rdt, ru)


def small_call(body, name, outs, scratch, *args, smem=0):
    return pl.pallas_call(
        body,
        out_shape=tuple(jax.ShapeDtypeStruct(shape, kind) for shape, kind in outs),
        in_specs=[SMEM] * smem + [VMEM] * (len(args) - smem),
        out_specs=[VMEM] * len(outs),
        scratch_shapes=scratch,
        compiler_params=pltpu.CompilerParams(vmem_limit_bytes=10 * 2**20),
        cost_estimate=pl.CostEstimate(flops=10**6, bytes_accessed=2 * 10**6, transcendentals=0),
        name=name,
    )(*args)


def swapped_b(x, axes):
    size = lax.axis_size(axes)
    pairs = [(i, i + 1) for i in range(1, size - 1, 2)]
    return lax.ppermute(x, axes, pairs + [(j, i) for i, j in pairs])


def swapped_a(x, axis):
    return lax.ppermute(x, axis, [(0, 1), (1, 0)])


def added(x, y):
    return (x.astype(F32) + y.astype(F32)).astype(BF16)


def scattered(x, axes):
    size = lax.axis_size(axes)
    parts = x.reshape(size, x.shape[0] // size, x.shape[1])
    got = lax.all_to_all(parts, axes, 0, 0, tiled=True)
    return got.astype(F32).sum(0).astype(BF16)


def gathered(x, axes):
    size = lax.axis_size(axes)
    parts = jnp.broadcast_to(x[None], (size,) + x.shape)
    return lax.all_to_all(parts, axes, 0, 0, tiled=True)


def per_device(field, cotangent, w_first, w_down, w_up, offsets, blend_table):
    rows_n = lax.axis_size(ROW)
    cols_n = lax.axis_size(COL)
    row_at = lax.axis_index(ROW)
    col_at = lax.axis_index(COL)
    where = jnp.stack([row_at, col_at]).astype(jnp.int32)
    both = jnp.stack([field, cotangent])
    places, fb, rf, rft, rdt, ru = prepared(
        where, offsets.transpose(0, 2, 1), blend_table, w_first, w_down, w_up
    )
    row_a, row_b = swapped_a(both, "zh"), swapped_b(both, ROW)
    row_a, row_b, places, fb, rf, rft, rdt, ru = lax.optimization_barrier(
        (row_a, row_b, places, fb, rf, rft, rdt, ru)
    )
    window_shape = (2, 32, TILE, C1)
    to_a, own, to_b = small_call(
        assemble_kernel,
        "assemble",
        [(window_shape, BF16)] * 3,
        [pltpu.VMEM((2, 48, TILE, C1), BF16)],
        places,
        row_a,
        both,
        row_b,
        smem=1,
    )
    side_a, side_b = swapped_a(to_a, "core"), swapped_b(to_b, COL)
    own, strip_b, keep, send = patch_work(
        places, side_a, own, side_b, fb, rf, rft, w_down.reshape(3, 3 * C1, C2), rdt, ru
    )
    got = swapped_a(send, "core")
    from_b = swapped_b(strip_b, COL)
    part = added(keep, got[:HALF_ROWS])
    part = scattered(part, ("x", "y"))
    part, from_b = lax.optimization_barrier((part, from_b))
    part = gathered(part, ("zl", "zh")).astype(F32).sum(0).astype(BF16)
    tile_shape = (2, TILE, TILE, C1)
    to_a, own, to_b = small_call(
        add_kernel,
        "add",
        [(tile_shape, BF16), (tile_shape, F32), (tile_shape, BF16)],
        [pltpu.VMEM((2, 48, TILE, C1), F32)],
        places,
        got,
        own,
        from_b,
        smem=1,
    )
    part, own, to_a, to_b = lax.optimization_barrier((part, own, to_a, to_b))
    row_a, row_b = swapped_a(to_a, "zh"), swapped_b(to_b, ROW)
    part = gathered(part, ("x", "y")).reshape(-1, C1)
    part, own, row_a, row_b = lax.optimization_barrier((part, own, row_a, row_b))
    other = swapped_a(part, "core")
    blended, field_grad = small_call(
        finish_kernel,
        "finish",
        [(field.shape, BF16), (field.shape, F32)],
        [],
        own,
        row_a,
        row_b,
    )
    scale = 1.0 / math.sqrt(TILE * rows_n * TILE * cols_n)
    g_first, g_down, g_up = small_call(
        functools.partial(unpack_kernel, scale),
        "unpack",
        [((9, C1, C1), F32), ((3, 3 * C1, C2), F32), ((4, C2, C1), F32)],
        [pltpu.VMEM((2, HALF_ROWS, C1), BF16)],
        places,
        part,
        other,
        smem=1,
    )
    return (
        blended,
        field_grad,
        g_first.reshape(w_first.shape),
        g_down.reshape(w_down.shape),
        g_up.reshape(w_up.shape),
    )


def solution(mesh):
    fine = Mesh(mesh.devices.reshape(8, 4, 2, 4, 2), ("y", "zl", "core", "x", "zh"))
    tiles = P(ROW, COL, None)
    return jax.shard_map(
        per_device,
        mesh=fine,
        in_specs=(tiles, tiles, P(), P(), P(), P(), P()),
        out_specs=(tiles, tiles, P(), P(), P()),
        check_vma=False,
    )
```

```python
import functools
import math

import jax
import jax.numpy as jnp
from jax import lax
from jax.experimental import pallas as pl
from jax.experimental.pallas import tpu as pltpu
from jax.sharding import Mesh, PartitionSpec as P

MARGIN = 8
ROW = ("x", "zh")
COL = ("y", "zl", "core")
F32 = jnp.float32
BF16 = jnp.bfloat16
REACH = 2
FAR = 1000
TILE = 16
C1 = 128
C2 = 256
FIRST_ROWS = 9 * C1
DOWN_ROWS = 18 * C1
UP_ROWS = 4 * C2
USED_ROWS = FIRST_ROWS + DOWN_ROWS + UP_ROWS
HALF_ROWS = 2304


def dot(a, b):
    return lax.dot_general(a, b, (((1,), (0,)), ((), ())), preferred_element_type=F32)


def dot_nt(a, b):
    return lax.dot_general(a, b, (((1,), (1,)), ((), ())), preferred_element_type=F32)


def prepare_kernel(
    where, offsets, table, w_first, w_down, w_up,
    places, fb, rf, rft, rdt, ru,
):
    row_at, col_at = where[0], where[1]
    rows_n, cols_n = offsets.shape[0], offsets.shape[2]
    core, zh = lax.rem(col_at, 2), lax.rem(row_at, 2)
    col_b = jnp.clip(col_at - 1 + 2 * core, 0, cols_n - 1)
    for k, col in enumerate((col_at + 1 - 2 * core, col_at, col_b)):
        places[k] = MARGIN + offsets[row_at, 0, col]
    places[3] = 32 * (1 - zh)
    places[4] = 32 * zh
    places[5] = MARGIN + offsets[row_at, 1, col_at]
    places[6] = core
    places[7] = 0
    sub = lax.broadcasted_iota(jnp.int32, (32, 32), 0)
    lane = lax.broadcasted_iota(jnp.int32, (32, 32), 1)
    column = jnp.where(sub < 16, 2 * sub, 2 * (sub - 16) + 1)
    table_t = table[...].astype(F32).T.astype(BF16)
    own_r = offsets[row_at, 0, col_at]
    own_c = offsets[row_at, 1, col_at]
    total = jnp.zeros((32, 32), F32)
    own = jnp.zeros((32, 32), F32)
    for row_step in range(-REACH, REACH + 1):
        for col_step in range(-REACH, REACH + 1):
            near_r, near_c = row_at + row_step, col_at + col_step
            inside = (near_r >= 0) & (near_r < rows_n) & (near_c >= 0) & (near_c < cols_n)
            at_r = jnp.clip(near_r, 0, rows_n - 1)
            at_c = jnp.clip(near_c, 0, cols_n - 1)
            down_by = row_step * TILE + offsets[at_r, 0, at_c] - own_r
            right_by = col_step * TILE + offsets[at_r, 1, at_c] - own_c
            down_by = jnp.where(inside, down_by, FAR)
            pick_c = (column - right_by == lane).astype(F32).astype(BF16)
            pick_r = (lane - down_by == sub).astype(F32).astype(BF16)
            placed = dot(pick_c, table_t)
            if row_step == 0 and col_step == 0:
                own = placed
            total = total + dot(placed.astype(BF16), pick_r)
    share = own / total
    for r in range(32):
        fb[r % 2, r // 2, :, :C1] = jnp.broadcast_to(share[:16, r : r + 1], (16, C1))
        fb[r % 2, r // 2, :, C1:] = jnp.broadcast_to(share[16:, r : r + 1], (16, C1))
    none = jnp.zeros((C1, C1), BF16)
    for t in range(3):
        for v in range(4):
            for b in range(2):
                rows, cols = pl.ds(v * C1, C1), pl.ds(b * C1, C1)
                held = 0 <= v - b <= 2
                rf[t, rows, cols] = w_first[t, v - b] if held else none
                rft[t, cols, rows] = w_first[2 - t, 2 - v + b] if held else none
        rdt[t, :C1, :C2] = w_down[t, 1]
        rdt[t, :C1, C2:] = jnp.zeros((C1, C2), BF16)
        rdt[t, C1:, :C2] = w_down[t, 2]
        rdt[t, C1:, C2:] = w_down[t, 0]
    for a in range(2):
        for b in range(2):
            ru[a, :, pl.ds(b * C1, C1)] = w_up[a, b]


def assemble_kernel(places, from_a, both, from_b, to_a, own, to_b, grown):
    grown[:, pl.ds(places[3], 16)] = from_a[...]
    grown[:, 16:32] = both[...]
    grown[:, pl.ds(places[4], 16)] = from_b[...]
    for side, out in enumerate((to_a, own, to_b)):
        out[...] = grown[:, pl.ds(places[side], 32)]


def add_kernel(places, from_a, own, from_b, to_a, mid, to_b, canvas):
    canvas[...] = jnp.zeros_like(canvas)
    canvas[:, pl.ds(places[1], 32)] = own[...]
    for side, strip in ((0, from_a[HALF_ROWS:].reshape(2, 32, 16, C1)), (2, from_b[...])):
        spot = (slice(None), pl.ds(places[side], 32))
        canvas[spot] = canvas[spot] + strip.astype(F32)
    to_a[...] = canvas[:, pl.ds(places[3], 16)].astype(BF16)
    mid[...] = canvas[:, 16:32]
    to_b[...] = canvas[:, pl.ds(places[4], 16)].astype(BF16)


def finish_kernel(own, from_a, from_b, blended, field_grad):
    total = own[...] + from_a[...].astype(F32) + from_b[...].astype(F32)
    blended[...] = total[0].astype(BF16)
    field_grad[...] = total[1]


def unpack_kernel(scale, places, own, other, g_first, g_down, g_up, halves):
    halves[places[6]] = own[...]
    halves[1 - places[6]] = other[...]

    def rows(base, count):
        half, at = base // HALF_ROWS, base % HALF_ROWS
        return halves[half, at : at + count].astype(F32) * scale

    for t in range(9):
        g_first[t] = rows(t * C1, C1)
    for t in range(3):
        base = FIRST_ROWS + 6 * t * C1
        g_down[t, :, :C1] = rows(base, 3 * C1)
        g_down[t, :, C1:] = rows(base + 3 * C1, 3 * C1)
    for t in range(4):
        g_up[t] = rows(FIRST_ROWS + DOWN_ROWS + t * C2, C2)


def shifted(x, by):
    j = lax.broadcasted_iota(jnp.int32, x.shape, 0) % 16
    moved = pltpu.roll(x, by % x.shape[0], 0)
    return jnp.where(j == (0 if by > 0 else 15), 0.0, moved)


def spread(x):
    return jnp.concatenate(
        [shifted(x[:, C1:], 1).astype(BF16), x.astype(BF16), shifted(x[:, :C1], -1).astype(BF16)], axis=1
    )


def window(ref, a, t):
    part = ref[(a + t) % 2, (a + t) // 2 : (a + t) // 2 + 16]
    return part.reshape(256, part.shape[-1])


def net_kernel(
    places, side_b, middle, side_a, fb, rf, rft, wd, rdt, ru,
    mid_o, strip_b, keep, send,
    fs, cs, xv, hv, gv, g4, gs, bs, can_b, can_g, halves,
):
    start_c, core = places[5], places[6]
    at_a, at_b = 32 * (1 - core), 32 * core

    def put(base, value):
        half, at = base // HALF_ROWS, base % HALF_ROWS
        halves[core if half == 0 else 1 - core, at : at + value.shape[0]] = value.astype(BF16)

    for ref in (xv, hv, gv):
        edge = jnp.zeros((16, ref.shape[-1]), BF16)
        ref[0, 0] = edge
        ref[1, 16] = edge
    g4[16] = jnp.zeros((16, 2 * C2), BF16)

    def stage(r, carry):
        for at, ref in ((at_a, side_a), (16, middle), (at_b, side_b)):
            spot = pl.ds(pl.multiple_of(at + 8, 8), 16)
            fs[r, spot, :] = ref[0, r].astype(F32)
            cs[r, spot, :] = ref[1, r].astype(F32)
        return carry

    lax.fori_loop(0, 32, stage, 0, unroll=4)
    j = lax.broadcasted_iota(jnp.int32, (16, C1), 0)

    def load(i, carry):
        for a in range(2):
            r = 2 * i + a
            at = start_c + 8
            before = jnp.where(j == 0, 0.0, fs[r, pl.ds(at - 1, 16, 2), :])
            even = fs[r, pl.ds(at, 16, 2), :]
            odd = fs[r, pl.ds(at + 1, 16, 2), :]
            after = jnp.where(j == 15, 0.0, fs[r, pl.ds(at + 2, 16, 2), :])
            xv[1 - a, i + a] = jnp.concatenate([before, even, odd, after], axis=1).astype(BF16)
            gs[a, i, :, :C1] = cs[r, pl.ds(at, 16, 2), :] * fb[a, i, :, :C1]
            gs[a, i, :, C1:] = cs[r, pl.ds(at + 1, 16, 2), :] * fb[a, i, :, C1:]
        return carry

    lax.fori_loop(0, 16, load, 0, unroll=2)

    h, slope_h = [], []
    for a in range(2):
        pre = dot(window(xv, a, 0), rf[0]) + dot(window(xv, a, 1), rf[1]) + dot(window(xv, a, 2), rf[2])
        sig = lax.logistic(pre)
        value = pre * sig
        slope_h.append(sig + value * (1.0 - sig))
        h.append(value.astype(BF16))
        hv[1 - a, a : a + 16] = jnp.concatenate(
            [shifted(value[:, C1:], 1).astype(BF16), h[a]], axis=1
        ).reshape(16, 16, 3 * C1)
    pre = dot(window(hv, 0, 0), wd[0]) + dot(window(hv, 0, 1), wd[1]) + dot(window(hv, 0, 2), wd[2])
    sig = lax.logistic(pre)
    value = pre * sig
    slope_d = sig + value * (1.0 - sig)
    d = value.astype(BF16)
    d_t = value.T.astype(BF16)
    g_d = jnp.zeros((256, C2), F32)
    for a in range(2):
        out = h[a].astype(F32) + dot(d, ru[a])
        bs[a] = (fb[a].reshape(256, 2 * C1) * out).reshape(16, 16, 2 * C1)
        g = gs[a].reshape(256, 2 * C1).astype(BF16)
        g_d = g_d + dot_nt(g, ru[a])
        g_up = dot(d_t, g)
        base = FIRST_ROWS + DOWN_ROWS + 2 * a * C2
        put(base, g_up[:, :C1])
        put(base + C2, g_up[:, C1:])
    g_pre = g_d.astype(BF16).astype(F32) * slope_d
    g4[0:16] = jnp.concatenate([g_pre.astype(BF16), shifted(g_pre, -1).astype(BF16)], axis=1).reshape(
        16, 16, 2 * C2
    )
    g_pre_t = g_pre.T.astype(BF16)
    for t in range(3):
        g_down = dot(g_pre_t, window(hv, 0, t)).T
        base = FIRST_ROWS + 6 * t * C1
        put(base, g_down[:, :C1])
        put(base + 3 * C1, g_down[:, C1:])
    here = g4[0:16].reshape(256, 2 * C2)
    below = g4[1:17].reshape(256, 2 * C2)
    g_h = [dot_nt(here, rdt[1]), dot_nt(here, rdt[2]) + dot_nt(below, rdt[0])]
    g_t = []
    for a in range(2):
        g_pre = (gs[a].reshape(256, 2 * C1) + g_h[a]) * slope_h[a]
        gv[1 - a, a : a + 16] = spread(g_pre).reshape(16, 16, 4 * C1)
        g_t.append(g_pre.T.astype(BF16))
    for t in range(3):
        g_first = dot(g_t[0], window(xv, 0, t)) + dot(g_t[1], window(xv, 1, t))
        for ct in range(3):
            block = (
                g_first[:C1, ct * C1 : (ct + 1) * C1] + g_first[C1:, (ct + 1) * C1 : (ct + 2) * C1]
            )
            put((3 * t + ct) * C1, block.T)
    put(USED_ROWS, jnp.zeros((2 * HALF_ROWS - USED_ROWS, C1), F32))
    keep[...] = halves[0]
    send[:HALF_ROWS] = halves[1]
    for a in range(2):
        g_x = (
            dot_nt(window(gv, a, 0), rft[0])
            + dot_nt(window(gv, a, 1), rft[1])
            + dot_nt(window(gv, a, 2), rft[2])
        )
        gs[a] = g_x.reshape(16, 16, 2 * C1)

    def clear(r, carry):
        can_b[r] = jnp.zeros((48, C1), F32)
        can_g[r] = jnp.zeros((48, C1), F32)
        return carry

    lax.fori_loop(0, 32, clear, 0, unroll=4)

    def place(i, carry):
        for a in range(2):
            r = 2 * i + a
            for b in range(2):
                can_b[r, pl.ds(start_c + b, 16, 2), :] = bs[a, i, :, b * C1 : (b + 1) * C1]
                can_g[r, pl.ds(start_c + b, 16, 2), :] = gs[a, i, :, b * C1 : (b + 1) * C1]
        return carry

    lax.fori_loop(0, 16, place, 0, unroll=2)

    def give(r, carry):
        for k, canvas in enumerate((can_b, can_g)):
            mid_o[k, r] = canvas[r, 16:32]
            strip = canvas[r, pl.ds(pl.multiple_of(at_a, 16), 16), :].astype(BF16)
            send[pl.ds(pl.multiple_of(HALF_ROWS + (32 * k + r) * 16, 16), 16)] = strip
            strip_b[k, r] = canvas[r, pl.ds(pl.multiple_of(at_b, 16), 16), :].astype(BF16)
        return carry

    lax.fori_loop(0, 32, give, 0, unroll=2)


VMEM = pl.BlockSpec(memory_space=pltpu.VMEM)
SMEM = pl.BlockSpec(memory_space=pltpu.SMEM)


def prepared(where, offsets, table, w_first, w_down, w_up):
    return pl.pallas_call(
        prepare_kernel,
        out_shape=(
            jax.ShapeDtypeStruct((8,), jnp.int32),
            jax.ShapeDtypeStruct((2, 16, 16, 2 * C1), F32),
            jax.ShapeDtypeStruct((3, 4 * C1, 2 * C1), BF16),
            jax.ShapeDtypeStruct((3, 2 * C1, 4 * C1), BF16),
            jax.ShapeDtypeStruct((3, 2 * C1, 2 * C2), BF16),
            jax.ShapeDtypeStruct((2, C2, 2 * C1), BF16),
        ),
        in_specs=[SMEM, SMEM, VMEM, VMEM, VMEM, VMEM],
        out_specs=[SMEM] + [VMEM] * 5,
        compiler_params=pltpu.CompilerParams(vmem_limit_bytes=10 * 2**20),
        cost_estimate=pl.CostEstimate(flops=5 * 10**6, bytes_accessed=10**7, transcendentals=0),
        name="prepare",
    )(where, offsets, table, w_first, w_down, w_up)


def patch_work(places, side_a, middle, side_b, fb, rf, rft, wd, rdt, ru):
    return pl.pallas_call(
        net_kernel,
        out_shape=(
            jax.ShapeDtypeStruct((2, 32, 16, C1), F32),
            jax.ShapeDtypeStruct((2, 32, 16, C1), BF16),
            jax.ShapeDtypeStruct((HALF_ROWS, C1), BF16),
            jax.ShapeDtypeStruct((HALF_ROWS + 2 * 32 * 16, C1), BF16),
        ),
        in_specs=[SMEM] + [VMEM] * 9,
        out_specs=[VMEM] * 4,
        scratch_shapes=[
            pltpu.VMEM((32, 64, C1), F32),
            pltpu.VMEM((32, 64, C1), F32),
            pltpu.VMEM((2, 17, 16, 4 * C1), BF16),
            pltpu.VMEM((2, 17, 16, 3 * C1), BF16),
            pltpu.VMEM((2, 17, 16, 4 * C1), BF16),
            pltpu.VMEM((17, 16, 2 * C2), BF16),
            pltpu.VMEM((2, 16, 16, 2 * C1), F32),
            pltpu.VMEM((2, 16, 16, 2 * C1), F32),
            pltpu.VMEM((32, 48, C1), F32),
            pltpu.VMEM((32, 48, C1), F32),
            pltpu.VMEM((2, HALF_ROWS, C1), BF16),
        ],
        compiler_params=pltpu.CompilerParams(vmem_limit_bytes=24 * 2**20),
        cost_estimate=pl.CostEstimate(flops=2 * 10**9, bytes_accessed=10**7, transcendentals=200000),
        name="patch_work",
    )(places, side_b, middle, side_a, fb, rf, rft, wd, rdt, ru)


def small_call(body, name, outs, scratch, *args, smem=0):
    return pl.pallas_call(
        body,
        out_shape=tuple(jax.ShapeDtypeStruct(shape, kind) for shape, kind in outs),
        in_specs=[SMEM] * smem + [VMEM] * (len(args) - smem),
        out_specs=[VMEM] * len(outs),
        scratch_shapes=scratch,
        compiler_params=pltpu.CompilerParams(vmem_limit_bytes=10 * 2**20),
        cost_estimate=pl.CostEstimate(flops=10**6, bytes_accessed=2 * 10**6, transcendentals=0),
        name=name,
    )(*args)


def swapped_b(x, axes):
    size = lax.axis_size(axes)
    pairs = [(i, i + 1) for i in range(1, size - 1, 2)]
    return lax.ppermute(x, axes, pairs + [(j, i) for i, j in pairs])


def swapped_a(x, axis):
    return lax.ppermute(x, axis, [(0, 1), (1, 0)])


def added(x, y):
    return (x.astype(F32) + y.astype(F32)).astype(BF16)


def scattered(x, axes):
    size = lax.axis_size(axes)
    parts = x.reshape(size, x.shape[0] // size, x.shape[1])
    got = lax.all_to_all(parts, axes, 0, 0, tiled=True)
    return got.astype(F32).sum(0).astype(BF16)


def gathered(x, axes):
    size = lax.axis_size(axes)
    parts = jnp.broadcast_to(x[None], (size,) + x.shape)
    return lax.all_to_all(parts, axes, 0, 0, tiled=True)


def per_device(field, cotangent, w_first, w_down, w_up, offsets, blend_table):
    rows_n = lax.axis_size(ROW)
    cols_n = lax.axis_size(COL)
    row_at = lax.axis_index(ROW)
    col_at = lax.axis_index(COL)
    where = jnp.stack([row_at, col_at]).astype(jnp.int32)
    both = jnp.stack([field, cotangent])
    places, fb, rf, rft, rdt, ru = prepared(
        where, offsets.transpose(0, 2, 1), blend_table, w_first, w_down, w_up
    )
    row_a, row_b = swapped_a(both, "zh"), swapped_b(both, ROW)
    row_a, row_b, places, fb, rf, rft, rdt, ru = lax.optimization_barrier(
        (row_a, row_b, places, fb, rf, rft, rdt, ru)
    )
    window_shape = (2, 32, TILE, C1)
    to_a, own, to_b = small_call(
        assemble_kernel,
        "assemble",
        [(window_shape, BF16)] * 3,
        [pltpu.VMEM((2, 48, TILE, C1), BF16)],
        places,
        row_a,
        both,
        row_b,
        smem=1,
    )
    side_a, side_b = swapped_a(to_a, "core"), swapped_b(to_b, COL)
    own, strip_b, keep, send = patch_work(
        places, side_a, own, side_b, fb, rf, rft, w_down.reshape(3, 3 * C1, C2), rdt, ru
    )
    got = swapped_a(send, "core")
    from_b = swapped_b(strip_b, COL)
    part = added(keep, got[:HALF_ROWS])
    part = scattered(part, ("x", "y"))
    part, from_b = lax.optimization_barrier((part, from_b))
    part = gathered(part, ("zl", "zh")).astype(F32).sum(0).astype(BF16)
    tile_shape = (2, TILE, TILE, C1)
    to_a, own, to_b = small_call(
        add_kernel,
        "add",
        [(tile_shape, BF16), (tile_shape, F32), (tile_shape, BF16)],
        [pltpu.VMEM((2, 48, TILE, C1), F32)],
        places,
        got,
        own,
        from_b,
        smem=1,
    )
    row_a = swapped_a(to_a, "zh")
    part, own, row_a, to_b = lax.optimization_barrier((part, own, row_a, to_b))
    row_b = swapped_b(to_b, ROW)
    part = gathered(part, ("x", "y")).reshape(-1, C1)
    part, own, row_a, row_b = lax.optimization_barrier((part, own, row_a, row_b))
    other = swapped_a(part, "core")
    blended, field_grad = small_call(
        finish_kernel,
        "finish",
        [(field.shape, BF16), (field.shape, F32)],
        [],
        own,
        row_a,
        row_b,
    )
    scale = 1.0 / math.sqrt(TILE * rows_n * TILE * cols_n)
    g_first, g_down, g_up = small_call(
        functools.partial(unpack_kernel, scale),
        "unpack",
        [((9, C1, C1), F32), ((3, 3 * C1, C2), F32), ((4, C2, C1), F32)],
        [pltpu.VMEM((2, HALF_ROWS, C1), BF16)],
        places,
        part,
        other,
        smem=1,
    )
    return (
        blended,
        field_grad,
        g_first.reshape(w_first.shape),
        g_down.reshape(w_down.shape),
        g_up.reshape(w_up.shape),
    )


def solution(mesh):
    fine = Mesh(mesh.devices.reshape(8, 4, 2, 4, 2), ("y", "zl", "core", "x", "zh"))
    tiles = P(ROW, COL, None)
    return jax.shard_map(
        per_device,
        mesh=fine,
        in_specs=(tiles, tiles, P(), P(), P(), P(), P()),
        out_specs=(tiles, tiles, P(), P(), P()),
        check_vma=False,
    )
```

```python
import functools
import math

import jax
import jax.numpy as jnp
from jax import lax
from jax.experimental import pallas as pl
from jax.experimental.pallas import tpu as pltpu
from jax.sharding import Mesh, PartitionSpec as P

MARGIN = 8
ROW = ("x", "zh")
COL = ("y", "zl", "core")
F32 = jnp.float32
BF16 = jnp.bfloat16
REACH = 2
FAR = 1000
TILE = 16
C1 = 128
C2 = 256
FIRST_ROWS = 9 * C1
DOWN_ROWS = 18 * C1
UP_ROWS = 4 * C2
USED_ROWS = FIRST_ROWS + DOWN_ROWS + UP_ROWS
HALF_ROWS = 2304


def dot(a, b):
    return lax.dot_general(a, b, (((1,), (0,)), ((), ())), preferred_element_type=F32)


def dot_nt(a, b):
    return lax.dot_general(a, b, (((1,), (1,)), ((), ())), preferred_element_type=F32)


def prepare_kernel(
    where, offsets, table, w_first, w_down, w_up,
    places, fb, rf, rft, rdt, ru,
):
    row_at, col_at = where[0], where[1]
    rows_n, cols_n = offsets.shape[0], offsets.shape[2]
    core, zh = lax.rem(col_at, 2), lax.rem(row_at, 2)
    col_b = jnp.clip(col_at - 1 + 2 * core, 0, cols_n - 1)
    for k, col in enumerate((col_at + 1 - 2 * core, col_at, col_b)):
        places[k] = MARGIN + offsets[row_at, 0, col]
    places[3] = 32 * (1 - zh)
    places[4] = 32 * zh
    places[5] = MARGIN + offsets[row_at, 1, col_at]
    places[6] = core
    places[7] = 0
    sub = lax.broadcasted_iota(jnp.int32, (32, 32), 0)
    lane = lax.broadcasted_iota(jnp.int32, (32, 32), 1)
    column = jnp.where(sub < 16, 2 * sub, 2 * (sub - 16) + 1)
    table_t = table[...].astype(F32).T.astype(BF16)
    own_r = offsets[row_at, 0, col_at]
    own_c = offsets[row_at, 1, col_at]
    total = jnp.zeros((32, 32), F32)
    own = jnp.zeros((32, 32), F32)
    for row_step in range(-REACH, REACH + 1):
        for col_step in range(-REACH, REACH + 1):
            near_r, near_c = row_at + row_step, col_at + col_step
            inside = (near_r >= 0) & (near_r < rows_n) & (near_c >= 0) & (near_c < cols_n)
            at_r = jnp.clip(near_r, 0, rows_n - 1)
            at_c = jnp.clip(near_c, 0, cols_n - 1)
            down_by = row_step * TILE + offsets[at_r, 0, at_c] - own_r
            right_by = col_step * TILE + offsets[at_r, 1, at_c] - own_c
            down_by = jnp.where(inside, down_by, FAR)
            pick_c = (column - right_by == lane).astype(F32).astype(BF16)
            pick_r = (lane - down_by == sub).astype(F32).astype(BF16)
            placed = dot(pick_c, table_t)
            if row_step == 0 and col_step == 0:
                own = placed
            total = total + dot(placed.astype(BF16), pick_r)
    share = own / total
    for r in range(32):
        fb[r % 2, r // 2, :, :C1] = jnp.broadcast_to(share[:16, r : r + 1], (16, C1))
        fb[r % 2, r // 2, :, C1:] = jnp.broadcast_to(share[16:, r : r + 1], (16, C1))
    none = jnp.zeros((C1, C1), BF16)
    for t in range(3):
        for v in range(4):
            for b in range(2):
                rows, cols = pl.ds(v * C1, C1), pl.ds(b * C1, C1)
                held = 0 <= v - b <= 2
                rf[t, rows, cols] = w_first[t, v - b] if held else none
                rft[t, cols, rows] = w_first[2 - t, 2 - v + b] if held else none
        rdt[t, :C1, :C2] = w_down[t, 1]
        rdt[t, :C1, C2:] = jnp.zeros((C1, C2), BF16)
        rdt[t, C1:, :C2] = w_down[t, 2]
        rdt[t, C1:, C2:] = w_down[t, 0]
    for a in range(2):
        for b in range(2):
            ru[a, :, pl.ds(b * C1, C1)] = w_up[a, b]


def assemble_kernel(places, from_a, both, from_b, to_a, own, to_b, grown):
    grown[:, pl.ds(places[3], 16)] = from_a[...]
    grown[:, 16:32] = both[...]
    grown[:, pl.ds(places[4], 16)] = from_b[...]
    for side, out in enumerate((to_a, own, to_b)):
        out[...] = grown[:, pl.ds(places[side], 32)]


def add_kernel(places, from_a, own, from_b, to_a, mid, to_b, canvas):
    canvas[...] = jnp.zeros_like(canvas)
    canvas[:, pl.ds(places[1], 32)] = own[...]
    for side, strip in ((0, from_a[HALF_ROWS:].reshape(2, 32, 16, C1)), (2, from_b[...])):
        spot = (slice(None), pl.ds(places[side], 32))
        canvas[spot] = canvas[spot] + strip.astype(F32)
    to_a[...] = canvas[:, pl.ds(places[3], 16)].astype(BF16)
    mid[...] = canvas[:, 16:32]
    to_b[...] = canvas[:, pl.ds(places[4], 16)].astype(BF16)


def finish_kernel(own, from_a, from_b, blended, field_grad):
    total = own[...] + from_a[...].astype(F32) + from_b[...].astype(F32)
    blended[...] = total[0].astype(BF16)
    field_grad[...] = total[1]


def unpack_kernel(scale, places, own, other, g_first, g_down, g_up):
    def write(parts):
        def rows(base, count):
            at = base % HALF_ROWS
            return parts[base // HALF_ROWS][at : at + count].astype(F32) * scale

        for t in range(9):
            g_first[t] = rows(t * C1, C1)
        for t in range(3):
            base = FIRST_ROWS + 6 * t * C1
            g_down[t, :, :C1] = rows(base, 3 * C1)
            g_down[t, :, C1:] = rows(base + 3 * C1, 3 * C1)
        for t in range(4):
            g_up[t] = rows(FIRST_ROWS + DOWN_ROWS + t * C2, C2)

    pl.when(places[6] == 0)(lambda: write((own, other)))
    pl.when(places[6] == 1)(lambda: write((other, own)))


def shifted(x, by):
    j = lax.broadcasted_iota(jnp.int32, x.shape, 0) % 16
    moved = pltpu.roll(x, by % x.shape[0], 0)
    return jnp.where(j == (0 if by > 0 else 15), 0.0, moved)


def spread(x):
    return jnp.concatenate(
        [shifted(x[:, C1:], 1).astype(BF16), x.astype(BF16), shifted(x[:, :C1], -1).astype(BF16)], axis=1
    )


def window(ref, a, t):
    part = ref[(a + t) % 2, (a + t) // 2 : (a + t) // 2 + 16]
    return part.reshape(256, part.shape[-1])


def net_kernel(
    places, side_b, middle, side_a, fb, rf, rft, wd, rdt, ru,
    mid_o, strip_b, keep, send,
    fs, cs, xv, hv, gv, g4, gs, bs, can_b, can_g, halves,
):
    start_c, core = places[5], places[6]
    at_a, at_b = 32 * (1 - core), 32 * core

    def put(base, value):
        half, at = base // HALF_ROWS, base % HALF_ROWS
        halves[core if half == 0 else 1 - core, at : at + value.shape[0]] = value.astype(BF16)

    for ref in (xv, hv, gv):
        edge = jnp.zeros((16, ref.shape[-1]), BF16)
        ref[0, 0] = edge
        ref[1, 16] = edge
    g4[16] = jnp.zeros((16, 2 * C2), BF16)

    def stage(r, carry):
        for at, ref in ((at_a, side_a), (16, middle), (at_b, side_b)):
            spot = pl.ds(pl.multiple_of(at + 8, 8), 16)
            fs[r, spot, :] = ref[0, r].astype(F32)
            cs[r, spot, :] = ref[1, r].astype(F32)
        return carry

    lax.fori_loop(0, 32, stage, 0, unroll=4)
    j = lax.broadcasted_iota(jnp.int32, (16, C1), 0)

    def load(i, carry):
        for a in range(2):
            r = 2 * i + a
            at = start_c + 8
            before = jnp.where(j == 0, 0.0, fs[r, pl.ds(at - 1, 16, 2), :])
            even = fs[r, pl.ds(at, 16, 2), :]
            odd = fs[r, pl.ds(at + 1, 16, 2), :]
            after = jnp.where(j == 15, 0.0, fs[r, pl.ds(at + 2, 16, 2), :])
            xv[1 - a, i + a] = jnp.concatenate([before, even, odd, after], axis=1).astype(BF16)
            gs[a, i, :, :C1] = cs[r, pl.ds(at, 16, 2), :] * fb[a, i, :, :C1]
            gs[a, i, :, C1:] = cs[r, pl.ds(at + 1, 16, 2), :] * fb[a, i, :, C1:]
        return carry

    lax.fori_loop(0, 16, load, 0, unroll=2)

    h, slope_h = [], []
    for a in range(2):
        pre = dot(window(xv, a, 0), rf[0]) + dot(window(xv, a, 1), rf[1]) + dot(window(xv, a, 2), rf[2])
        sig = lax.logistic(pre)
        value = pre * sig
        slope_h.append(sig + value * (1.0 - sig))
        h.append(value.astype(BF16))
        hv[1 - a, a : a + 16] = jnp.concatenate(
            [shifted(value[:, C1:], 1).astype(BF16), h[a]], axis=1
        ).reshape(16, 16, 3 * C1)
    pre = dot(window(hv, 0, 0), wd[0]) + dot(window(hv, 0, 1), wd[1]) + dot(window(hv, 0, 2), wd[2])
    sig = lax.logistic(pre)
    value = pre * sig
    slope_d = sig + value * (1.0 - sig)
    d = value.astype(BF16)
    d_t = value.T.astype(BF16)
    g_d = jnp.zeros((256, C2), F32)
    for a in range(2):
        out = h[a].astype(F32) + dot(d, ru[a])
        bs[a] = (fb[a].reshape(256, 2 * C1) * out).reshape(16, 16, 2 * C1)
        g = gs[a].reshape(256, 2 * C1).astype(BF16)
        g_d = g_d + dot_nt(g, ru[a])
        g_up = dot(d_t, g)
        base = FIRST_ROWS + DOWN_ROWS + 2 * a * C2
        put(base, g_up[:, :C1])
        put(base + C2, g_up[:, C1:])
    g_pre = g_d.astype(BF16).astype(F32) * slope_d
    g4[0:16] = jnp.concatenate([g_pre.astype(BF16), shifted(g_pre, -1).astype(BF16)], axis=1).reshape(
        16, 16, 2 * C2
    )
    g_pre_t = g_pre.T.astype(BF16)
    for t in range(3):
        g_down = dot(g_pre_t, window(hv, 0, t)).T
        base = FIRST_ROWS + 6 * t * C1
        put(base, g_down[:, :C1])
        put(base + 3 * C1, g_down[:, C1:])
    here = g4[0:16].reshape(256, 2 * C2)
    below = g4[1:17].reshape(256, 2 * C2)
    g_h = [dot_nt(here, rdt[1]), dot_nt(here, rdt[2]) + dot_nt(below, rdt[0])]
    g_t = []
    for a in range(2):
        g_pre = (gs[a].reshape(256, 2 * C1) + g_h[a]) * slope_h[a]
        gv[1 - a, a : a + 16] = spread(g_pre).reshape(16, 16, 4 * C1)
        g_t.append(g_pre.T.astype(BF16))
    for t in range(3):
        g_first = dot(g_t[0], window(xv, 0, t)) + dot(g_t[1], window(xv, 1, t))
        for ct in range(3):
            block = (
                g_first[:C1, ct * C1 : (ct + 1) * C1] + g_first[C1:, (ct + 1) * C1 : (ct + 2) * C1]
            )
            put((3 * t + ct) * C1, block.T)
    put(USED_ROWS, jnp.zeros((2 * HALF_ROWS - USED_ROWS, C1), F32))
    keep[...] = halves[0]
    send[:HALF_ROWS] = halves[1]
    for a in range(2):
        g_x = (
            dot_nt(window(gv, a, 0), rft[0])
            + dot_nt(window(gv, a, 1), rft[1])
            + dot_nt(window(gv, a, 2), rft[2])
        )
        gs[a] = g_x.reshape(16, 16, 2 * C1)

    def clear(r, carry):
        can_b[r] = jnp.zeros((48, C1), F32)
        can_g[r] = jnp.zeros((48, C1), F32)
        return carry

    lax.fori_loop(0, 32, clear, 0, unroll=4)

    def place(i, carry):
        for a in range(2):
            r = 2 * i + a
            for b in range(2):
                can_b[r, pl.ds(start_c + b, 16, 2), :] = bs[a, i, :, b * C1 : (b + 1) * C1]
                can_g[r, pl.ds(start_c + b, 16, 2), :] = gs[a, i, :, b * C1 : (b + 1) * C1]
        return carry

    lax.fori_loop(0, 16, place, 0, unroll=2)

    def give(r, carry):
        for k, canvas in enumerate((can_b, can_g)):
            mid_o[k, r] = canvas[r, 16:32]
            strip = canvas[r, pl.ds(pl.multiple_of(at_a, 16), 16), :].astype(BF16)
            send[pl.ds(pl.multiple_of(HALF_ROWS + (32 * k + r) * 16, 16), 16)] = strip
            strip_b[k, r] = canvas[r, pl.ds(pl.multiple_of(at_b, 16), 16), :].astype(BF16)
        return carry

    lax.fori_loop(0, 32, give, 0, unroll=2)


VMEM = pl.BlockSpec(memory_space=pltpu.VMEM)
SMEM = pl.BlockSpec(memory_space=pltpu.SMEM)


def prepared(where, offsets, table, w_first, w_down, w_up):
    return pl.pallas_call(
        prepare_kernel,
        out_shape=(
            jax.ShapeDtypeStruct((8,), jnp.int32),
            jax.ShapeDtypeStruct((2, 16, 16, 2 * C1), F32),
            jax.ShapeDtypeStruct((3, 4 * C1, 2 * C1), BF16),
            jax.ShapeDtypeStruct((3, 2 * C1, 4 * C1), BF16),
            jax.ShapeDtypeStruct((3, 2 * C1, 2 * C2), BF16),
            jax.ShapeDtypeStruct((2, C2, 2 * C1), BF16),
        ),
        in_specs=[SMEM, SMEM, VMEM, VMEM, VMEM, VMEM],
        out_specs=[SMEM] + [VMEM] * 5,
        compiler_params=pltpu.CompilerParams(vmem_limit_bytes=10 * 2**20),
        cost_estimate=pl.CostEstimate(flops=5 * 10**6, bytes_accessed=10**7, transcendentals=0),
        name="prepare",
    )(where, offsets, table, w_first, w_down, w_up)


def patch_work(places, side_a, middle, side_b, fb, rf, rft, wd, rdt, ru):
    return pl.pallas_call(
        net_kernel,
        out_shape=(
            jax.ShapeDtypeStruct((2, 32, 16, C1), F32),
            jax.ShapeDtypeStruct((2, 32, 16, C1), BF16),
            jax.ShapeDtypeStruct((HALF_ROWS, C1), BF16),
            jax.ShapeDtypeStruct((HALF_ROWS + 2 * 32 * 16, C1), BF16),
        ),
        in_specs=[SMEM] + [VMEM] * 9,
        out_specs=[VMEM] * 4,
        scratch_shapes=[
            pltpu.VMEM((32, 64, C1), F32),
            pltpu.VMEM((32, 64, C1), F32),
            pltpu.VMEM((2, 17, 16, 4 * C1), BF16),
            pltpu.VMEM((2, 17, 16, 3 * C1), BF16),
            pltpu.VMEM((2, 17, 16, 4 * C1), BF16),
            pltpu.VMEM((17, 16, 2 * C2), BF16),
            pltpu.VMEM((2, 16, 16, 2 * C1), F32),
            pltpu.VMEM((2, 16, 16, 2 * C1), F32),
            pltpu.VMEM((32, 48, C1), F32),
            pltpu.VMEM((32, 48, C1), F32),
            pltpu.VMEM((2, HALF_ROWS, C1), BF16),
        ],
        compiler_params=pltpu.CompilerParams(vmem_limit_bytes=24 * 2**20),
        cost_estimate=pl.CostEstimate(flops=2 * 10**9, bytes_accessed=10**7, transcendentals=200000),
        name="patch_work",
    )(places, side_b, middle, side_a, fb, rf, rft, wd, rdt, ru)


def small_call(body, name, outs, scratch, *args, smem=0):
    return pl.pallas_call(
        body,
        out_shape=tuple(jax.ShapeDtypeStruct(shape, kind) for shape, kind in outs),
        in_specs=[SMEM] * smem + [VMEM] * (len(args) - smem),
        out_specs=[VMEM] * len(outs),
        scratch_shapes=scratch,
        compiler_params=pltpu.CompilerParams(vmem_limit_bytes=10 * 2**20),
        cost_estimate=pl.CostEstimate(flops=10**6, bytes_accessed=2 * 10**6, transcendentals=0),
        name=name,
    )(*args)


def swapped_b(x, axes):
    size = lax.axis_size(axes)
    pairs = [(i, i + 1) for i in range(1, size - 1, 2)]
    return lax.ppermute(x, axes, pairs + [(j, i) for i, j in pairs])


def swapped_a(x, axis):
    return lax.ppermute(x, axis, [(0, 1), (1, 0)])


def added(x, y):
    return (x.astype(F32) + y.astype(F32)).astype(BF16)


def scattered(x, axes):
    size = lax.axis_size(axes)
    parts = x.reshape(size, x.shape[0] // size, x.shape[1])
    got = lax.all_to_all(parts, axes, 0, 0, tiled=True)
    return got.astype(F32).sum(0).astype(BF16)


def gathered(x, axes):
    size = lax.axis_size(axes)
    parts = jnp.broadcast_to(x[None], (size,) + x.shape)
    return lax.all_to_all(parts, axes, 0, 0, tiled=True)


def per_device(field, cotangent, w_first, w_down, w_up, offsets, blend_table):
    rows_n = lax.axis_size(ROW)
    cols_n = lax.axis_size(COL)
    row_at = lax.axis_index(ROW)
    col_at = lax.axis_index(COL)
    where = jnp.stack([row_at, col_at]).astype(jnp.int32)
    both = jnp.stack([field, cotangent])
    places, fb, rf, rft, rdt, ru = prepared(
        where, offsets.transpose(0, 2, 1), blend_table, w_first, w_down, w_up
    )
    row_a, row_b = swapped_a(both, "zh"), swapped_b(both, ROW)
    row_a, row_b, places, fb, rf, rft, rdt, ru = lax.optimization_barrier(
        (row_a, row_b, places, fb, rf, rft, rdt, ru)
    )
    window_shape = (2, 32, TILE, C1)
    to_a, own, to_b = small_call(
        assemble_kernel,
        "assemble",
        [(window_shape, BF16)] * 3,
        [pltpu.VMEM((2, 48, TILE, C1), BF16)],
        places,
        row_a,
        both,
        row_b,
        smem=1,
    )
    side_a, side_b = swapped_a(to_a, "core"), swapped_b(to_b, COL)
    own, strip_b, keep, send = patch_work(
        places, side_a, own, side_b, fb, rf, rft, w_down.reshape(3, 3 * C1, C2), rdt, ru
    )
    got = swapped_a(send, "core")
    from_b = swapped_b(strip_b, COL)
    part = added(keep, got[:HALF_ROWS])
    part = scattered(part, ("x", "y"))
    part, from_b = lax.optimization_barrier((part, from_b))
    part = gathered(part, ("zl", "zh")).astype(F32).sum(0).astype(BF16)
    tile_shape = (2, TILE, TILE, C1)
    to_a, own, to_b = small_call(
        add_kernel,
        "add",
        [(tile_shape, BF16), (tile_shape, F32), (tile_shape, BF16)],
        [pltpu.VMEM((2, 48, TILE, C1), F32)],
        places,
        got,
        own,
        from_b,
        smem=1,
    )
    part, own, to_a, to_b = lax.optimization_barrier((part, own, to_a, to_b))
    row_a, row_b = swapped_a(to_a, "zh"), swapped_b(to_b, ROW)
    part = gathered(part, ("x", "y")).reshape(-1, C1)
    part, row_b, own, row_a = lax.optimization_barrier((part, row_b, own, row_a))
    other = swapped_a(part, "core")
    blended, field_grad = small_call(
        finish_kernel,
        "finish",
        [(field.shape, BF16), (field.shape, F32)],
        [],
        own,
        row_a,
        row_b,
    )
    scale = 1.0 / math.sqrt(TILE * rows_n * TILE * cols_n)
    g_first, g_down, g_up = small_call(
        functools.partial(unpack_kernel, scale),
        "unpack",
        [((9, C1, C1), F32), ((3, 3 * C1, C2), F32), ((4, C2, C1), F32)],
        [],
        places,
        part,
        other,
        smem=1,
    )
    return (
        blended,
        field_grad,
        g_first.reshape(w_first.shape),
        g_down.reshape(w_down.shape),
        g_up.reshape(w_up.shape),
    )


def solution(mesh):
    fine = Mesh(mesh.devices.reshape(8, 4, 2, 4, 2), ("y", "zl", "core", "x", "zh"))
    tiles = P(ROW, COL, None)
    return jax.shard_map(
        per_device,
        mesh=fine,
        in_specs=(tiles, tiles, P(), P(), P(), P(), P()),
        out_specs=(tiles, tiles, P(), P(), P()),
        check_vma=False,
    )
```

```python
import functools
import math

import jax
import jax.numpy as jnp
from jax import lax
from jax.experimental import pallas as pl
from jax.experimental.pallas import tpu as pltpu
from jax.sharding import Mesh, PartitionSpec as P

MARGIN = 8
ROW = ("x", "zh")
COL = ("y", "zl", "core")
PLANE = ("x", "y")
DEPTH = ("zl", "zh")
F32 = jnp.float32
BF16 = jnp.bfloat16
REACH = 2
FAR = 1000
TILE = 16
C1 = 128
C2 = 256
FIRST_ROWS = 9 * C1
DOWN_ROWS = 18 * C1
UP_ROWS = 4 * C2
USED_ROWS = FIRST_ROWS + DOWN_ROWS + UP_ROWS
HALF_ROWS = 2304


def dot(a, b):
    return lax.dot_general(a, b, (((1,), (0,)), ((), ())), preferred_element_type=F32)


def dot_nt(a, b):
    return lax.dot_general(a, b, (((1,), (1,)), ((), ())), preferred_element_type=F32)


def prepare_kernel(
    where, offsets, table, w_first, w_down, w_up,
    places, fb, rf, rft, rdt, ru,
):
    row_at, col_at = where[0], where[1]
    rows_n, cols_n = offsets.shape[0], offsets.shape[2]
    core, zh = lax.rem(col_at, 2), lax.rem(row_at, 2)
    col_b = jnp.clip(col_at - 1 + 2 * core, 0, cols_n - 1)
    for k, col in enumerate((col_at + 1 - 2 * core, col_at, col_b)):
        places[k] = MARGIN + offsets[row_at, 0, col]
    places[3] = 32 * (1 - zh)
    places[4] = 32 * zh
    places[5] = MARGIN + offsets[row_at, 1, col_at]
    places[6] = core
    places[7] = 0
    sub = lax.broadcasted_iota(jnp.int32, (32, 32), 0)
    lane = lax.broadcasted_iota(jnp.int32, (32, 32), 1)
    column = jnp.where(sub < 16, 2 * sub, 2 * (sub - 16) + 1)
    table_t = table[...].astype(F32).T.astype(BF16)
    own_r = offsets[row_at, 0, col_at]
    own_c = offsets[row_at, 1, col_at]
    total = jnp.zeros((32, 32), F32)
    own = jnp.zeros((32, 32), F32)
    for row_step in range(-REACH, REACH + 1):
        for col_step in range(-REACH, REACH + 1):
            near_r, near_c = row_at + row_step, col_at + col_step
            inside = (near_r >= 0) & (near_r < rows_n) & (near_c >= 0) & (near_c < cols_n)
            at_r = jnp.clip(near_r, 0, rows_n - 1)
            at_c = jnp.clip(near_c, 0, cols_n - 1)
            down_by = row_step * TILE + offsets[at_r, 0, at_c] - own_r
            right_by = col_step * TILE + offsets[at_r, 1, at_c] - own_c
            down_by = jnp.where(inside, down_by, FAR)
            pick_c = (column - right_by == lane).astype(F32).astype(BF16)
            pick_r = (lane - down_by == sub).astype(F32).astype(BF16)
            placed = dot(pick_c, table_t)
            if row_step == 0 and col_step == 0:
                own = placed
            total = total + dot(placed.astype(BF16), pick_r)
    share = own / total
    for r in range(32):
        fb[r % 2, r // 2, :, :C1] = jnp.broadcast_to(share[:16, r : r + 1], (16, C1))
        fb[r % 2, r // 2, :, C1:] = jnp.broadcast_to(share[16:, r : r + 1], (16, C1))
    none = jnp.zeros((C1, C1), BF16)
    for t in range(3):
        for v in range(4):
            for b in range(2):
                rows, cols = pl.ds(v * C1, C1), pl.ds(b * C1, C1)
                held = 0 <= v - b <= 2
                rf[t, rows, cols] = w_first[t, v - b] if held else none
                rft[t, cols, rows] = w_first[2 - t, 2 - v + b] if held else none
        rdt[t, :C1, :C2] = w_down[t, 1]
        rdt[t, :C1, C2:] = jnp.zeros((C1, C2), BF16)
        rdt[t, C1:, :C2] = w_down[t, 2]
        rdt[t, C1:, C2:] = w_down[t, 0]
    for a in range(2):
        for b in range(2):
            ru[a, :, pl.ds(b * C1, C1)] = w_up[a, b]


def assemble_kernel(places, from_a, both, from_b, to_a, own, to_b, grown):
    grown[:, pl.ds(places[3], 16)] = from_a[...]
    grown[:, 16:32] = both[...]
    grown[:, pl.ds(places[4], 16)] = from_b[...]
    for side, out in enumerate((to_a, own, to_b)):
        out[...] = grown[:, pl.ds(places[side], 32)]


def add_kernel(places, from_a, own, from_b, to_a, mid, to_b, canvas):
    canvas[...] = jnp.zeros_like(canvas)
    canvas[:, pl.ds(places[1], 32)] = own[...]
    for side, strip in ((0, from_a[HALF_ROWS:].reshape(2, 32, 16, C1)), (2, from_b[...])):
        spot = (slice(None), pl.ds(places[side], 32))
        canvas[spot] = canvas[spot] + strip.astype(F32)
    to_a[...] = canvas[:, pl.ds(places[3], 16)].astype(BF16)
    mid[...] = canvas[:, 16:32]
    to_b[...] = canvas[:, pl.ds(places[4], 16)].astype(BF16)


def finish_kernel(own, from_a, from_b, blended, field_grad):
    total = own[...] + from_a[...].astype(F32) + from_b[...].astype(F32)
    blended[...] = total[0].astype(BF16)
    field_grad[...] = total[1]


def sum_kernel(parts, copies):
    total = parts[0].astype(F32)
    for k in range(1, parts.shape[0]):
        total = total + parts[k].astype(F32)
    total = total.astype(BF16)
    for k in range(copies.shape[0]):
        copies[k] = total


def unpack_kernel(scale, core, own, other, g_first, g_down, g_up):
    def write(parts):
        def rows(base, count):
            at = base % HALF_ROWS
            return parts[base // HALF_ROWS][at : at + count].astype(F32) * scale

        for t in range(9):
            g_first[t] = rows(t * C1, C1)
        for t in range(3):
            base = FIRST_ROWS + 6 * t * C1
            g_down[t, :, :C1] = rows(base, 3 * C1)
            g_down[t, :, C1:] = rows(base + 3 * C1, 3 * C1)
        for t in range(4):
            g_up[t] = rows(FIRST_ROWS + DOWN_ROWS + t * C2, C2)

    pl.when(core[0] == 0)(lambda: write((own, other)))
    pl.when(core[0] == 1)(lambda: write((other, own)))


def shifted(x, by):
    j = lax.broadcasted_iota(jnp.int32, x.shape, 0) % 16
    moved = pltpu.roll(x, by % x.shape[0], 0)
    return jnp.where(j == (0 if by > 0 else 15), 0.0, moved)


def spread(x):
    return jnp.concatenate(
        [shifted(x[:, C1:], 1).astype(BF16), x.astype(BF16), shifted(x[:, :C1], -1).astype(BF16)], axis=1
    )


def window(ref, a, t):
    part = ref[(a + t) % 2, (a + t) // 2 : (a + t) // 2 + 16]
    return part.reshape(256, part.shape[-1])


def net_kernel(
    places, side_b, middle, side_a, fb, rf, rft, wd, rdt, ru,
    mid_o, strip_b, keep, send,
    fs, cs, xv, hv, gv, g4, gs, bs, can_b, can_g, halves,
):
    start_c, core = places[5], places[6]
    at_a, at_b = 32 * (1 - core), 32 * core

    def put(base, value):
        half, at = base // HALF_ROWS, base % HALF_ROWS
        halves[core if half == 0 else 1 - core, at : at + value.shape[0]] = value.astype(BF16)

    for ref in (xv, hv, gv):
        edge = jnp.zeros((16, ref.shape[-1]), BF16)
        ref[0, 0] = edge
        ref[1, 16] = edge
    g4[16] = jnp.zeros((16, 2 * C2), BF16)

    def stage(r, carry):
        for at, ref in ((at_a, side_a), (16, middle), (at_b, side_b)):
            spot = pl.ds(pl.multiple_of(at + 8, 8), 16)
            fs[r, spot, :] = ref[0, r].astype(F32)
            cs[r, spot, :] = ref[1, r].astype(F32)
        return carry

    lax.fori_loop(0, 32, stage, 0, unroll=4)
    j = lax.broadcasted_iota(jnp.int32, (16, C1), 0)

    def load(i, carry):
        for a in range(2):
            r = 2 * i + a
            at = start_c + 8
            before = jnp.where(j == 0, 0.0, fs[r, pl.ds(at - 1, 16, 2), :])
            even = fs[r, pl.ds(at, 16, 2), :]
            odd = fs[r, pl.ds(at + 1, 16, 2), :]
            after = jnp.where(j == 15, 0.0, fs[r, pl.ds(at + 2, 16, 2), :])
            xv[1 - a, i + a] = jnp.concatenate([before, even, odd, after], axis=1).astype(BF16)
            gs[a, i, :, :C1] = cs[r, pl.ds(at, 16, 2), :] * fb[a, i, :, :C1]
            gs[a, i, :, C1:] = cs[r, pl.ds(at + 1, 16, 2), :] * fb[a, i, :, C1:]
        return carry

    lax.fori_loop(0, 16, load, 0, unroll=2)

    h, slope_h = [], []
    for a in range(2):
        pre = dot(window(xv, a, 0), rf[0]) + dot(window(xv, a, 1), rf[1]) + dot(window(xv, a, 2), rf[2])
        sig = lax.logistic(pre)
        value = pre * sig
        slope_h.append(sig + value * (1.0 - sig))
        h.append(value.astype(BF16))
        hv[1 - a, a : a + 16] = jnp.concatenate(
            [shifted(value[:, C1:], 1).astype(BF16), h[a]], axis=1
        ).reshape(16, 16, 3 * C1)
    pre = dot(window(hv, 0, 0), wd[0]) + dot(window(hv, 0, 1), wd[1]) + dot(window(hv, 0, 2), wd[2])
    sig = lax.logistic(pre)
    value = pre * sig
    slope_d = sig + value * (1.0 - sig)
    d = value.astype(BF16)
    d_t = value.T.astype(BF16)
    g_d = jnp.zeros((256, C2), F32)
    for a in range(2):
        out = h[a].astype(F32) + dot(d, ru[a])
        bs[a] = (fb[a].reshape(256, 2 * C1) * out).reshape(16, 16, 2 * C1)
        g = gs[a].reshape(256, 2 * C1).astype(BF16)
        g_d = g_d + dot_nt(g, ru[a])
        g_up = dot(d_t, g)
        base = FIRST_ROWS + DOWN_ROWS + 2 * a * C2
        put(base, g_up[:, :C1])
        put(base + C2, g_up[:, C1:])
    g_pre = g_d.astype(BF16).astype(F32) * slope_d
    g4[0:16] = jnp.concatenate([g_pre.astype(BF16), shifted(g_pre, -1).astype(BF16)], axis=1).reshape(
        16, 16, 2 * C2
    )
    g_pre_t = g_pre.T.astype(BF16)
    for t in range(3):
        g_down = dot(g_pre_t, window(hv, 0, t)).T
        base = FIRST_ROWS + 6 * t * C1
        put(base, g_down[:, :C1])
        put(base + 3 * C1, g_down[:, C1:])
    here = g4[0:16].reshape(256, 2 * C2)
    below = g4[1:17].reshape(256, 2 * C2)
    g_h = [dot_nt(here, rdt[1]), dot_nt(here, rdt[2]) + dot_nt(below, rdt[0])]
    g_t = []
    for a in range(2):
        g_pre = (gs[a].reshape(256, 2 * C1) + g_h[a]) * slope_h[a]
        gv[1 - a, a : a + 16] = spread(g_pre).reshape(16, 16, 4 * C1)
        g_t.append(g_pre.T.astype(BF16))
    for t in range(3):
        g_first = dot(g_t[0], window(xv, 0, t)) + dot(g_t[1], window(xv, 1, t))
        for ct in range(3):
            block = (
                g_first[:C1, ct * C1 : (ct + 1) * C1] + g_first[C1:, (ct + 1) * C1 : (ct + 2) * C1]
            )
            put((3 * t + ct) * C1, block.T)
    put(USED_ROWS, jnp.zeros((2 * HALF_ROWS - USED_ROWS, C1), F32))
    keep[...] = halves[0]
    send[:HALF_ROWS] = halves[1]
    for a in range(2):
        g_x = (
            dot_nt(window(gv, a, 0), rft[0])
            + dot_nt(window(gv, a, 1), rft[1])
            + dot_nt(window(gv, a, 2), rft[2])
        )
        gs[a] = g_x.reshape(16, 16, 2 * C1)

    def clear(r, carry):
        can_b[r] = jnp.zeros((48, C1), F32)
        can_g[r] = jnp.zeros((48, C1), F32)
        return carry

    lax.fori_loop(0, 32, clear, 0, unroll=4)

    def place(i, carry):
        for a in range(2):
            r = 2 * i + a
            for b in range(2):
                can_b[r, pl.ds(start_c + b, 16, 2), :] = bs[a, i, :, b * C1 : (b + 1) * C1]
                can_g[r, pl.ds(start_c + b, 16, 2), :] = gs[a, i, :, b * C1 : (b + 1) * C1]
        return carry

    lax.fori_loop(0, 16, place, 0, unroll=2)

    def give(r, carry):
        for k, canvas in enumerate((can_b, can_g)):
            mid_o[k, r] = canvas[r, 16:32]
            strip = canvas[r, pl.ds(pl.multiple_of(at_a, 16), 16), :].astype(BF16)
            send[pl.ds(pl.multiple_of(HALF_ROWS + (32 * k + r) * 16, 16), 16)] = strip
            strip_b[k, r] = canvas[r, pl.ds(pl.multiple_of(at_b, 16), 16), :].astype(BF16)
        return carry

    lax.fori_loop(0, 32, give, 0, unroll=2)


VMEM = pl.BlockSpec(memory_space=pltpu.VMEM)
SMEM = pl.BlockSpec(memory_space=pltpu.SMEM)


def prepared(where, offsets, table, w_first, w_down, w_up):
    return pl.pallas_call(
        prepare_kernel,
        out_shape=(
            jax.ShapeDtypeStruct((8,), jnp.int32),
            jax.ShapeDtypeStruct((2, 16, 16, 2 * C1), F32),
            jax.ShapeDtypeStruct((3, 4 * C1, 2 * C1), BF16),
            jax.ShapeDtypeStruct((3, 2 * C1, 4 * C1), BF16),
            jax.ShapeDtypeStruct((3, 2 * C1, 2 * C2), BF16),
            jax.ShapeDtypeStruct((2, C2, 2 * C1), BF16),
        ),
        in_specs=[SMEM, SMEM, VMEM, VMEM, VMEM, VMEM],
        out_specs=[SMEM] + [VMEM] * 5,
        compiler_params=pltpu.CompilerParams(vmem_limit_bytes=10 * 2**20),
        cost_estimate=pl.CostEstimate(flops=5 * 10**6, bytes_accessed=10**7, transcendentals=0),
        name="prepare",
    )(where, offsets, table, w_first, w_down, w_up)


def patch_work(places, side_a, middle, side_b, fb, rf, rft, wd, rdt, ru):
    return pl.pallas_call(
        net_kernel,
        out_shape=(
            jax.ShapeDtypeStruct((2, 32, 16, C1), F32),
            jax.ShapeDtypeStruct((2, 32, 16, C1), BF16),
            jax.ShapeDtypeStruct((HALF_ROWS, C1), BF16),
            jax.ShapeDtypeStruct((HALF_ROWS + 2 * 32 * 16, C1), BF16),
        ),
        in_specs=[SMEM] + [VMEM] * 9,
        out_specs=[VMEM] * 4,
        scratch_shapes=[
            pltpu.VMEM((32, 64, C1), F32),
            pltpu.VMEM((32, 64, C1), F32),
            pltpu.VMEM((2, 17, 16, 4 * C1), BF16),
            pltpu.VMEM((2, 17, 16, 3 * C1), BF16),
            pltpu.VMEM((2, 17, 16, 4 * C1), BF16),
            pltpu.VMEM((17, 16, 2 * C2), BF16),
            pltpu.VMEM((2, 16, 16, 2 * C1), F32),
            pltpu.VMEM((2, 16, 16, 2 * C1), F32),
            pltpu.VMEM((32, 48, C1), F32),
            pltpu.VMEM((32, 48, C1), F32),
            pltpu.VMEM((2, HALF_ROWS, C1), BF16),
        ],
        compiler_params=pltpu.CompilerParams(vmem_limit_bytes=24 * 2**20),
        cost_estimate=pl.CostEstimate(flops=2 * 10**9, bytes_accessed=10**7, transcendentals=200000),
        name="patch_work",
    )(places, side_b, middle, side_a, fb, rf, rft, wd, rdt, ru)


def small_call(body, name, outs, scratch, *args, smem=0):
    return pl.pallas_call(
        body,
        out_shape=tuple(jax.ShapeDtypeStruct(shape, kind) for shape, kind in outs),
        in_specs=[SMEM] * smem + [VMEM] * (len(args) - smem),
        out_specs=[VMEM] * len(outs),
        scratch_shapes=scratch,
        compiler_params=pltpu.CompilerParams(vmem_limit_bytes=10 * 2**20),
        cost_estimate=pl.CostEstimate(flops=10**6, bytes_accessed=2 * 10**6, transcendentals=0),
        name=name,
    )(*args)


def swapped_b(x, axes):
    size = lax.axis_size(axes)
    pairs = [(i, i + 1) for i in range(1, size - 1, 2)]
    return lax.ppermute(x, axes, pairs + [(j, i) for i, j in pairs])


def swapped_a(x, axis):
    return lax.ppermute(x, axis, [(0, 1), (1, 0)])


def added(x, y):
    return (x.astype(F32) + y.astype(F32)).astype(BF16)


def exchanged(parts, axes):
    return lax.all_to_all(parts, axes, 0, 0, tiled=True)


def summed_for(axes, parts):
    shape = (lax.axis_size(axes),) + parts.shape[1:]
    return small_call(sum_kernel, "sum", [(shape, BF16)], [], parts)[0]


def per_device(field, cotangent, w_first, w_down, w_up, offsets, blend_table):
    rows_n = lax.axis_size(ROW)
    cols_n = lax.axis_size(COL)
    row_at = lax.axis_index(ROW)
    col_at = lax.axis_index(COL)
    where = jnp.stack([row_at, col_at]).astype(jnp.int32)
    both = jnp.stack([field, cotangent])
    places, fb, rf, rft, rdt, ru = prepared(
        where, offsets.transpose(0, 2, 1), blend_table, w_first, w_down, w_up
    )
    row_a, row_b = swapped_a(both, "zh"), swapped_b(both, ROW)
    row_a, row_b, places, fb, rf, rft, rdt, ru = lax.optimization_barrier(
        (row_a, row_b, places, fb, rf, rft, rdt, ru)
    )
    window_shape = (2, 32, TILE, C1)
    to_a, own, to_b = small_call(
        assemble_kernel,
        "assemble",
        [(window_shape, BF16)] * 3,
        [pltpu.VMEM((2, 48, TILE, C1), BF16)],
        places,
        row_a,
        both,
        row_b,
        smem=1,
    )
    side_a, side_b = swapped_a(to_a, "core"), swapped_b(to_b, COL)
    own, strip_b, keep, send = patch_work(
        places, side_a, own, side_b, fb, rf, rft, w_down.reshape(3, 3 * C1, C2), rdt, ru
    )
    got = swapped_a(send, "core")
    from_b = swapped_b(strip_b, COL)
    part = added(keep, got[:HALF_ROWS])
    part = exchanged(part.reshape(lax.axis_size(PLANE), -1, C1), PLANE)
    part = summed_for(DEPTH, part)
    part, from_b = lax.optimization_barrier((part, from_b))
    part = summed_for(PLANE, exchanged(part, DEPTH))
    tile_shape = (2, TILE, TILE, C1)
    to_a, own, to_b = small_call(
        add_kernel,
        "add",
        [(tile_shape, BF16), (tile_shape, F32), (tile_shape, BF16)],
        [pltpu.VMEM((2, 48, TILE, C1), F32)],
        places,
        got,
        own,
        from_b,
        smem=1,
    )
    part, own, to_a, to_b = lax.optimization_barrier((part, own, to_a, to_b))
    row_a, row_b = swapped_a(to_a, "zh"), swapped_b(to_b, ROW)
    part = exchanged(part, PLANE).reshape(-1, C1)
    part, row_b, own, row_a = lax.optimization_barrier((part, row_b, own, row_a))
    other = swapped_a(part, "core")
    blended, field_grad = small_call(
        finish_kernel,
        "finish",
        [(field.shape, BF16), (field.shape, F32)],
        [],
        own,
        row_a,
        row_b,
    )
    scale = 1.0 / math.sqrt(TILE * rows_n * TILE * cols_n)
    g_first, g_down, g_up = small_call(
        functools.partial(unpack_kernel, scale),
        "unpack",
        [((9, C1, C1), F32), ((3, 3 * C1, C2), F32), ((4, C2, C1), F32)],
        [],
        lax.axis_index("core").astype(jnp.int32)[None],
        part,
        other,
        smem=1,
    )
    return (
        blended,
        field_grad,
        g_first.reshape(w_first.shape),
        g_down.reshape(w_down.shape),
        g_up.reshape(w_up.shape),
    )


def solution(mesh):
    fine = Mesh(mesh.devices.reshape(8, 4, 2, 4, 2), ("y", "zl", "core", "x", "zh"))
    tiles = P(ROW, COL, None)
    return jax.shard_map(
        per_device,
        mesh=fine,
        in_specs=(tiles, tiles, P(), P(), P(), P(), P()),
        out_specs=(tiles, tiles, P(), P(), P()),
        check_vma=False,
    )
```

```python
import functools
import math

import jax
import jax.numpy as jnp
from jax import lax
from jax.experimental import pallas as pl
from jax.experimental.pallas import tpu as pltpu
from jax.sharding import Mesh, PartitionSpec as P

MARGIN = 8
ROW = ("x", "zh")
COL = ("y", "zl", "core")
PLANE = ("y", "x")
DEPTH = ("zl", "zh")
F32 = jnp.float32
BF16 = jnp.bfloat16
REACH = 2
FAR = 1000
TILE = 16
C1 = 128
C2 = 256
FIRST_ROWS = 9 * C1
DOWN_ROWS = 18 * C1
UP_ROWS = 4 * C2
USED_ROWS = FIRST_ROWS + DOWN_ROWS + UP_ROWS
HALF_ROWS = 2304


def dot(a, b):
    return lax.dot_general(a, b, (((1,), (0,)), ((), ())), preferred_element_type=F32)


def dot_nt(a, b):
    return lax.dot_general(a, b, (((1,), (1,)), ((), ())), preferred_element_type=F32)


def prepare_kernel(
    where, offsets, table, w_first, w_down, w_up,
    places, fb, rf, rft, rdt, ru,
):
    row_at, col_at = where[0], where[1]
    rows_n, cols_n = offsets.shape[0], offsets.shape[2]
    core, zh = lax.rem(col_at, 2), lax.rem(row_at, 2)
    col_b = jnp.clip(col_at - 1 + 2 * core, 0, cols_n - 1)
    for k, col in enumerate((col_at + 1 - 2 * core, col_at, col_b)):
        places[k] = MARGIN + offsets[row_at, 0, col]
    places[3] = 32 * (1 - zh)
    places[4] = 32 * zh
    places[5] = MARGIN + offsets[row_at, 1, col_at]
    places[6] = core
    places[7] = 0
    sub = lax.broadcasted_iota(jnp.int32, (32, 32), 0)
    lane = lax.broadcasted_iota(jnp.int32, (32, 32), 1)
    column = jnp.where(sub < 16, 2 * sub, 2 * (sub - 16) + 1)
    table_t = table[...].astype(F32).T.astype(BF16)
    own_r = offsets[row_at, 0, col_at]
    own_c = offsets[row_at, 1, col_at]
    total = jnp.zeros((32, 32), F32)
    own = jnp.zeros((32, 32), F32)
    for row_step in range(-REACH, REACH + 1):
        for col_step in range(-REACH, REACH + 1):
            near_r, near_c = row_at + row_step, col_at + col_step
            inside = (near_r >= 0) & (near_r < rows_n) & (near_c >= 0) & (near_c < cols_n)
            at_r = jnp.clip(near_r, 0, rows_n - 1)
            at_c = jnp.clip(near_c, 0, cols_n - 1)
            down_by = row_step * TILE + offsets[at_r, 0, at_c] - own_r
            right_by = col_step * TILE + offsets[at_r, 1, at_c] - own_c
            down_by = jnp.where(inside, down_by, FAR)
            pick_c = (column - right_by == lane).astype(F32).astype(BF16)
            pick_r = (lane - down_by == sub).astype(F32).astype(BF16)
            placed = dot(pick_c, table_t)
            if row_step == 0 and col_step == 0:
                own = placed
            total = total + dot(placed.astype(BF16), pick_r)
    share = own / total
    for r in range(32):
        fb[r % 2, r // 2, :, :C1] = jnp.broadcast_to(share[:16, r : r + 1], (16, C1))
        fb[r % 2, r // 2, :, C1:] = jnp.broadcast_to(share[16:, r : r + 1], (16, C1))
    none = jnp.zeros((C1, C1), BF16)
    for t in range(3):
        for v in range(4):
            for b in range(2):
                rows, cols = pl.ds(v * C1, C1), pl.ds(b * C1, C1)
                held = 0 <= v - b <= 2
                rf[t, rows, cols] = w_first[t, v - b] if held else none
                rft[t, cols, rows] = w_first[2 - t, 2 - v + b] if held else none
        rdt[t, :C1, :C2] = w_down[t, 1]
        rdt[t, :C1, C2:] = jnp.zeros((C1, C2), BF16)
        rdt[t, C1:, :C2] = w_down[t, 2]
        rdt[t, C1:, C2:] = w_down[t, 0]
    for a in range(2):
        for b in range(2):
            ru[a, :, pl.ds(b * C1, C1)] = w_up[a, b]


def assemble_kernel(places, from_a, both, from_b, to_a, own, to_b, grown):
    grown[:, pl.ds(places[3], 16)] = from_a[...]
    grown[:, 16:32] = both[...]
    grown[:, pl.ds(places[4], 16)] = from_b[...]
    for side, out in enumerate((to_a, own, to_b)):
        out[...] = grown[:, pl.ds(places[side], 32)]


def add_kernel(places, from_a, own, from_b, to_a, mid, to_b, canvas):
    canvas[...] = jnp.zeros_like(canvas)
    canvas[:, pl.ds(places[1], 32)] = own[...]
    for side, strip in ((0, from_a[HALF_ROWS:].reshape(2, 32, 16, C1)), (2, from_b[...])):
        spot = (slice(None), pl.ds(places[side], 32))
        canvas[spot] = canvas[spot] + strip.astype(F32)
    to_a[...] = canvas[:, pl.ds(places[3], 16)].astype(BF16)
    mid[...] = canvas[:, 16:32]
    to_b[...] = canvas[:, pl.ds(places[4], 16)].astype(BF16)


def finish_kernel(own, from_a, from_b, blended, field_grad):
    total = own[...] + from_a[...].astype(F32) + from_b[...].astype(F32)
    blended[...] = total[0].astype(BF16)
    field_grad[...] = total[1]


def sum_kernel(parts, copies):
    total = parts[0].astype(F32)
    for k in range(1, parts.shape[0]):
        total = total + parts[k].astype(F32)
    total = total.astype(BF16)
    for k in range(copies.shape[0]):
        copies[k] = total


def unpack_kernel(scale, core, own, other, g_first, g_down, g_up):
    def write(parts):
        def rows(base, count):
            at = base % HALF_ROWS
            return parts[base // HALF_ROWS][at : at + count].astype(F32) * scale

        for t in range(9):
            g_first[t] = rows(t * C1, C1)
        for t in range(3):
            base = FIRST_ROWS + 6 * t * C1
            g_down[t, :, :C1] = rows(base, 3 * C1)
            g_down[t, :, C1:] = rows(base + 3 * C1, 3 * C1)
        for t in range(4):
            g_up[t] = rows(FIRST_ROWS + DOWN_ROWS + t * C2, C2)

    pl.when(core[0] == 0)(lambda: write((own, other)))
    pl.when(core[0] == 1)(lambda: write((other, own)))


def shifted(x, by):
    j = lax.broadcasted_iota(jnp.int32, x.shape, 0) % 16
    moved = pltpu.roll(x, by % x.shape[0], 0)
    return jnp.where(j == (0 if by > 0 else 15), 0.0, moved)


def spread(x):
    return jnp.concatenate(
        [shifted(x[:, C1:], 1).astype(BF16), x.astype(BF16), shifted(x[:, :C1], -1).astype(BF16)], axis=1
    )


def window(ref, a, t):
    part = ref[(a + t) % 2, (a + t) // 2 : (a + t) // 2 + 16]
    return part.reshape(256, part.shape[-1])


def net_kernel(
    places, side_b, middle, side_a, fb, rf, rft, wd, rdt, ru,
    mid_o, strip_b, keep, send,
    fs, cs, xv, hv, gv, g4, gs, bs, can_b, can_g, halves,
):
    start_c, core = places[5], places[6]
    at_a, at_b = 32 * (1 - core), 32 * core

    def put(base, value):
        half, at = base // HALF_ROWS, base % HALF_ROWS
        halves[core if half == 0 else 1 - core, at : at + value.shape[0]] = value.astype(BF16)

    for ref in (xv, hv, gv):
        edge = jnp.zeros((16, ref.shape[-1]), BF16)
        ref[0, 0] = edge
        ref[1, 16] = edge
    g4[16] = jnp.zeros((16, 2 * C2), BF16)

    def stage(r, carry):
        for at, ref in ((at_a, side_a), (16, middle), (at_b, side_b)):
            spot = pl.ds(pl.multiple_of(at + 8, 8), 16)
            fs[r, spot, :] = ref[0, r].astype(F32)
            cs[r, spot, :] = ref[1, r].astype(F32)
        return carry

    lax.fori_loop(0, 32, stage, 0, unroll=4)
    j = lax.broadcasted_iota(jnp.int32, (16, C1), 0)

    def load(i, carry):
        for a in range(2):
            r = 2 * i + a
            at = start_c + 8
            before = jnp.where(j == 0, 0.0, fs[r, pl.ds(at - 1, 16, 2), :])
            even = fs[r, pl.ds(at, 16, 2), :]
            odd = fs[r, pl.ds(at + 1, 16, 2), :]
            after = jnp.where(j == 15, 0.0, fs[r, pl.ds(at + 2, 16, 2), :])
            xv[1 - a, i + a] = jnp.concatenate([before, even, odd, after], axis=1).astype(BF16)
            gs[a, i, :, :C1] = cs[r, pl.ds(at, 16, 2), :] * fb[a, i, :, :C1]
            gs[a, i, :, C1:] = cs[r, pl.ds(at + 1, 16, 2), :] * fb[a, i, :, C1:]
        return carry

    lax.fori_loop(0, 16, load, 0, unroll=2)

    h, slope_h = [], []
    for a in range(2):
        pre = dot(window(xv, a, 0), rf[0]) + dot(window(xv, a, 1), rf[1]) + dot(window(xv, a, 2), rf[2])
        sig = lax.logistic(pre)
        value = pre * sig
        slope_h.append(sig + value * (1.0 - sig))
        h.append(value.astype(BF16))
        hv[1 - a, a : a + 16] = jnp.concatenate(
            [shifted(value[:, C1:], 1).astype(BF16), h[a]], axis=1
        ).reshape(16, 16, 3 * C1)
    pre = dot(window(hv, 0, 0), wd[0]) + dot(window(hv, 0, 1), wd[1]) + dot(window(hv, 0, 2), wd[2])
    sig = lax.logistic(pre)
    value = pre * sig
    slope_d = sig + value * (1.0 - sig)
    d = value.astype(BF16)
    d_t = value.T.astype(BF16)
    g_d = jnp.zeros((256, C2), F32)
    for a in range(2):
        out = h[a].astype(F32) + dot(d, ru[a])
        bs[a] = (fb[a].reshape(256, 2 * C1) * out).reshape(16, 16, 2 * C1)
        g = gs[a].reshape(256, 2 * C1).astype(BF16)
        g_d = g_d + dot_nt(g, ru[a])
        g_up = dot(d_t, g)
        base = FIRST_ROWS + DOWN_ROWS + 2 * a * C2
        put(base, g_up[:, :C1])
        put(base + C2, g_up[:, C1:])
    g_pre = g_d.astype(BF16).astype(F32) * slope_d
    g4[0:16] = jnp.concatenate([g_pre.astype(BF16), shifted(g_pre, -1).astype(BF16)], axis=1).reshape(
        16, 16, 2 * C2
    )
    g_pre_t = g_pre.T.astype(BF16)
    for t in range(3):
        g_down = dot(g_pre_t, window(hv, 0, t)).T
        base = FIRST_ROWS + 6 * t * C1
        put(base, g_down[:, :C1])
        put(base + 3 * C1, g_down[:, C1:])
    here = g4[0:16].reshape(256, 2 * C2)
    below = g4[1:17].reshape(256, 2 * C2)
    g_h = [dot_nt(here, rdt[1]), dot_nt(here, rdt[2]) + dot_nt(below, rdt[0])]
    g_t = []
    for a in range(2):
        g_pre = (gs[a].reshape(256, 2 * C1) + g_h[a]) * slope_h[a]
        gv[1 - a, a : a + 16] = spread(g_pre).reshape(16, 16, 4 * C1)
        g_t.append(g_pre.T.astype(BF16))
    for t in range(3):
        g_first = dot(g_t[0], window(xv, 0, t)) + dot(g_t[1], window(xv, 1, t))
        for ct in range(3):
            block = (
                g_first[:C1, ct * C1 : (ct + 1) * C1] + g_first[C1:, (ct + 1) * C1 : (ct + 2) * C1]
            )
            put((3 * t + ct) * C1, block.T)
    put(USED_ROWS, jnp.zeros((2 * HALF_ROWS - USED_ROWS, C1), F32))
    keep[...] = halves[0]
    send[:HALF_ROWS] = halves[1]
    for a in range(2):
        g_x = (
            dot_nt(window(gv, a, 0), rft[0])
            + dot_nt(window(gv, a, 1), rft[1])
            + dot_nt(window(gv, a, 2), rft[2])
        )
        gs[a] = g_x.reshape(16, 16, 2 * C1)

    def clear(r, carry):
        can_b[r] = jnp.zeros((48, C1), F32)
        can_g[r] = jnp.zeros((48, C1), F32)
        return carry

    lax.fori_loop(0, 32, clear, 0, unroll=4)

    def place(i, carry):
        for a in range(2):
            r = 2 * i + a
            for b in range(2):
                can_b[r, pl.ds(start_c + b, 16, 2), :] = bs[a, i, :, b * C1 : (b + 1) * C1]
                can_g[r, pl.ds(start_c + b, 16, 2), :] = gs[a, i, :, b * C1 : (b + 1) * C1]
        return carry

    lax.fori_loop(0, 16, place, 0, unroll=2)

    def give(r, carry):
        for k, canvas in enumerate((can_b, can_g)):
            mid_o[k, r] = canvas[r, 16:32]
            strip = canvas[r, pl.ds(pl.multiple_of(at_a, 16), 16), :].astype(BF16)
            send[pl.ds(pl.multiple_of(HALF_ROWS + (32 * k + r) * 16, 16), 16)] = strip
            strip_b[k, r] = canvas[r, pl.ds(pl.multiple_of(at_b, 16), 16), :].astype(BF16)
        return carry

    lax.fori_loop(0, 32, give, 0, unroll=2)


VMEM = pl.BlockSpec(memory_space=pltpu.VMEM)
SMEM = pl.BlockSpec(memory_space=pltpu.SMEM)


def prepared(where, offsets, table, w_first, w_down, w_up):
    return pl.pallas_call(
        prepare_kernel,
        out_shape=(
            jax.ShapeDtypeStruct((8,), jnp.int32),
            jax.ShapeDtypeStruct((2, 16, 16, 2 * C1), F32),
            jax.ShapeDtypeStruct((3, 4 * C1, 2 * C1), BF16),
            jax.ShapeDtypeStruct((3, 2 * C1, 4 * C1), BF16),
            jax.ShapeDtypeStruct((3, 2 * C1, 2 * C2), BF16),
            jax.ShapeDtypeStruct((2, C2, 2 * C1), BF16),
        ),
        in_specs=[SMEM, SMEM, VMEM, VMEM, VMEM, VMEM],
        out_specs=[SMEM] + [VMEM] * 5,
        compiler_params=pltpu.CompilerParams(vmem_limit_bytes=10 * 2**20),
        cost_estimate=pl.CostEstimate(flops=5 * 10**6, bytes_accessed=10**7, transcendentals=0),
        name="prepare",
    )(where, offsets, table, w_first, w_down, w_up)


def patch_work(places, side_a, middle, side_b, fb, rf, rft, wd, rdt, ru):
    return pl.pallas_call(
        net_kernel,
        out_shape=(
            jax.ShapeDtypeStruct((2, 32, 16, C1), F32),
            jax.ShapeDtypeStruct((2, 32, 16, C1), BF16),
            jax.ShapeDtypeStruct((HALF_ROWS, C1), BF16),
            jax.ShapeDtypeStruct((HALF_ROWS + 2 * 32 * 16, C1), BF16),
        ),
        in_specs=[SMEM] + [VMEM] * 9,
        out_specs=[VMEM] * 4,
        scratch_shapes=[
            pltpu.VMEM((32, 64, C1), F32),
            pltpu.VMEM((32, 64, C1), F32),
            pltpu.VMEM((2, 17, 16, 4 * C1), BF16),
            pltpu.VMEM((2, 17, 16, 3 * C1), BF16),
            pltpu.VMEM((2, 17, 16, 4 * C1), BF16),
            pltpu.VMEM((17, 16, 2 * C2), BF16),
            pltpu.VMEM((2, 16, 16, 2 * C1), F32),
            pltpu.VMEM((2, 16, 16, 2 * C1), F32),
            pltpu.VMEM((32, 48, C1), F32),
            pltpu.VMEM((32, 48, C1), F32),
            pltpu.VMEM((2, HALF_ROWS, C1), BF16),
        ],
        compiler_params=pltpu.CompilerParams(vmem_limit_bytes=24 * 2**20),
        cost_estimate=pl.CostEstimate(flops=2 * 10**9, bytes_accessed=10**7, transcendentals=200000),
        name="patch_work",
    )(places, side_b, middle, side_a, fb, rf, rft, wd, rdt, ru)


def small_call(body, name, outs, scratch, *args, smem=0):
    return pl.pallas_call(
        body,
        out_shape=tuple(jax.ShapeDtypeStruct(shape, kind) for shape, kind in outs),
        in_specs=[SMEM] * smem + [VMEM] * (len(args) - smem),
        out_specs=[VMEM] * len(outs),
        scratch_shapes=scratch,
        compiler_params=pltpu.CompilerParams(vmem_limit_bytes=10 * 2**20),
        cost_estimate=pl.CostEstimate(flops=10**6, bytes_accessed=2 * 10**6, transcendentals=0),
        name=name,
    )(*args)


def swapped_b(x, axes):
    size = lax.axis_size(axes)
    pairs = [(i, i + 1) for i in range(1, size - 1, 2)]
    return lax.ppermute(x, axes, pairs + [(j, i) for i, j in pairs])


def swapped_a(x, axis):
    return lax.ppermute(x, axis, [(0, 1), (1, 0)])


def added(x, y):
    return (x.astype(F32) + y.astype(F32)).astype(BF16)


def exchanged(parts, axes):
    return lax.all_to_all(parts, axes, 0, 0, tiled=True)


def summed_for(axes, parts):
    shape = (lax.axis_size(axes),) + parts.shape[1:]
    return small_call(sum_kernel, "sum", [(shape, BF16)], [], parts)[0]


def per_device(field, cotangent, w_first, w_down, w_up, offsets, blend_table):
    rows_n = lax.axis_size(ROW)
    cols_n = lax.axis_size(COL)
    row_at = lax.axis_index(ROW)
    col_at = lax.axis_index(COL)
    where = jnp.stack([row_at, col_at]).astype(jnp.int32)
    both = jnp.stack([field, cotangent])
    places, fb, rf, rft, rdt, ru = prepared(
        where, offsets.transpose(0, 2, 1), blend_table, w_first, w_down, w_up
    )
    row_a, row_b = swapped_a(both, "zh"), swapped_b(both, ROW)
    row_a, row_b, places, fb, rf, rft, rdt, ru = lax.optimization_barrier(
        (row_a, row_b, places, fb, rf, rft, rdt, ru)
    )
    window_shape = (2, 32, TILE, C1)
    to_a, own, to_b = small_call(
        assemble_kernel,
        "assemble",
        [(window_shape, BF16)] * 3,
        [pltpu.VMEM((2, 48, TILE, C1), BF16)],
        places,
        row_a,
        both,
        row_b,
        smem=1,
    )
    side_a, side_b = swapped_a(to_a, "core"), swapped_b(to_b, COL)
    own, strip_b, keep, send = patch_work(
        places, side_a, own, side_b, fb, rf, rft, w_down.reshape(3, 3 * C1, C2), rdt, ru
    )
    got = swapped_a(send, "core")
    from_b = swapped_b(strip_b, COL)
    part = added(keep, got[:HALF_ROWS])
    part = exchanged(part.reshape(lax.axis_size(PLANE), -1, C1), PLANE)
    part = summed_for(DEPTH, part)
    part, from_b = lax.optimization_barrier((part, from_b))
    part = summed_for(PLANE, exchanged(part, DEPTH))
    tile_shape = (2, TILE, TILE, C1)
    to_a, own, to_b = small_call(
        add_kernel,
        "add",
        [(tile_shape, BF16), (tile_shape, F32), (tile_shape, BF16)],
        [pltpu.VMEM((2, 48, TILE, C1), F32)],
        places,
        got,
        own,
        from_b,
        smem=1,
    )
    part, own, to_a, to_b = lax.optimization_barrier((part, own, to_a, to_b))
    row_a, row_b = swapped_a(to_a, "zh"), swapped_b(to_b, ROW)
    part = exchanged(part, PLANE).reshape(-1, C1)
    part, row_b, own, row_a = lax.optimization_barrier((part, row_b, own, row_a))
    other = swapped_a(part, "core")
    blended, field_grad = small_call(
        finish_kernel,
        "finish",
        [(field.shape, BF16), (field.shape, F32)],
        [],
        own,
        row_a,
        row_b,
    )
    scale = 1.0 / math.sqrt(TILE * rows_n * TILE * cols_n)
    g_first, g_down, g_up = small_call(
        functools.partial(unpack_kernel, scale),
        "unpack",
        [((9, C1, C1), F32), ((3, 3 * C1, C2), F32), ((4, C2, C1), F32)],
        [],
        lax.axis_index("core").astype(jnp.int32)[None],
        part,
        other,
        smem=1,
    )
    return (
        blended,
        field_grad,
        g_first.reshape(w_first.shape),
        g_down.reshape(w_down.shape),
        g_up.reshape(w_up.shape),
    )


def solution(mesh):
    fine = Mesh(mesh.devices.reshape(8, 4, 2, 4, 2), ("y", "zl", "core", "x", "zh"))
    tiles = P(ROW, COL, None)
    return jax.shard_map(
        per_device,
        mesh=fine,
        in_specs=(tiles, tiles, P(), P(), P(), P(), P()),
        out_specs=(tiles, tiles, P(), P(), P()),
        check_vma=False,
    )
```
